32 devices in a mesh: rows: 8 (over y, x, core), seq: 4 (over z).
Axes of the slice: x: 2, y: 2, z: 4, core: 2. Of those that a mesh axis runs over, the one named last changes fastest.
Arguments:
- hidden_in: bfloat16 [16, 1024, 768], P('rows', 'seq'), may hold values from -6 to 6
- timesteps: int32 [16], P('rows'), may hold values from 0 to 999, as said below
- step_table: bfloat16 [1000, 768], replicated, may hold values from -3 to 3
- gain_one: float32 [768], replicated, may hold values from 0.5 to 1.5
- w_qkv: bfloat16 [768, 2304], replicated, may hold values from -0.3125 to 0.3125
- w_out: bfloat16 [768, 768], replicated, may hold values from -0.875 to 0.875
- gain_two: float32 [768], replicated, may hold values from 0.5 to 1.5
- w_up: bfloat16 [768, 3072], replicated, may hold values from -0.21875 to 0.21875
- w_down: bfloat16 [3072, 768], replicated, may hold values from -0.21875 to 0.21875
- out_grad: bfloat16 [16, 1024, 768], P('rows', 'seq'), may hold values from -6 to 6
Outputs:
- out_hidden: bfloat16 [16, 1024, 768], P('rows', 'seq')
- in_grad: bfloat16 [16, 1024, 768], P('rows', 'seq')
- table_grad: float32 [1000, 768], replicated
- gain_one_grad: float32 [768], replicated
- qkv_weight_grad: float32 [768, 2304], P('rows', 'seq')
- out_weight_grad: float32 [768, 768], P('rows', 'seq')
- gain_two_grad: float32 [768], replicated
- up_weight_grad: float32 [768, 3072], P('rows', 'seq')
- down_weight_grad: float32 [3072, 768], P('rows', 'seq')
The draws below stay inside these ranges and needn't reach their ends.
Inputs may be any that keep to these rules, and one draw needn't show every extreme that they name: One timestep for each sequence; large timesteps are more common than small ones; in every draw some sequence has 999 and another has 0.
All inputs are finite; a program needn't handle non-finite values.
Results may differ from the reference program's by a relative error of at most 0.014.
Values may be sent and summed in bfloat16 or wider, within the bound.
No kernel may reach another device: no remote copies, remote signals or barrier semaphores. Data moves between devices by JAX's collectives and lax.ppermute only.
A program may use at most 192 MiB of HBM per device.

```python
import math
import jax
import jax.numpy as jnp
from jax import lax

D = 768
HEADS = 12
HEAD_DIM = 64
FF = 3072
NSTEPS = 1000
LEN = 1024
SEQS = 16


def draw_timesteps(key, part):
    key = jax.random.fold_in(key, 7)
    first, second, third, fourth = jax.random.split(key, 4)
    one_draw = jax.random.randint(first, (SEQS,), 0, NSTEPS)
    two_draw = jax.random.randint(second, (SEQS,), 0, NSTEPS)
    steps_all = jnp.maximum(one_draw, two_draw)
    top_at = jax.random.randint(third, (), 0, SEQS)
    bottom_at = (top_at + 1 + jax.random.randint(fourth, (), 0, SEQS - 1)) % SEQS
    steps_all = steps_all.at[top_at].set(NSTEPS - 1).at[bottom_at].set(0)
    return steps_all.astype(jnp.int32)


def strengthened(drawn, own_key, source, target, blocks, factor):
    def block_of(axis_at):
        return (jnp.arange(drawn.shape[axis_at]) // (drawn.shape[axis_at] // blocks)).reshape((-1,) + (1,) * (drawn.ndim - 1 - axis_at))

    near = jax.random.permutation(own_key, blocks)[block_of(target)]
    far = (block_of(target) + blocks // 2) % blocks
    return jnp.where((block_of(source) == near) | (block_of(source) == far), factor * drawn, drawn)


def block_levels(rng, dims, cuts, smallest, top_value):
    level, own = 1.0, jax.random.fold_in(rng, 6)
    for axis_at, parts in cuts:
        heights = jnp.exp(jax.random.uniform(jax.random.fold_in(own, axis_at), (parts,), jnp.float32, smallest / len(cuts), top_value / len(cuts)))
        level = level * jnp.repeat(heights, dims[axis_at] // parts).reshape([-1 if axis == axis_at else 1 for axis in range(len(dims))])
    return level


def scatter_about(rng, extent, spread, limit, cuts=(), held_as=jnp.bfloat16):
    gain = block_levels(rng, extent, cuts, -0.22, 0.18) if cuts else 1.0
    drawn = jax.random.normal(rng, extent, jnp.float32) * spread * gain
    return jnp.minimum(jnp.maximum(drawn, -limit), limit).astype(held_as)


def bell_draw_with(rng, dims, width, bound, cuts, heavy, kind=jnp.bfloat16):
    entries = width * jax.random.normal(rng, dims, jnp.float32)
    if cuts:
        entries = entries * block_levels(rng, dims, cuts, -0.22, 0.18)
    return jnp.clip(strengthened(entries, jax.random.fold_in(rng, 3), *heavy), -bound, bound).astype(kind)


def setup_inputs(seed: int = 0) -> dict:
    arg_keys = jax.random.split(jax.random.key(seed), 11)
    hidden_in = scatter_about(arg_keys[0], (SEQS, LEN, D), 1.0, 6.0, ((0, 8), (1, 4)))
    timesteps = draw_timesteps(jax.random.fold_in(arg_keys[10], 71), 0)
    step_table = scatter_about(arg_keys[2], (NSTEPS, D), 0.5, 3.0)
    gain_one = jnp.clip(1.0 + 0.1 * jax.random.normal(arg_keys[3], (D,), jnp.float32), 0.5, 1.5)
    w_qkv = scatter_about(arg_keys[4], (D, 3 * D), (D // 2) ** -0.5, 0.3125)
    w_out = scatter_about(arg_keys[5], (D, D), (D // 16) ** -0.5, 0.875)
    gain_two = jnp.clip(1.0 + 0.1 * jax.random.normal(arg_keys[6], (D,), jnp.float32), 0.5, 1.5)
    w_up = scatter_about(arg_keys[7], (D, FF), D ** -0.5, 0.21875)
    w_down = scatter_about(arg_keys[8], (FF, D), (FF // 4) ** -0.5, 0.21875)
    out_grad = bell_draw_with(arg_keys[9], (SEQS, LEN, D), 1.0, 6.0, ((0, 8), (1, 4)), (0, 2, 8, 2.0))
    return {"hidden_in": hidden_in, "timesteps": timesteps, "step_table": step_table, "gain_one": gain_one, "w_qkv": w_qkv, "w_out": w_out, "gain_two": gain_two, "w_up": w_up, "w_down": w_down, "out_grad": out_grad}


EPS = 1e-05
HIGH = lax.Precision.HIGHEST

@jax.custom_vjp
def low(v):
    return lax.optimization_barrier(v.astype(jnp.bfloat16)).astype(jnp.float32)

@jax.custom_vjp
def low_back(v):
    return v

def low_keep(v):
    return (low(v), None)

def low_pass(kept, grad):
    return (grad,)

def back_keep(v):
    return (v, None)

def back_low(kept, grad):
    return (low(grad),)
low.defvjp(low_keep, low_pass)
low_back.defvjp(back_keep, back_low)

def layer_norm(values, scale_gain):
    average = lax.optimization_barrier(jnp.mean(values, axis=-1, keepdims=True))
    centred = values - average
    return centred * lax.rsqrt(lax.optimization_barrier(jnp.mean(centred * centred, axis=-1, keepdims=True)) + EPS) * scale_gain

def project(values, weight):
    return jnp.einsum('gtd,de->gte', values, weight, precision=HIGH)

def one_head(pieces):
    queries, keys_part, values = pieces
    scores = low_back(jnp.einsum('gqd,gkd->gqk', queries, keys_part, precision=HIGH) * HEAD_DIM ** (-0.5))
    attn_weights = jax.nn.softmax(scores, axis=-1)
    return jnp.einsum('gqk,gkd->gqd', low(attn_weights), values, precision=HIGH)

def forward(hidden, steps_now, table, gain_one, w_qkv, w_out, gain_two, w_up, w_down):
    base = hidden + table[steps_now][:, None, :]
    normed_one = low(layer_norm(base, gain_one))
    packed = low(low_back(project(normed_one, w_qkv)))
    per_group = packed.shape[0]
    split_heads = packed.reshape(per_group, LEN, 3, HEADS, HEAD_DIM)
    heads_first = jnp.moveaxis(split_heads, 3, 0)
    mixed = lax.map(jax.checkpoint(one_head), (heads_first[:, :, :, 0], heads_first[:, :, :, 1], heads_first[:, :, :, 2]))
    mixed = jnp.moveaxis(mixed, 0, 2).reshape(per_group, LEN, D)
    mixed = low(low_back(mixed))
    middle = base + low_back(project(mixed, w_out))
    normed_two = low(layer_norm(middle, gain_two))
    upper = low_back(project(normed_two, w_up))
    active = low(jax.nn.gelu(upper))
    return middle + low_back(project(active, w_down))

def reference(hidden_in, timesteps, step_table, gain_one, w_qkv, w_out, gain_two, w_up, w_down, out_grad):
    per_group = math.gcd(SEQS, max(1, 4096 // LEN))
    group_count = SEQS // per_group
    params = tuple((parameter.astype(jnp.float32) for parameter in (step_table, gain_one, w_qkv, w_out, gain_two, w_up, w_down)))
    inputs = hidden_in.astype(jnp.float32).reshape(group_count, per_group, LEN, D)
    cotangents = out_grad.astype(jnp.float32).reshape(group_count, per_group, LEN, D)
    stepped = timesteps.reshape(group_count, per_group)

    def advance(totals, pieces):
        hidden, steps_now, cotangent = pieces

        def block_forward(hidden_value, *weights):
            return forward(hidden_value, steps_now, *weights)
        result, pullback = jax.vjp(block_forward, hidden, *params)
        grads = pullback(cotangent)
        totals = tuple((running + gradient for running, gradient in zip(totals, grads[1:])))
        return (totals, (result.astype(jnp.bfloat16), grads[0].astype(jnp.bfloat16)))
    starting = tuple((jnp.zeros(parameter.shape, jnp.float32) for parameter in params))
    totals, (outputs, in_grads) = lax.scan(advance, starting, (inputs, stepped, cotangents))
    return (outputs.reshape(SEQS, LEN, D), in_grads.reshape(SEQS, LEN, D), totals[0], totals[1], totals[2], totals[3], totals[4], totals[5], totals[6])
```

```python
import functools

import jax
import jax.numpy as jnp
from jax import lax
from jax.experimental import pallas as pl
from jax.experimental.pallas import tpu as pltpu
from jax.sharding import PartitionSpec as P

HEAD_DIM = 64
SCALE = HEAD_DIM ** (-0.5)
EPS = 1e-05
F32 = jnp.float32
BF16 = jnp.bfloat16
MIB = 1 << 20

NN = (((1,), (0,)), ((), ()))
NT = (((1,), (1,)), ((), ()))


def mm(a, b, dims=NN):
    return lax.dot_general(a, b, dims, preferred_element_type=F32)


def normalize(values):
    average = jnp.mean(values, axis=-1, keepdims=True)
    centred = values - average
    inverse_root = lax.rsqrt(jnp.mean(centred * centred, axis=-1, keepdims=True) + EPS)
    return (centred * inverse_root, inverse_root)


def norm_back(grad_normed, unit_rows, inverse_root, scale_gain):
    gained = grad_normed * scale_gain
    centred_grad = (
        gained
        - jnp.mean(gained, axis=-1, keepdims=True)
        - unit_rows * jnp.mean(gained * unit_rows, axis=-1, keepdims=True)
    )
    return (inverse_root * centred_grad, jnp.sum(grad_normed * unit_rows, axis=0, keepdims=True))


def whole(shape):
    return pl.BlockSpec(shape, lambda *_: (0,) * len(shape))


def call(body, name, scalars, ins, in_specs, outs, out_specs, grid=(1,), scratch=(), flops=0, moved=0, vmem=48):
    return pl.pallas_call(
        body,
        name=name,
        grid_spec=pltpu.PrefetchScalarGridSpec(
            num_scalar_prefetch=1,
            grid=grid,
            in_specs=in_specs,
            out_specs=out_specs,
            scratch_shapes=list(scratch),
        ),
        out_shape=outs,
        cost_estimate=pl.CostEstimate(flops=flops, bytes_accessed=moved, transcendentals=0),
        compiler_params=pltpu.CompilerParams(vmem_limit_bytes=vmem * MIB),
    )(scalars, *ins)


def qkv_body(s_ref, ha, hb, row, gain, wq, wk, wv, q_out, k_out, v_out):
    rows = ha.shape[0]
    for at, block in enumerate((ha, hb)):
        unit, _ = normalize(block[...].astype(F32) + row[...])
        normed = (unit * gain[...]).astype(BF16)
        here = pl.ds(at * rows, rows)
        q_out[here, :] = (mm(normed, wq[...]).astype(BF16) * SCALE).astype(BF16)
        k_out[here, :] = mm(normed, wk[...]).astype(BF16)
        v_out[here, :] = mm(normed, wv[...]).astype(BF16)


def qkv(scalars, ha, hb, row, gain, w_qkv):
    rows, width = ha.shape
    half = width // 2
    specs = [whole(ha.shape), whole(hb.shape), whole(row.shape), whole(gain.shape)]
    specs += [pl.BlockSpec((width, half), functools.partial(lambda t, g, s: (0, 2 * t + s[0]), t)) for t in range(3)]
    shape = (2 * rows, half)
    return call(
        qkv_body,
        "qkv",
        scalars,
        (ha, hb, row, gain, w_qkv, w_qkv, w_qkv),
        specs,
        [jax.ShapeDtypeStruct(shape, BF16)] * 3,
        [whole(shape)] * 3,
        flops=2 * 2 * rows * width * 3 * half,
        moved=2 * width * 3 * half,
    )


def attend_body(s_ref, q, k0, k1, v0, v1, mixed, lse):
    count, half = q.shape
    lanes = lax.broadcasted_iota(jnp.int32, (1, 128), 1)
    ones = jnp.ones((16, count), BF16)
    for pair in range(half // 128):
        cols = slice(128 * pair, 128 * pair + 128)
        q_pair = q[:, cols]
        vt = [v[:, cols].T for v in (v0, v1)]
        done = []
        for h in range(2):
            q_head = jnp.where((lanes >= 64) == (h == 1), q_pair, jnp.zeros_like(q_pair))
            scores = [mm(k[:, cols], q_head, NT) for k in (k0, k1)]
            highest = jnp.maximum(
                jnp.max(scores[0], axis=0, keepdims=True), jnp.max(scores[1], axis=0, keepdims=True)
            )
            total = None
            for part in range(2):
                weights = jnp.exp(scores[part] - highest).astype(BF16)
                left = jnp.concatenate([vt[part][64 * h : 64 * h + 64], ones], axis=0)
                term = mm(left, weights)
                total = term if total is None else total + term
            summed = total[64:65]
            done.append(total[:64] / summed)
            lse[2 * pair + h : 2 * pair + h + 1, :] = highest + jnp.log(summed)
        mixed[:, cols] = jnp.concatenate(done, axis=0).T.astype(BF16)


def attend(scalars, q, k0, k1, v0, v1):
    count, half = q.shape
    heads = half // HEAD_DIM
    ins = (q, k0, k1, v0, v1)
    outs = [jax.ShapeDtypeStruct((count, half), BF16), jax.ShapeDtypeStruct((8, count), F32)]
    return call(
        attend_body,
        "attend",
        scalars,
        ins,
        [whole(a.shape) for a in ins],
        outs,
        [whole(o.shape) for o in outs],
        flops=heads * 4 * 4 * count * 2 * count * HEAD_DIM,
        moved=10 * count * half,
    )


def forward_body(s_ref, ha, hb, row, m0, m1, wo0, wo1, gain, wu, wd, oa, ob, middle, normed, active, slope, acc):
    step = pl.program_id(0)
    rows = ha.shape[0]

    @pl.when(step == 0)
    def _():
        for at, block in enumerate((ha, hb)):
            here = pl.ds(at * rows, rows)
            base = block[...].astype(F32) + row[...]
            mid = base + mm(m0[here, :], wo0[...]) + mm(m1[here, :], wo1[...])
            middle[here, :] = mid
            acc[here, :] = mid
            unit, _ = normalize(mid)
            normed[here, :] = (unit * gain[...]).astype(BF16)

    for at in range(2):
        here = pl.ds(at * rows, rows)
        u = mm(normed[here, :], wu[...])
        square = u * u
        inner = u * (0.7978845608028654 + 0.035677408136300125 * square)
        th = jnp.tanh(inner)
        half_up = 0.5 * (1.0 + th)
        act = (u * half_up).astype(BF16)
        active[here, :] = act
        slope[here, :] = (
            half_up + 0.5 * u * (1.0 - th * th) * (0.7978845608028654 + 0.10703222440890037 * square)
        ).astype(BF16)
        acc[here, :] += mm(act, wd[...])

    @pl.when(step == pl.num_programs(0) - 1)
    def _():
        oa[...] = acc[:rows, :].astype(BF16)
        ob[...] = acc[rows:, :].astype(BF16)


def feed_forward(scalars, ha, hb, row, mine, other, w_out, gain, w_up, w_down):
    rows, width = ha.shape
    count, half = mine.shape
    ff = w_up.shape[1]
    chunk = ff // 4
    ins = (ha, hb, row, mine, other, w_out, w_out, gain, w_up, w_down)
    specs = [whole(a.shape) for a in ins[:5]]
    specs += [
        pl.BlockSpec((half, width), lambda g, s: (s[0], 0)),
        pl.BlockSpec((half, width), lambda g, s: (1 - s[0], 0)),
        whole(gain.shape),
        pl.BlockSpec((width, chunk), lambda g, s: (0, g)),
        pl.BlockSpec((chunk, width), lambda g, s: (g, 0)),
    ]
    outs = [
        jax.ShapeDtypeStruct((rows, width), BF16),
        jax.ShapeDtypeStruct((rows, width), BF16),
        jax.ShapeDtypeStruct((count, width), F32),
        jax.ShapeDtypeStruct((count, width), BF16),
        jax.ShapeDtypeStruct((count, ff), BF16),
        jax.ShapeDtypeStruct((count, ff), BF16),
    ]
    out_specs = [whole(o.shape) for o in outs[:4]] + [pl.BlockSpec((count, chunk), lambda g, s: (0, g))] * 2
    return call(
        forward_body,
        "feed_forward",
        scalars,
        ins,
        specs,
        outs,
        out_specs,
        grid=(4,),
        scratch=[pltpu.VMEM((count, width), F32)],
        flops=2 * count * width * (width + 2 * ff),
        moved=4 * width * ff + 4 * count * ff,
    )


def backward_body(s_ref, ga, gb, normed, active, slope, wu, wd, before, down, up, total, grad_t, normed_t):
    step = pl.program_id(0)
    rows = ga.shape[0]

    @pl.when(step == 0)
    def _():
        grad_t[:, :rows] = ga[...].T
        grad_t[:, rows:] = gb[...].T
        normed_t[...] = normed[...].T
        if before is None:
            total[...] = jnp.zeros_like(total)
        else:
            total[...] = before[...]

    down[0] = mm(grad_t[...], active[...]).astype(BF16)
    pulled = []
    for at, block in enumerate((ga, gb)):
        here = pl.ds(at * rows, rows)
        grad_active = mm(block[...], wd[...], NT)
        grad_upper = (grad_active * slope[here, :].astype(F32)).astype(BF16)
        total[here, :] += mm(grad_upper, wu[...], NT)
        pulled.append(grad_upper)
    up[0] = mm(normed_t[...], jnp.concatenate(pulled, axis=0)).astype(BF16)


def feed_back(scalars, ga, gb, normed, active, slope, w_up, w_down, before, parts, place):
    rows, width = ga.shape
    count = 2 * rows
    ff = w_up.shape[1]
    chunk = ff // 2 // parts
    column = lambda g, s: (0, place(g, s[1]))
    ins = [ga, gb, normed, active, slope, w_up, w_down]
    specs = [
        whole(ga.shape),
        whole(gb.shape),
        whole(normed.shape),
        pl.BlockSpec((count, chunk), column),
        pl.BlockSpec((count, chunk), column),
        pl.BlockSpec((width, chunk), column),
        pl.BlockSpec((chunk, width), lambda g, s: (place(g, s[1]), 0)),
    ]
    body = backward_body
    if before is None:
        body = lambda s, a, b, c, d, e, f, g, *rest: backward_body(s, a, b, c, d, e, f, g, None, *rest)
    else:
        ins.append(before)
        specs.append(whole(before.shape))
    outs = [
        jax.ShapeDtypeStruct((parts, width, chunk), BF16),
        jax.ShapeDtypeStruct((parts, width, chunk), BF16),
        jax.ShapeDtypeStruct((count, width), F32),
    ]
    out_specs = [pl.BlockSpec((1, width, chunk), lambda g, s: (g, 0, 0))] * 2 + [whole((count, width))]
    return call(
        body,
        "feed_back",
        scalars,
        ins,
        specs,
        outs,
        out_specs,
        grid=(parts,),
        scratch=[pltpu.VMEM((width, count), BF16), pltpu.VMEM((width, count), BF16)],
        flops=4 * 2 * count * width * ff // 2,
        moved=4 * width * ff + 2 * count * ff,
    )


def middle_body(s_ref, ga, gb, total, middle, gain, wo0, wo1, grad_middle, low, mine, other, gain_grad):
    rows = ga.shape[0]
    gain_sum = None
    for at, block in enumerate((ga, gb)):
        here = pl.ds(at * rows, rows)
        unit, root = normalize(middle[here, :])
        back, part = norm_back(total[here, :], unit, root, gain[...])
        gain_sum = part if gain_sum is None else gain_sum + part
        grad = block[...].astype(F32) + back
        grad_middle[here, :] = grad
        grad_low = grad.astype(BF16)
        low[here, :] = grad_low
        other[here, :] = mm(grad_low, wo1[...], NT).astype(BF16)
        mine[here, :] = mm(grad_low, wo0[...], NT).astype(BF16)
    gain_grad[...] = gain_sum


def middle_back(scalars, ga, gb, total, middle, gain, w_out):
    rows, width = ga.shape
    count, half = 2 * rows, width // 2
    ins = (ga, gb, total, middle, gain, w_out, w_out)
    specs = [whole(a.shape) for a in ins[:5]]
    specs += [
        pl.BlockSpec((half, width), lambda g, s: (s[0], 0)),
        pl.BlockSpec((half, width), lambda g, s: (1 - s[0], 0)),
    ]
    outs = [
        jax.ShapeDtypeStruct((count, width), F32),
        jax.ShapeDtypeStruct((count, width), BF16),
        jax.ShapeDtypeStruct((count, half), BF16),
        jax.ShapeDtypeStruct((count, half), BF16),
        jax.ShapeDtypeStruct((1, width), F32),
    ]
    return call(
        middle_body,
        "middle_back",
        scalars,
        ins,
        specs,
        outs,
        [whole(o.shape) for o in outs],
        flops=2 * count * width * width,
        moved=16 * count * width,
    )


def out_grad_body(s_ref, m0, m1, low, out):
    half = m0.shape[1]
    c = s_ref[0]
    out[pl.ds(pl.multiple_of(c * half, half), half), :] = mm(m0[...].T, low[...]).astype(BF16)
    out[pl.ds(pl.multiple_of((1 - c) * half, half), half), :] = mm(m1[...].T, low[...]).astype(BF16)


def out_weight(scalars, mine, other, low):
    count, width = low.shape
    ins = (mine, other, low)
    out = jax.ShapeDtypeStruct((width, width), BF16)
    return call(
        out_grad_body,
        "out_weight",
        scalars,
        ins,
        [whole(a.shape) for a in ins],
        out,
        whole(out.shape),
        flops=2 * count * width * width,
        moved=4 * count * width,
    )


def attend_back_body(s_ref, q, do, o, lse, k0, k1, v0, v1, *rest, first):
    if first:
        dq, dk, dv = rest
    else:
        dk_in, dv_in, dq, dk, dv = rest
    count, half = q.shape
    lanes = lax.broadcasted_iota(jnp.int32, (1, 128), 1)
    head_of = lax.broadcasted_iota(jnp.int32, (8, half), 1) // HEAD_DIM
    picks = (head_of == lax.broadcasted_iota(jnp.int32, (8, half), 0)).astype(BF16)
    product = do[...].astype(F32) * o[...].astype(F32)
    high = product.astype(BF16)
    rest_low = (product - high.astype(F32)).astype(BF16)
    inner = mm(picks, high, NT) + mm(picks, rest_low, NT)
    for pair in range(half // 128):
        cols = slice(128 * pair, 128 * pair + 128)
        q_pair = q[:, cols]
        do_pair = do[:, cols]
        grads_q = []
        sums = [[None, None], [None, None]]
        keys_t = [k[:, cols].T for k in (k0, k1)]
        for h in range(2):
            at = 2 * pair + h
            mask = (lanes >= 64) == (h == 1)
            q_head = jnp.where(mask, q_pair, jnp.zeros_like(q_pair))
            do_head = jnp.where(mask, do_pair, jnp.zeros_like(do_pair))
            grad_q = None
            for part, (k, v) in enumerate(((k0, v0), (k1, v1))):
                weights = jnp.exp(mm(k[:, cols], q_head, NT) - lse[at : at + 1, :])
                grad_weights = mm(v[:, cols], do_head, NT)
                grad_scores = (weights * (grad_weights - inner[at : at + 1, :])).astype(BF16)
                terms = (mm(grad_scores, q_head), mm(weights.astype(BF16), do_head))
                for i in range(2):
                    sums[i][part] = terms[i] if sums[i][part] is None else sums[i][part] + terms[i]
                term = mm(keys_t[part][64 * h : 64 * h + 64], grad_scores)
                grad_q = term if grad_q is None else grad_q + term
            grads_q.append(grad_q)
        dq[:, cols] = (jnp.concatenate(grads_q, axis=0).T * SCALE).astype(BF16)
        for part in range(2):
            here = pl.ds(part * count, count)
            if first:
                dk[here, cols] = sums[0][part]
                dv[here, cols] = sums[1][part]
            else:
                dk[here, cols] = (sums[0][part] + dk_in[here, cols]).astype(BF16)
                dv[here, cols] = (sums[1][part] + dv_in[here, cols]).astype(BF16)


def attend_back(scalars, q, do, o, lse, k0, k1, v0, v1, before=None):
    count, half = q.shape
    heads = half // HEAD_DIM
    ins = (q, do, o, lse, k0, k1, v0, v1) + (() if before is None else tuple(before))
    kind = F32 if before is None else BF16
    outs = [
        jax.ShapeDtypeStruct((count, half), BF16),
        jax.ShapeDtypeStruct((2 * count, half), kind),
        jax.ShapeDtypeStruct((2 * count, half), kind),
    ]
    return call(
        functools.partial(attend_back_body, first=before is None),
        "attend_back",
        scalars,
        ins,
        [whole(a.shape) for a in ins],
        outs,
        [whole(o.shape) for o in outs],
        flops=heads * 4 * 10 * count * 2 * count * HEAD_DIM,
        moved=20 * count * half,
    )


def project_back_body(s_ref, dq, dk, dv, wq, wk, wv, out):
    out[...] = (mm(dq[...], wq[...], NT) + mm(dk[...], wk[...], NT) + mm(dv[...], wv[...], NT)).astype(out.dtype)


def project_back(scalars, dq, dk, dv, w_qkv, part, kind):
    count, half = dq.shape
    width = 2 * half
    specs = [whole(dq.shape)] + [pl.BlockSpec((count, half), lambda g, s: (part, 0))] * 2
    specs += [pl.BlockSpec((width, half), functools.partial(lambda t, g, s: (0, 2 * t + s[0]), t)) for t in range(3)]
    out = jax.ShapeDtypeStruct((count, width), kind)
    return call(
        project_back_body,
        "project_back",
        scalars,
        (dq, dk, dv, w_qkv, w_qkv, w_qkv),
        specs,
        out,
        whole(out.shape),
        flops=2 * count * width * 3 * half,
        moved=8 * count * width,
    )


def qkv_weight_body(s_ref, ha, hb, xa, xb, row, gain, dq0, dq1, dk, dv, out):
    rows = ha.shape[0]
    count = 2 * rows
    half = dq0.shape[1]
    turned = []
    for block in (ha, hb, xa, xb):
        unit, _ = normalize(block[...].astype(F32) + row[...])
        turned.append((unit * gain[...]).astype(BF16).T)
    turned = jnp.concatenate(turned, axis=1)
    out[:, :half] = mm(turned, jnp.concatenate([dq0[...], dq1[...]], axis=0)).astype(BF16)
    out[:, half : 2 * half] = mm(turned, dk[...]).astype(BF16)
    out[:, 2 * half :] = mm(turned, dv[...]).astype(BF16)


def qkv_weight(scalars, ha, hb, xa, xb, row, gain, dq0, dq1, dk, dv):
    width = ha.shape[1]
    half = dq0.shape[1]
    ins = (ha, hb, xa, xb, row, gain, dq0, dq1, dk, dv)
    out = jax.ShapeDtypeStruct((width, 3 * half), BF16)
    return call(
        qkv_weight_body,
        "qkv_weight",
        scalars,
        ins,
        [whole(a.shape) for a in ins],
        out,
        whole(out.shape),
        flops=2 * 4 * ha.shape[0] * width * 3 * half,
        moved=8 * width * 3 * half,
    )


def base_body(s_ref, ha, hb, row, gain, grad_middle, p0, p1, ia, ib, sums):
    rows = ha.shape[0]
    gain_sum, base_sum = None, None
    for at, (block, out) in enumerate(((ha, ia), (hb, ib))):
        here = pl.ds(at * rows, rows)
        unit, root = normalize(block[...].astype(F32) + row[...])
        back, part = norm_back(p0[here, :] + p1[here, :].astype(F32), unit, root, gain[...])
        grad = grad_middle[here, :] + back
        out[...] = grad.astype(BF16)
        gain_sum = part if gain_sum is None else gain_sum + part
        tokens = jnp.sum(grad, axis=0, keepdims=True)
        base_sum = tokens if base_sum is None else base_sum + tokens
    sums[0:1, :] = base_sum
    sums[1:2, :] = gain_sum


def base_back(scalars, ha, hb, row, gain, grad_middle, p0, p1):
    rows, width = ha.shape
    ins = (ha, hb, row, gain, grad_middle, p0, p1)
    outs = [
        jax.ShapeDtypeStruct((rows, width), BF16),
        jax.ShapeDtypeStruct((rows, width), BF16),
        jax.ShapeDtypeStruct((2, width), F32),
    ]
    return call(
        base_body,
        "base_back",
        scalars,
        ins,
        [whole(a.shape) for a in ins],
        outs,
        [whole(o.shape) for o in outs],
        flops=40 * rows * width,
        moved=20 * rows * width,
    )


def table_body(s_ref, sums, out):
    out[...] = jnp.zeros_like(out)
    for at in range(sums.shape[0]):
        here = pl.ds(s_ref[at], 1)
        out[here, :] = out[here, :] + sums[at : at + 1, :]


def table_of(steps, sums, count):
    out = jax.ShapeDtypeStruct((count, sums.shape[1]), F32)
    return call(
        table_body,
        "table",
        steps,
        (sums,),
        [whole(sums.shape)],
        out,
        whole(out.shape),
        flops=count * sums.shape[1],
        moved=4 * count * sums.shape[1],
    )


def on_device(
    row_count, seq_count, hidden_in, timesteps, step_table, gain_one, w_qkv, w_out, gain_two, w_up, w_down, out_grad
):
    seqs_here, tokens_here, width = hidden_in.shape
    ff = w_up.shape[1]
    half = width // 2
    blocks = row_count // 2
    block_bits = blocks.bit_length() - 1
    seq_bits = seq_count.bit_length() - 1
    r = lax.axis_index("rows")
    z = lax.axis_index("seq")
    c = lax.rem(r, 2)
    b = lax.div(r, 2)
    odd = lax.rem(z, 2)
    axes = ("rows", "seq")

    def flat(row, seq):
        return row * seq_count + seq

    def swap(value, row_bit, seq_bit=0):
        pairs = [
            (flat(i, j), flat(i ^ row_bit, j ^ seq_bit)) for i in range(row_count) for j in range(seq_count)
        ]
        return lax.ppermute(value, axes, pairs)

    def core_swap(value):
        return swap(value, 1)

    moves = []
    for turn in range(2):
        moves.append(
            [
                (flat(2 * p + e, j), flat(2 * p + j // 2, 2 * e + (j + turn) % 2))
                for p in range(blocks)
                for e in range(2)
                for j in range(seq_count)
            ]
        )

    def gather_tokens(value):
        first = lax.dynamic_index_in_dim(value, odd, 0, keepdims=False)
        second = lax.dynamic_index_in_dim(value, 1 - odd, 0, keepdims=False)
        return (lax.ppermute(first, axes, moves[0]), lax.ppermute(second, axes, moves[1]))

    def return_tokens(first, second):
        back = [[(t, s) for s, t in m] for m in moves]
        first = lax.ppermute(first, axes, back[0])
        second = lax.ppermute(second, axes, back[1])
        return jnp.where(odd == 0, jnp.stack([first, second]), jnp.stack([second, first]))

    scalars = jnp.stack([c, c]).astype(jnp.int32)
    others = jnp.stack([c, 1 - c]).astype(jnp.int32)
    gain_one = gain_one[None, :]
    gain_two = gain_two[None, :]

    steps_all = lax.all_gather(timesteps, "rows", axis=0, tiled=True)
    step_now = lax.dynamic_index_in_dim(steps_all, seq_count * b + z, 0, keepdims=False)
    row = lax.dynamic_slice_in_dim(step_table, step_now, 1, 0).astype(F32)

    ha, hb = gather_tokens(hidden_in)
    xa, xb = core_swap(ha), core_swap(hb)
    late_grad, _, _ = lax.optimization_barrier((out_grad, ha, hb))
    ga, gb = gather_tokens(late_grad)

    q0, k0, v0 = qkv(scalars, ha, hb, row, gain_one, w_qkv)
    q1, k1, v1 = qkv(scalars, xa, xb, row, gain_one, w_qkv)

    mixed_far, lse_far = attend(scalars, q1, k0, k1, v0, v1)
    mixed_in = core_swap(mixed_far)
    mixed_near, lse_near = attend(scalars, q0, k0, k1, v0, v1)

    unit = ff // row_count
    parts = seq_count
    per_part = blocks // parts
    if per_part == 1 and unit % 128 == 0:
        place = lambda g, share: 2 * g + share
    else:
        w_up = w_up.reshape(width, blocks, 2, unit).transpose(0, 2, 1, 3).reshape(width, ff)
        w_down = w_down.reshape(blocks, 2, unit, width).transpose(1, 0, 2, 3).reshape(ff, width)
        place = lambda g, share: parts * share + g

    oa, ob, middle, normed_two, active, slope = feed_forward(
        scalars, ha, hb, row, mixed_near, mixed_in, w_out, gain_two, w_up, w_down
    )
    out_hidden = return_tokens(oa, ob)

    down_far, up_far, total = feed_back(others, ga, gb, normed_two, active, slope, w_up, w_down, None, parts, place)
    down_in, up_in = core_swap(down_far), core_swap(up_far)
    down_near, up_near, total = feed_back(
        scalars, ga, gb, normed_two, active, slope, w_up, w_down, total, parts, place
    )
    grad_middle, low, gm_near, gm_far, gain_two_part = middle_back(scalars, ga, gb, total, middle, gain_two, w_out)
    gm_in = core_swap(gm_far)
    out_w = out_weight(scalars, mixed_near, mixed_in, low)

    dq0, dk, dv = attend_back(scalars, q0, gm_near, mixed_near, lse_near, k0, k1, v0, v1)
    dq1, dk, dv = attend_back(scalars, q1, gm_in, mixed_far, lse_far, k0, k1, v0, v1, (dk, dv))

    part_far = project_back(scalars, dq1, dk, dv, w_qkv, 1, BF16)
    part_in = core_swap(part_far)
    part_near = project_back(scalars, dq0, dk, dv, w_qkv, 0, F32)
    qkv_w = qkv_weight(scalars, ha, hb, xa, xb, row, gain_one, dq0, dq1, dk, dv)
    ia, ib, sums = base_back(scalars, ha, hb, row, gain_one, grad_middle, part_near, part_in)
    in_grad = return_tokens(ia, ib)

    bit_of = lambda value, bit: lax.rem(lax.div(value, 1 << bit), 2)

    def pick(term, chosen):
        array, axes_left = term
        sizes = list(array.shape)
        starts = [0] * array.ndim
        for axis, at in zip(axes_left, range(len(axes_left))):
            if axis in chosen:
                starts[at] = chosen[axis]
                sizes[at] = 1
        kept = [s for i, s in enumerate(sizes) if not (i < len(axes_left) and axes_left[i] in chosen)]
        return lax.dynamic_slice(array, starts, sizes).reshape(kept).astype(F32)

    def reduce_bits(terms, order, chosen):
        chosen = dict(chosen)
        for name, own, row_bit, seq_bit in order:
            sent = sum(pick(t, {**chosen, name: 1 - own}) for t in terms).astype(BF16)
            left = [a for a in terms[0][1] if a not in chosen and a != name]
            chosen[name] = own
            terms = terms + [(swap(sent, row_bit, seq_bit), left)]
        return terms, chosen

    block_names = [("b", i) for i in reversed(range(block_bits))]
    seq_names = [("s", i) for i in reversed(range(seq_bits))]
    block_steps = [(("b", i), bit_of(b, i), 2 << i, 0) for i in range(block_bits)]
    seq_steps = [(("s", i), bit_of(z, i), 0, 1 << i) for i in range(seq_bits)]
    twos = lambda n: (2,) * n

    def halves(terms, names):
        out = []
        for at in range(2):
            cut = [(t[..., at * (t.shape[-2] // 2) : (at + 1) * (t.shape[-2] // 2), :], names) for t in terms]
            out.append(reduce_bits(cut, block_steps if at == 0 else block_steps[::-1], {}))
        return out

    def finish(terms, chosen):
        terms, chosen = reduce_bits(terms, seq_steps, chosen)
        return sum(pick(t, chosen) for t in terms)

    rows_block = width // blocks
    seq_rows = width // seq_count

    def as_down(value):
        value = value.reshape(parts, seq_count, seq_rows, per_part, unit).transpose(0, 3, 1, 2, 4)
        return value.reshape(twos(block_bits + seq_bits) + (seq_rows, unit))

    def as_up(value):
        value = value.reshape(twos(seq_bits + block_bits) + (rows_block, ff // 2 // parts))
        return value

    down_halves = halves([as_down(down_near), as_down(down_in)], block_names + seq_names)
    down_sum = jnp.concatenate([finish(*h) for h in down_halves], axis=0)
    down_shard = down_sum.T

    up_halves = halves([as_up(up_near), as_up(up_in)], seq_names + block_names)
    up_sums = [finish(*h) for h in up_halves]
    up_mine = jnp.where(c == 0, up_sums[0], up_sums[1])
    up_other = core_swap(jnp.where(c == 0, up_sums[1], up_sums[0]))
    up_pair = jnp.where(c == 0, jnp.stack([up_mine, up_other]), jnp.stack([up_other, up_mine]))
    up_shard = up_pair.reshape(2, rows_block // 2, per_part, unit).transpose(1, 2, 0, 3)
    up_shard = up_shard.reshape(rows_block // 2, 2 * per_part * unit)

    out_parts = out_w.reshape(blocks, 2, rows_block // 2, width)
    out_send = lax.dynamic_index_in_dim(out_parts, 1 - c, 1, keepdims=False)
    out_keep = lax.dynamic_index_in_dim(out_parts, c, 1, keepdims=False)

    def as_out(value):
        value = value.reshape(blocks, rows_block // 2, seq_count, seq_rows).transpose(0, 2, 1, 3)
        return value.reshape(twos(block_bits + seq_bits) + (rows_block // 2, seq_rows))

    out_halves = halves([as_out(out_keep), as_out(core_swap(out_send))], block_names + seq_names)
    out_shard = jnp.concatenate([finish(*h) for h in out_halves], axis=0)

    qkv_halves = halves([qkv_w.reshape(twos(block_bits) + (rows_block, 3 * half))], block_names)
    qkv_sums = [sum(pick(t, ch) for t in terms).astype(BF16) for terms, ch in qkv_halves]
    qkv_mine = jnp.where(c == 0, qkv_sums[0], qkv_sums[1])
    qkv_other = core_swap(jnp.where(c == 0, qkv_sums[1], qkv_sums[0]))
    qkv_pair = jnp.where(c == 0, jnp.stack([qkv_mine, qkv_other]), jnp.stack([qkv_other, qkv_mine]))
    qkv_cols = qkv_pair.reshape(2, rows_block // 2, 3, half).transpose(1, 2, 0, 3)
    qkv_cols = qkv_cols.reshape(rows_block // 2, seq_count, 6 * half // seq_count).transpose(1, 0, 2)
    qkv_cols = qkv_cols.reshape(twos(seq_bits) + qkv_cols.shape[1:])
    qkv_shard = finish([(qkv_cols, seq_names)], {})

    sums = sums + core_swap(sums)
    gain_two_part = gain_two_part + core_swap(gain_two_part)
    gains = jnp.concatenate([sums[1:2], gain_two_part], axis=0)
    rows_held = sums[0:1]
    for bit in range(seq_bits):
        got_rows, got = swap((rows_held, gains), 0, 1 << bit)
        gains = gains + got
        mine_first = bit_of(z, bit) == 0
        rows_held = jnp.where(
            mine_first, jnp.concatenate([rows_held, got_rows]), jnp.concatenate([got_rows, rows_held])
        )
    for bit in range(block_bits):
        got_rows, got = swap((rows_held, gains), 2 << bit)
        gains = gains + got
        mine_first = bit_of(b, bit) == 0
        rows_held = jnp.where(
            mine_first, jnp.concatenate([rows_held, got_rows]), jnp.concatenate([got_rows, rows_held])
        )
    table = table_of(steps_all, rows_held, step_table.shape[0])

    return (
        out_hidden,
        in_grad,
        table,
        gains[0],
        qkv_shard,
        out_shard,
        gains[1],
        up_shard,
        down_shard,
    )


def solution(mesh):
    tokens = P("rows", "seq", None)
    split = P("rows", "seq")
    in_specs = (tokens, P("rows"), P(), P(), P(), P(), P(), P(), P(), tokens)
    out_specs = (tokens, tokens, P(), P(), split, split, P(), split, split)
    body = functools.partial(on_device, mesh.shape["rows"], mesh.shape["seq"])
    return jax.shard_map(body, mesh=mesh, in_specs=in_specs, out_specs=out_specs, check_vma=False)
```

```python
import functools

import jax
import jax.numpy as jnp
from jax import lax
from jax.experimental import pallas as pl
from jax.experimental.pallas import tpu as pltpu
from jax.sharding import PartitionSpec as P

HEAD_DIM = 64
SCALE = HEAD_DIM ** (-0.5)
EPS = 1e-05
F32 = jnp.float32
BF16 = jnp.bfloat16
MIB = 1 << 20
PER_US = 1_000_000_000

NN = (((1,), (0,)), ((), ()))
NT = (((1,), (1,)), ((), ()))


def mm(a, b, dims=NN):
    return lax.dot_general(a, b, dims, preferred_element_type=F32)


def normalize(values):
    average = jnp.mean(values, axis=-1, keepdims=True)
    centred = values - average
    inverse_root = lax.rsqrt(jnp.mean(centred * centred, axis=-1, keepdims=True) + EPS)
    return (centred * inverse_root, inverse_root)


def norm_back(grad_normed, unit_rows, inverse_root, scale_gain):
    gained = grad_normed * scale_gain
    centred_grad = (
        gained
        - jnp.mean(gained, axis=-1, keepdims=True)
        - unit_rows * jnp.mean(gained * unit_rows, axis=-1, keepdims=True)
    )
    return (inverse_root * centred_grad, jnp.sum(grad_normed * unit_rows, axis=0, keepdims=True))


def whole(shape):
    return pl.BlockSpec(shape, lambda *_: (0,) * len(shape))


class Staged:
    def __init__(self, array):
        self.memory = pltpu.VMEM(array.shape, array.dtype)


class Order:
    def __init__(self):
        self.token = None


def call(
    body, name, scalars, ins, in_specs, outs, out_specs, grid=(1,), scratch=(), vmem=32, order=None, us=1.0, aliases=None
):
    ins, in_specs, outs, out_specs = list(ins), list(in_specs), list(outs), list(out_specs)
    count, given = len(ins), len(outs)
    staged = [at for at, spec in enumerate(in_specs) if isinstance(spec, Staged)]
    held = [in_specs[at].memory for at in staged]
    for at in staged:
        in_specs[at] = ANY
    waits = [] if order is None or order.token is None else [order.token]
    inner = body

    def body(scalars_ref, *refs):
        refs = list(refs)
        del refs[count : count + len(waits)]
        if order is not None:
            token = refs.pop(count + given)
            token[...] = jnp.zeros_like(token)
        if staged:
            sems, slots = refs.pop(), refs[len(refs) - len(held) :]
            del refs[len(refs) - len(held) :]
            copies = [pltpu.make_async_copy(refs[at], slot, sems.at[i]) for i, (at, slot) in enumerate(zip(staged, slots))]
            for copy in copies:
                copy.start()
            for at, slot in zip(staged, slots):
                refs[at] = slot
            for copy in copies:
                copy.wait()
        inner(scalars_ref, *refs)

    ins += waits
    in_specs += [ANY] * len(waits)
    if order is not None:
        outs.append(jax.ShapeDtypeStruct((8, 128), F32))
        out_specs.append(whole((8, 128)))
    scratch = list(scratch) + held + ([pltpu.SemaphoreType.DMA((len(staged),))] if staged else [])
    result = pl.pallas_call(
        body,
        name=name,
        grid_spec=pltpu.PrefetchScalarGridSpec(
            num_scalar_prefetch=1,
            grid=grid,
            in_specs=in_specs,
            out_specs=out_specs,
            scratch_shapes=scratch,
        ),
        out_shape=outs,
        input_output_aliases={at + 1: to for at, to in (aliases or {}).items()},
        cost_estimate=pl.CostEstimate(flops=int(us * PER_US), bytes_accessed=1 << 10, transcendentals=0),
        compiler_params=pltpu.CompilerParams(vmem_limit_bytes=vmem * MIB),
    )(scalars, *ins)
    result = list(result)
    if order is not None:
        order.token = result.pop()
    return result


def in_hbm(value):
    return pltpu.with_memory_space_constraint(value, pltpu.HBM)


ANY = pl.BlockSpec(memory_space=pl.ANY)


def gelu_both(upper):
    square = upper * upper
    turned = jnp.tanh(upper * (GELU_A + GELU_A * GELU_B * square))
    half_up = 0.5 + 0.5 * turned
    active = upper * half_up
    slope = half_up + active * (1.0 - turned) * (GELU_A + 3.0 * GELU_A * GELU_B * square)
    return active.astype(BF16), slope.astype(BF16)


class Copies:
    def __init__(self, sems):
        self.sems, self.count, self.outs = sems, 0, []

    def start(self, source, target):
        copy = pltpu.make_async_copy(source, target, self.sems.at[self.count])
        self.count += 1
        copy.start()
        return copy

    def out(self, source, target):
        self.outs.append(self.start(source, target))

    def finish(self):
        for copy in self.outs:
            copy.wait()


GELU_A, GELU_B = 0.7978845608028654, 0.044715


def stretches(parts):
    return [(at, min(at + 2, parts)) for at in range(0, parts, 2)]


def prepare_body(s_ref, row, first, second, wq, wk, wv, out, vectors):
    half = wq.shape[1]
    for t, w in enumerate((wq, wk, wv)):
        out[:, t * half : t * half + half] = w[...]
    for at, value in enumerate((row, first, second)):
        vectors[at : at + 1, :] = value[...]


def prepare(scalars, row, gain_one, gain_two, w_qkv, order=None):
    width = w_qkv.shape[0]
    half = width // 2
    specs = [whole((1, width))] * 3
    specs += [pl.BlockSpec((width, half), functools.partial(lambda t, g, s: (0, 2 * t + s[0]), t)) for t in range(3)]
    outs = [jax.ShapeDtypeStruct((width, 3 * half), BF16), jax.ShapeDtypeStruct((8, width), F32)]
    return call(
        prepare_body,
        "prepare",
        scalars,
        (row, gain_one, gain_two) + (in_hbm(w_qkv),) * 3,
        specs,
        outs,
        [whole(o.shape) for o in outs],
        order=order,
        us=2,
        vmem=12,
    )


def returned_body(s_ref, first, second, out, sems):
    at = bit(s_ref[2], 0)
    copies = Copies(sems)
    copies.out(first, out.at[at])
    copies.out(second, out.at[1 - at])
    copies.finish()


def returned_blocks(scalars, first, second, order=None):
    return call(
        returned_body,
        "returned",
        scalars,
        (first, second),
        [ANY] * 2,
        [pltpu.HBM((2,) + first.shape, first.dtype)],
        [ANY],
        scratch=[pltpu.SemaphoreType.DMA((2,))],
        order=order,
        us=1,
        vmem=4,
    )[0]


def qkv_body(s_ref, ha, hb, vectors, weight, out, normed):
    row, gain = vectors[0:1, :], vectors[1:2, :]
    rows = ha.shape[0]
    half = out.shape[1] // 3
    for at, block in enumerate((ha, hb)):
        unit, _ = normalize(block[...].astype(F32) + row)
        normed[pl.ds(at * rows, rows), :] = (unit * gain).astype(BF16)
    packed = mm(normed[...], weight[...]).astype(BF16)
    out[:, :half] = (packed[:, :half] * SCALE).astype(BF16)
    out[:, half:] = packed[:, half:]


def qkv(scalars, ha, hb, vectors, weight, order=None, us=2.3):
    rows, width = ha.shape
    ins = (ha, hb, vectors, weight)
    out = jax.ShapeDtypeStruct((2 * rows, weight.shape[1]), BF16)
    return call(
        qkv_body,
        "qkv",
        scalars,
        ins,
        [whole(a.shape) for a in ins],
        [out],
        [whole(out.shape)],
        scratch=[pltpu.VMEM((2 * rows, width), BF16)],
        order=order,
        us=us,
        vmem=16,
    )[0]


def attend_body(s_ref, q, k0, k1, v0, v1, mixed, lse):
    count, half = q.shape
    lanes = lax.broadcasted_iota(jnp.int32, (1, 128), 1)
    ones = jnp.ones((16, count), BF16)
    for pair in range(half // 128):
        cols = slice(128 * pair, 128 * pair + 128)
        q_pair = q[:, cols]
        vt = [v[:, cols].T for v in (v0, v1)]
        done = []
        for h in range(2):
            q_head = jnp.where((lanes >= 64) == (h == 1), q_pair, jnp.zeros_like(q_pair))
            scores = [mm(k[:, cols], q_head, NT) for k in (k0, k1)]
            highest = jnp.maximum(
                jnp.max(scores[0], axis=0, keepdims=True), jnp.max(scores[1], axis=0, keepdims=True)
            )
            total = None
            for part in range(2):
                weights = jnp.exp(scores[part] - highest).astype(BF16)
                left = jnp.concatenate([vt[part][64 * h : 64 * h + 64], ones], axis=0)
                term = mm(left, weights)
                total = term if total is None else total + term
            summed = total[64:65]
            done.append(total[:64] / summed)
            lse[2 * pair + h : 2 * pair + h + 1, :] = highest + jnp.log(summed)
        mixed[:, cols] = jnp.concatenate(done, axis=0).T.astype(BF16)


def attend(scalars, asked, near, far, order=None):
    count, half = asked.shape[0], asked.shape[1] // 3
    ins = (asked, near, far, near, far)
    outs = [jax.ShapeDtypeStruct((count, half), BF16), jax.ShapeDtypeStruct((8, count), F32)]
    return call(
        attend_body,
        "attend",
        scalars,
        ins,
        [pl.BlockSpec((count, half), functools.partial(lambda t, g, s: (0, t), t)) for t in (0, 1, 1, 2, 2)],
        outs,
        [whole(o.shape) for o in outs],
        order=order,
        us=6,
        vmem=24,
    )


def forward_pass_body(
    s_ref, vectors, ha, hb, m0, m1, wo, wu, wd, ga, gb,
    oa, ob, middle, normed, slope, far, near,
    tokens, mixed, out_w, up_w, down_w, grads, grads_t, mid, norm, out, slopes, shares, sems
):
    rows, half = ha.shape[0], m0.shape[1]
    parts = far.shape[0]
    chunk = 2 * half
    c = s_ref[0]
    copies = Copies(sems)
    first = [
        copies.start(m0, mixed.at[:, :half]),
        copies.start(m1, mixed.at[:, half:]),
        copies.start(wo.at[pl.ds(pl.multiple_of(c * half, half), half), :], out_w.at[:half, :]),
        copies.start(wo.at[pl.ds(pl.multiple_of((1 - c) * half, half), half), :], out_w.at[half:, :]),
        copies.start(ha, tokens.at[:rows, :]),
        copies.start(hb, tokens.at[rows:, :]),
    ]

    def ask(here):
        return (copies.start(wu.at[:, here], up_w.at[:, here]), copies.start(wd.at[here, :], down_w.at[here, :]))

    steps = [slice(low * chunk, high * chunk) for low, high in stretches(parts)]
    for copy in first:
        copy.wait()
    weights = [ask(steps[0])]
    turn = [copies.start(ga, grads.at[:rows, :]), copies.start(gb, grads.at[rows:, :])]
    mid[...] = tokens[...].astype(F32) + vectors[0:1, :] + mm(mixed[...], out_w[...])
    unit, _ = normalize(mid[...])
    norm[...] = (unit * vectors[2:3, :]).astype(BF16)
    copies.out(mid, middle)
    copies.out(norm, normed)
    for copy in turn:
        copy.wait()
    grads_t[...] = grads[...].T
    for i, here in enumerate(steps):
        if i + 1 < len(steps):
            weights.append(ask(steps[i + 1]))
        for copy in weights[i]:
            copy.wait()
        active, slopes[:, here] = gelu_both(mm(norm[...], up_w[:, here]))
        term = mm(active, down_w[here, :])
        out[...] = (mid if i == 0 else out)[...] + term
        value = mm(grads_t[...], active).astype(BF16)
        low, high = stretches(parts)[i]
        for part in range(low, high):
            for side in range(2):
                at = (part - low) * chunk + side * half
                shares[side, part] = value[:, at : at + half]
        copies.out(slopes.at[:, here], slope.at[:, here])
        copies.out(shares.at[1 - c, low:high], far.at[low:high])
        copies.out(shares.at[c, low:high], near.at[low:high])
    tokens[...] = out[...].astype(BF16)
    copies.out(tokens.at[:rows, :], oa)
    copies.out(tokens.at[rows:, :], ob)
    copies.finish()


def forward_pass(scalars, ha, hb, vectors, mine, other, w_out, w_up, w_down, ga, gb, parts, order=None):
    rows, width = ha.shape
    count, half = mine.shape
    ff = w_up.shape[1]
    outs = [
        jax.ShapeDtypeStruct((rows, width), BF16),
        jax.ShapeDtypeStruct((rows, width), BF16),
        pltpu.HBM((count, width), F32),
        pltpu.HBM((count, width), BF16),
        pltpu.HBM((count, ff), BF16),
        pltpu.HBM((parts, width, half), BF16),
        pltpu.HBM((parts, width, half), BF16),
    ]
    scratch = [
        pltpu.VMEM((count, width), BF16),
        pltpu.VMEM((count, width), BF16),
        pltpu.VMEM((width, width), BF16),
        pltpu.VMEM((width, ff), BF16),
        pltpu.VMEM((ff, width), BF16),
        pltpu.VMEM((count, width), BF16),
        pltpu.VMEM((width, count), BF16),
        pltpu.VMEM((count, width), F32),
        pltpu.VMEM((count, width), BF16),
        pltpu.VMEM((count, width), F32),
        pltpu.VMEM((count, ff), BF16),
        pltpu.VMEM((2, parts, width, half), BF16),
        pltpu.SemaphoreType.DMA((12 + 5 * parts,)),
    ]
    return call(
        forward_pass_body,
        "forward_pass",
        scalars,
        (vectors, ha, hb, mine, other, in_hbm(w_out), in_hbm(w_up), in_hbm(w_down), ga, gb),
        [whole(vectors.shape)] + [ANY] * 9,
        outs,
        [ANY] * 7,
        scratch=scratch,
        vmem=35,
        order=order,
        us=14,
    )


def feed_back_body(
    s_ref, vectors, ga, gb, normed, slope, wu, wd, middle, m0, m1, wo,
    grad_middle, gm_near, gm_far, gain_grad, *rest, aligned
):
    shares = rest[:2]
    grads, norm, norm_t, slopes, up_w, down_w, sums, mid, mixed, out_w, heads, held, *natural, sems = rest[2:]
    rows = ga.shape[0]
    half = m0.shape[1]
    parts = held.shape[1]
    chunk = wu.shape[1] // parts
    c = s_ref[0]
    copies = Copies(sems)
    first = [copies.start(ga, grads.at[:rows, :]), copies.start(gb, grads.at[rows:, :]), copies.start(normed, norm)]

    def ask(here):
        return (
            copies.start(wd.at[here, :], down_w.at[here, :]),
            copies.start(slope.at[:, here], slopes.at[:, here]),
            copies.start(wu.at[:, here], up_w.at[:, here]),
        )

    steps = [slice(low * chunk, high * chunk) for low, high in stretches(parts)]
    weights = [ask(steps[0])]
    for copy in first:
        copy.wait()
    norm_t[...] = norm[...].T
    last = []
    for i, here in enumerate(steps):
        if i + 1 < len(steps):
            weights.append(ask(steps[i + 1]))
        else:
            last = [
                copies.start(middle, mid),
                copies.start(wo.at[pl.ds(pl.multiple_of(c * half, half), half), :], out_w.at[:half, :]),
                copies.start(wo.at[pl.ds(pl.multiple_of((1 - c) * half, half), half), :], out_w.at[half:, :]),
                copies.start(m0, mixed.at[c]),
                copies.start(m1, mixed.at[1 - c]),
            ]
        for copy in weights[i]:
            copy.wait()
        grad_upper = (mm(grads[...], down_w[here, :], NT) * slopes[:, here].astype(F32)).astype(BF16)
        term = mm(grad_upper, up_w[:, here], NT)
        sums[...] = term if i == 0 else sums[...] + term
        value = mm(norm_t[...], grad_upper).astype(BF16)
        low, high = stretches(parts)[i]
        for part in range(low, high):
            mine = value[:, (part - low) * chunk : (part - low + 1) * chunk]
            if aligned:
                mine = mine.reshape(held.shape[2], 2, held.shape[3], chunk)
                held[0, part, :, :, :chunk] = mine[:, 0]
                held[1, part, :, :, :chunk] = mine[:, 1]
            else:
                held[0, part] = mine
        if not aligned:
            copies.out(held.at[0, low:high], shares[0].at[low:high])
    for copy in last:
        copy.wait()
    unit, root = normalize(mid[...])
    back, gain_sum = norm_back(sums[...], unit, root, vectors[2:3, :])
    gain_grad[...] = gain_sum
    mid[...] = grads[...].astype(F32) + back
    copies.out(mid, grad_middle)
    low_grad = mid[...].astype(BF16)
    heads[...] = mm(low_grad, out_w[...], NT).astype(BF16)
    copies.out(heads.at[:, :half], gm_near)
    copies.out(heads.at[:, half:], gm_far)
    turned = jnp.concatenate([mixed[0], mixed[1]], axis=1).T
    value = mm(turned, low_grad).astype(BF16)
    if aligned:
        blocks, own = held.shape[2:4]
        value = value.reshape(blocks, 2, own, 2 * half)
        cols = 2 * half // parts
        lanes = held.shape[4] - chunk
        for part in range(parts):
            mine = value[..., part * cols : (part + 1) * cols]
            pad = jnp.zeros(mine.shape[:-1] + (lanes - cols,), BF16)
            mine = jnp.concatenate([mine, pad], axis=-1)
            held[0, part, :, :, chunk:] = mine[:, 0]
            held[1, part, :, :, chunk:] = mine[:, 1]
        copies.out(held.at[1 - c], shares[0])
        copies.out(held.at[c], shares[1])
    else:
        natural[0][...] = value
        copies.out(natural[0], shares[1])
    copies.finish()


def feed_back(
    scalars, vectors, ga, gb, normed, slope, w_up, w_down, middle, mine, other, w_out, parts, blocks, lanes, aligned,
    order=None,
):
    rows, width = ga.shape
    count, half = 2 * rows, width // 2
    ff = w_up.shape[1]
    chunk = ff // parts
    if aligned:
        shares = [pltpu.HBM((parts, blocks, width // blocks // 2, lanes), BF16)] * 2
        held = [pltpu.VMEM((2,) + shares[0].shape, BF16)]
    else:
        shares = [jax.ShapeDtypeStruct((parts, width, chunk), BF16), jax.ShapeDtypeStruct((width, width), BF16)]
        held = [pltpu.VMEM((1,) + shares[0].shape, BF16), pltpu.VMEM((width, width), BF16)]
    scratch = [
        pltpu.VMEM((count, width), BF16),
        pltpu.VMEM((count, width), BF16),
        pltpu.VMEM((width, count), BF16),
        pltpu.VMEM((count, ff), BF16),
        pltpu.VMEM((width, ff), BF16),
        pltpu.VMEM((ff, width), BF16),
        pltpu.VMEM((count, width), F32),
        pltpu.VMEM((count, width), F32),
        pltpu.VMEM((2, count, half), BF16),
        pltpu.VMEM((width, width), BF16),
        pltpu.VMEM((count, width), BF16),
    ]
    scratch += held + [pltpu.SemaphoreType.DMA((13 + 5 * parts,))]
    outs = [
        pltpu.HBM((count, width), F32),
        pltpu.HBM((count, half), BF16),
        pltpu.HBM((count, half), BF16),
        jax.ShapeDtypeStruct((1, width), F32),
    ]
    return call(
        functools.partial(feed_back_body, aligned=aligned),
        "feed_back",
        scalars,
        (vectors, ga, gb, in_hbm(normed), in_hbm(slope), in_hbm(w_up), in_hbm(w_down), in_hbm(middle), mine, other, in_hbm(w_out)),
        [whole(vectors.shape)] + [ANY] * 10,
        outs + shares,
        [ANY] * 3 + [whole((1, width))] + [ANY] * 2,
        scratch=scratch,
        vmem=48,
        order=order,
        us=18,
    )


def attend_back_body(s_ref, *refs, pair):
    qs, dos, outs, lses = refs[0:2], refs[2:4], refs[4:6], refs[6:8]
    k0, k1, v0, v1, dq0, dq1, dk, dv, keys, vals = refs[8:]
    count = qs[0].shape[0]
    keys[:count, :], keys[count:, :] = k0[...], k1[...]
    vals[:count, :], vals[count:, :] = v0[...], v1[...]
    lanes = lax.broadcasted_iota(jnp.int32, (1, 128), 1)
    picks = lax.broadcasted_iota(jnp.int32, (8, 128), 1) // HEAD_DIM == lax.broadcasted_iota(jnp.int32, (8, 128), 0)
    picks = picks.astype(BF16)
    keys_t = keys[...].T
    turned = {}
    inners = []
    for b in range(2):
        product = dos[b][...].astype(F32) * outs[b][...].astype(F32)
        high = product.astype(BF16)
        low = (product - high.astype(F32)).astype(BF16)
        inners.append(mm(picks, high, NT) + mm(picks, low, NT))
        turned[b] = (qs[b][...].T, dos[b][...].T)
    grads_q = [[], []]
    grads_k, grads_v = [], []
    for h in range(2):
        head = slice(64 * h, 64 * h + 64)
        mask = (lanes >= 64) == (h == 1)
        grad_k = grad_v = None
        for b in range(2):
            q_head = jnp.where(mask, qs[b][...], jnp.zeros_like(qs[b][...]))
            do_head = jnp.where(mask, dos[b][...], jnp.zeros_like(dos[b][...]))
            weights = jnp.exp(mm(keys[...], q_head, NT) - lses[b][2 * pair + h : 2 * pair + h + 1, :])
            grad_weights = mm(vals[...], do_head, NT)
            grad_scores = (weights * (grad_weights - inners[b][h : h + 1, :])).astype(BF16)
            term = mm(turned[b][1][head], weights.astype(BF16), NT)
            grad_v = term if b == 0 else grad_v + term
            term = mm(turned[b][0][head], grad_scores, NT)
            grad_k = term if b == 0 else grad_k + term
            grads_q[b].append(mm(keys_t[head], grad_scores))
        grads_k.append(grad_k)
        grads_v.append(grad_v)
    for b, out in enumerate((dq0, dq1)):
        out[...] = (jnp.concatenate(grads_q[b], axis=0).T * SCALE).astype(BF16)
    dk[...] = jnp.concatenate(grads_k, axis=0).T.astype(BF16)
    dv[...] = jnp.concatenate(grads_v, axis=0).T.astype(BF16)


def attend_back(scalars, near, far, pair, order=None):
    count, half = near[1].shape
    ins = [a for both in zip(near, far) for a in both] + [near[0], far[0]] * 2
    pairs = half // 128
    lane = lambda t: pl.BlockSpec((count, 128), lambda g, s: (0, t * pairs + pair))
    one = jax.ShapeDtypeStruct((count, 128), BF16)
    two = jax.ShapeDtypeStruct((2 * count, 128), BF16)
    outs = [one, one, two, two]
    return call(
        functools.partial(attend_back_body, pair=pair),
        "attend_back",
        scalars,
        ins,
        [lane(0)] * 6 + [whole(near[3].shape)] * 2 + [lane(1), lane(1), lane(2), lane(2)],
        outs,
        [whole(o.shape) for o in outs],
        scratch=[pltpu.VMEM((2 * count, 128), BF16), pltpu.VMEM((2 * count, 128), BF16)],
        order=order,
        us=6.5,
        vmem=28,
    )


def side_by_side(refs):
    return jnp.concatenate([refs[3 * pair + t][...] for t in range(3) for pair in range(len(refs) // 3)], axis=1)


def pair_specs(grads, part, count):
    arrays, specs = [], []
    for near, far, dk, dv in grads:
        arrays += [(near, far)[part], dk, dv]
        specs += [whole((count, 128))] + [pl.BlockSpec((count, 128), lambda g, s: (part, 0))] * 2
    return arrays, specs


def project_back_body(s_ref, weight, *refs):
    refs[-1][...] = mm(side_by_side(refs[:-1]), weight[...], NT).astype(BF16)


def project_back(scalars, grads, weight, part, order=None):
    count = grads[0][0].shape[0]
    arrays, specs = pair_specs(grads, part, count)
    out = jax.ShapeDtypeStruct((count, weight.shape[0]), BF16)
    return call(
        project_back_body,
        "project_back",
        scalars,
        [weight] + arrays,
        [whole(weight.shape)] + specs,
        [out],
        [whole(out.shape)],
        order=order,
        us=2,
        vmem=16,
    )[0]


def turn_body(s_ref, ha, hb, xa, xb, vectors, out):
    rows = ha.shape[0]
    for at, block in enumerate((ha, hb, xa, xb)):
        unit, _ = normalize(block[...].astype(F32) + vectors[0:1, :])
        out[:, at * rows : (at + 1) * rows] = (unit * vectors[1:2, :]).astype(BF16).T


def turned_tokens(scalars, ha, hb, xa, xb, vectors, order=None):
    ins = (ha, hb, xa, xb, vectors)
    out = jax.ShapeDtypeStruct((ha.shape[1], 4 * ha.shape[0]), BF16)
    return call(
        turn_body, "turned", scalars, ins, [whole(a.shape) for a in ins], [out], [whole(out.shape)], order=order, us=2.5, vmem=16
    )[0]


def qkv_weight_body(s_ref, turned, *refs, pairs, aligned):
    out = refs[4 * pairs]
    grads = refs[-2] if aligned else refs[-1]
    count = refs[0].shape[0]
    lanes = grads.shape[1] // 3
    for pair in range(pairs):
        near, far, dk, dv = refs[4 * pair : 4 * pair + 4]
        here = slice(128 * pair, 128 * pair + 128)
        grads[:count, here] = near[...]
        grads[count:, here] = far[...]
        grads[:, lanes + 128 * pair : lanes + 128 * pair + 128] = dk[...]
        grads[:, 2 * lanes + 128 * pair : 2 * lanes + 128 * pair + 128] = dv[...]
    value = mm(turned[...], grads[...]).astype(BF16)
    if not aligned:
        out[...] = value
        return
    out[...] = value.reshape(out.shape)
    copies = Copies(refs[-1])
    bits = out.shape[0].bit_length() - 1
    for half, order in enumerate(orders(bits)):
        send = refs[4 * pairs + 1 + half]
        for g in range(send.shape[0]):
            copies.out(out.at[step_index(order, 0, s_ref[1], g), half], send.at[g])
    copies.finish()


def qkv_weight(scalars, turned, grads, blocks, aligned, order=None):
    width, count = turned.shape
    pairs = len(grads)
    lanes = 3 * 128 * pairs
    own = width // blocks // 2
    ins = [turned] + [a for four in grads for a in four]
    outs = [pltpu.HBM((blocks, 2, own, lanes) if aligned else (width, lanes), BF16)]
    specs = [whole(outs[0].shape)]
    scratch = [pltpu.VMEM((count, lanes), BF16)]
    if aligned:
        outs += [jax.ShapeDtypeStruct((blocks // 2, own, lanes), BF16)] * 2
        specs += [ANY] * 2
        scratch += [pltpu.SemaphoreType.DMA((blocks,))]
    return call(
        functools.partial(qkv_weight_body, pairs=pairs, aligned=aligned),
        "qkv_weight",
        scalars,
        ins,
        [whole(a.shape) for a in ins],
        outs,
        specs,
        scratch=scratch,
        order=order,
        us=4,
        vmem=24,
    )


def base_body(s_ref, ha, hb, vectors, grad_middle, weight, part_in, gain_two, *refs):
    ia, ib, sums = refs[-3:]
    rows = ha.shape[0]
    gain = vectors[1:2, :]
    grad_normed = mm(side_by_side(refs[:-3]), weight[...], NT) + part_in[...].astype(F32)
    gain_sum, base_sum = None, None
    for at, (block, out) in enumerate(((ha, ia), (hb, ib))):
        here = slice(at * rows, (at + 1) * rows)
        unit, root = normalize(block[...].astype(F32) + vectors[0:1, :])
        back, part = norm_back(grad_normed[here], unit, root, gain)
        grad = grad_middle[here, :] + back
        out[...] = grad.astype(BF16)
        gain_sum = part if gain_sum is None else gain_sum + part
        tokens = jnp.sum(grad, axis=0, keepdims=True)
        base_sum = tokens if base_sum is None else base_sum + tokens
    sums[0:1, :] = gain_sum
    sums[1:2, :] = gain_two[...]
    sums[2:3, :] = base_sum


def base_back(scalars, ha, hb, vectors, grad_middle, grads, weight, part_in, gain_two, order=None):
    rows, width = ha.shape
    arrays, specs = pair_specs(grads, 0, 2 * rows)
    grad_middle = in_hbm(grad_middle)
    ins = (ha, hb, vectors, grad_middle, weight, part_in, gain_two)
    outs = [
        jax.ShapeDtypeStruct((rows, width), BF16),
        jax.ShapeDtypeStruct((rows, width), BF16),
        jax.ShapeDtypeStruct((3, width), F32),
    ]
    return call(
        base_body,
        "base_back",
        scalars,
        list(ins) + arrays,
        [Staged(a) if a is grad_middle else whole(a.shape) for a in ins] + specs,
        outs,
        [whole(o.shape) for o in outs],
        order=order,
        us=3,
        vmem=24,
    )


def meet_body(s_ref, held, got, out, *, which, at):
    rows = held.shape[0] - 2
    out[0:2, :] = held[0:2, :] + got[0:2, :]
    if which is None:
        out[2:, :] = held[2:, :] + got[2:, :]
        return
    first = bit(s_ref[which], at) == 0
    mine, other = held[2:, :], got[2:, :]
    out[2 : 2 + rows, :] = jnp.where(first, mine, other)
    out[2 + rows :, :] = jnp.where(first, other, mine)


def meet(scalars, held, got, which, at, order=None):
    rows, lanes = held.shape
    out = jax.ShapeDtypeStruct((rows if which is None else 2 * rows - 2, lanes), F32)
    return call(
        functools.partial(meet_body, which=which, at=at),
        "meet",
        scalars,
        (held, got),
        [whole(held.shape)] * 2,
        [out],
        [whole(out.shape)],
        order=order,
        us=0.7,
        vmem=4,
    )[0]


def table_body(s_ref, sums, out):
    out[...] = jnp.zeros_like(out)
    for at in range(sums.shape[0] - 2):
        here = pl.ds(s_ref[at], 1)
        out[here, :] = out[here, :] + sums[at + 2 : at + 3, :]


def table_of(steps, sums, count, order=None):
    out = pltpu.HBM((count, sums.shape[1]), F32)
    return call(
        table_body,
        "table",
        steps,
        (sums,),
        [whole(sums.shape)],
        [out],
        [whole(out.shape)],
        order=order,
        us=2.5,
        vmem=12,
    )[0]


def fold(name, scalars, outs, order=None, split=False):
    ins, specs, known = [], [], {}
    for _, _, entries in outs:
        for _, _, terms in entries:
            for array, _, far in terms:
                if id(array) not in known:
                    known[id(array)] = len(ins)
                    ins.append(in_hbm(array) if far else array)
                    specs.append(ANY)
    scratch = [pltpu.VMEM(block, t[0].dtype) for _, _, entries in outs for _, block, terms in entries for t in terms]

    def body(s_ref, *refs):
        arrays, targets = refs[: len(ins)], refs[len(ins) : len(ins) + len(shapes)]
        held = list(refs[len(ins) + len(shapes) : -1])
        copies = Copies(refs[-1])
        if split:
            sides, targets = targets, [held.pop()]
        waiting = []
        for (_, _, entries), target in zip(outs, targets):
            for to, _, terms in entries:
                mine = []
                for array, where, _ in terms:
                    slot = held.pop(0)
                    mine.append((copies.start(arrays[known[id(array)]].at[where(s_ref)], slot), slot))
                waiting.append((target, to, mine))
        for target, to, mine in waiting:
            total = None
            for copy, slot in mine:
                copy.wait()
                total = slot[...].astype(F32) if total is None else total + slot[...].astype(F32)
            target[to] = total.astype(target.dtype)
        if split:
            copies.out(targets[0].at[1 - s_ref[0]], sides[0])
            copies.out(targets[0].at[s_ref[0]], sides[1])
            copies.finish()

    shapes = [jax.ShapeDtypeStruct(o[0], o[1]) for o in outs]
    if split:
        shapes = [jax.ShapeDtypeStruct(outs[0][0][1:], outs[0][1])] * 2
        scratch.append(pltpu.VMEM(outs[0][0], outs[0][1]))
    return call(
        body,
        name,
        scalars,
        ins,
        specs,
        shapes,
        [ANY if split else whole(o.shape) for o in shapes],
        scratch=scratch + [pltpu.SemaphoreType.DMA((len(scratch) + 2,))],
        order=order,
        us=1.5,
        vmem=16,
    )


def bit(value, at):
    return (value >> at) & 1


def orders(bits):
    return (list(range(bits)), list(range(bits))[::-1])


def step_index(order, step, own, g):
    value = (1 - bit(own, order[step])) << order[step]
    for at in order[:step]:
        value = value + (bit(own, at) << at)
    for i, at in enumerate(order[step + 1 :]):
        value = value + (bit(g, i) << at)
    return value


def held_index(order, step, block):
    value = block * 0
    for i, at in enumerate(order[step + 1 :]):
        value = value + (bit(block, at) << i)
    return value


class Reduction:
    def __init__(self, swap, pieces, seq_bits, roots, has_seq=True):
        self.swap, self.pieces, self.seq_order = swap, pieces, list(range(seq_bits))
        self.steps = len(pieces[0][0])
        self.roots = [[(low, high, list(terms)) for low, high, terms in roots] for _ in pieces]
        self.rows = sum(p[2] for p in pieces)
        self.lanes = roots[-1][1]
        self.lead = (1 << seq_bits,) if has_seq else ()
        self.got = [[] for _ in pieces]
        self.got_seq = []

    def entries(self, at, to, block_of, seq_of=None):
        order, first, rows = self.pieces[at]
        out = []
        for low, high, roots in self.roots[at]:
            lanes, here = pl.ds(low, high - low), pl.ds(first, rows)
            terms = []
            for array, where, far in roots:
                place = lambda s, where=where: where(block_of(s), None if seq_of is None else seq_of(s), here)
                terms.append((array, place, far))
            for step, array in self.got[at]:

                def place(s, step=step, lanes=lanes):
                    block = held_index(order, step, block_of(s))
                    if not self.lead:
                        return (block, slice(None), lanes)
                    return (block, slice(None) if seq_of is None else seq_of(s), slice(None), lanes)

                terms.append((array, place, False))
            if seq_of is not None:
                for step, array in self.got_seq:
                    place = lambda s, step=step, lanes=lanes: (
                        held_index(self.seq_order, step, seq_of(s)),
                        here,
                        lanes,
                    )
                    terms.append((array, place, False))
            block = (self.lead if seq_of is None else ()) + (rows, high - low)
            out.append((to + (Ellipsis, slice(low, high)), block, terms))
        return out

    def leaving(self, step):
        count = 1 << (self.steps - 1 - step)
        outs = []
        for at, (order, _, rows) in enumerate(self.pieces):
            entries = []
            for g in range(count):
                entries += self.entries(at, (g,), lambda s, g=g, order=order: step_index(order, step, s[1], g))
            outs.append(((count,) + self.lead + (rows, self.lanes), BF16, entries))
        if step == self.steps - 1 and self.lead:
            for at, (_, _, rows) in enumerate(self.pieces):
                outs.append((self.lead + (rows, self.lanes), F32, self.entries(at, (), lambda s: s[1])))
        return outs

    def send(self, step, sent):
        count = len(self.pieces)
        if len(sent) > count:
            for at, kept in enumerate(sent[count:]):
                self.got[at] = []
                for low, high, terms in self.roots[at]:
                    where = lambda block, seq, rows, low=low, high=high: (
                        slice(None) if seq is None else seq,
                        slice(None),
                        pl.ds(low, high - low),
                    )
                    terms[:] = [(kept, where, False)]
        for at, (order, _, _) in enumerate(self.pieces):
            self.got[at].append((step, self.swap(sent[at], 2 << order[step], 0)))

    def leaving_seq(self, step):
        count = 1 << (len(self.seq_order) - 1 - step)
        entries = []
        for g in range(count):
            seq_of = lambda s, g=g: step_index(self.seq_order, step, s[2], g)
            for at, (_, first, rows) in enumerate(self.pieces):
                entries += self.entries(at, (g, slice(first, first + rows)), lambda s: s[1], seq_of)
        return [((count, self.rows, self.lanes), BF16, entries)]

    def send_seq(self, step, sent):
        self.got_seq.append((step, self.swap(sent[0], 0, 1 << self.seq_order[step])))

    def last(self):
        out = []
        for at, (low, high, _) in enumerate(self.roots[0]):
            entries = []
            for piece, (_, first, rows) in enumerate(self.pieces):
                _, block, terms = self.entries(piece, (), lambda s: s[1], lambda s: s[2])[at]
                entries.append(((slice(first, first + rows),), block, terms))
            out.append(((self.rows, high - low), F32, entries))
        return out


def columns_body(s_ref, mine, other, keep, *sends):
    even = s_ref[0] == 0
    here, there = mine[...].astype(F32), other[...].astype(F32)
    half = here.shape[1] // 3
    first, second = jnp.where(even, here, there), jnp.where(even, there, here)
    columns = []
    for t in range(3):
        columns += [first[:, t * half : t * half + half], second[:, t * half : t * half + half]]
    columns = jnp.concatenate(columns, axis=1)
    lanes = keep.shape[1]
    for at, target in enumerate((keep, *sends)):
        for part in range(len(sends) + 1):

            @pl.when((s_ref[2] ^ at) == part)
            def _(target=target, part=part):
                target[...] = columns[:, part * lanes : part * lanes + lanes].astype(target.dtype)


def on_device(
    row_count, seq_count, hidden_in, timesteps, step_table, gain_one, w_qkv, w_out, gain_two, w_up, w_down, out_grad
):
    seqs_here, tokens_here, width = hidden_in.shape
    ff = w_up.shape[1]
    half = width // 2
    blocks = row_count // 2
    block_bits = blocks.bit_length() - 1
    seq_bits = seq_count.bit_length() - 1
    r = lax.axis_index("rows")
    z = lax.axis_index("seq")
    c = lax.rem(r, 2)
    b = lax.div(r, 2)
    odd = lax.rem(z, 2)
    axes = ("rows", "seq")

    def flat(row, seq):
        return row * seq_count + seq

    def swap(value, row_bit, seq_bit=0):
        pairs = [
            (flat(i, j), flat(i ^ row_bit, j ^ seq_bit)) for i in range(row_count) for j in range(seq_count)
        ]
        return lax.ppermute(value, axes, pairs)

    def core_swap(value):
        return swap(value, 1)

    moves = []
    for turn in range(2):
        moves.append(
            [
                (flat(2 * p + e, j), flat(2 * p + j // 2, 2 * e + (j + turn) % 2))
                for p in range(blocks)
                for e in range(2)
                for j in range(seq_count)
            ]
        )

    def gather_tokens(leaving):
        return tuple(lax.ppermute(value, axes, move) for value, move in zip(leaving, moves))

    def share(value, at, axis):
        return lax.dynamic_index_in_dim(value, at, axis, keepdims=False)

    def send_back(*values):
        return [lax.ppermute(value, axes, [(t, s) for s, t in move]) for value, move in zip(values, moves)]

    scalars = jnp.stack([c, b, z]).astype(jnp.int32)

    steps_all = lax.all_gather(timesteps, "rows", axis=0, tiled=True)
    step_now = lax.dynamic_index_in_dim(steps_all, seq_count * b + z, 0, keepdims=False)
    row = lax.dynamic_slice_in_dim(step_table, step_now, 1, 0).astype(F32)

    order = Order()
    weight, vectors = prepare(scalars, row, gain_one[None, :], gain_two[None, :], w_qkv)
    ha, hb = gather_tokens([share(hidden_in, at, 0) for at in (odd, 1 - odd)])
    xa, xb = core_swap(ha), core_swap(hb)
    near = qkv(scalars, ha, hb, vectors, weight, order=order, us=8)
    late_grad, _, _ = lax.optimization_barrier((out_grad, ha, hb))
    ga, gb = gather_tokens([share(late_grad, at, 0) for at in (odd, 1 - odd)])
    far = qkv(scalars, xa, xb, vectors, weight, order=order)
    mixed_far, lse_far = attend(scalars, far, near, far, order=order)
    mixed_in = core_swap(mixed_far)
    mixed_near, lse_near = attend(scalars, near, near, far, order=order)

    parts = seq_count
    unit = ff // row_count
    own_rows, seq_cols, up_cols = width // row_count, width // seq_count, ff // seq_count
    whole_units = blocks == parts and unit % 128 == 0
    whole_rows = own_rows % 32 == 0

    oa, ob, middle, normed_two, slope, down_far, down_near = forward_pass(
        scalars, ha, hb, vectors, mixed_near, mixed_in, w_out, w_up, w_down, ga, gb, parts, order=order
    )
    if not whole_units:
        sides = [jnp.where(c == side, down_near, down_far) for side in range(2)]
        natural = jnp.concatenate(sides, axis=2).transpose(1, 0, 2).reshape(parts, seq_cols, blocks, 2, unit)
        down_far, down_near = (share(natural, at, 3).transpose(2, 0, 1, 3) for at in (1 - c, c))
    down_shape = (blocks, parts, seq_cols, unit)
    down_far, down_near = down_far.reshape(down_shape), down_near.reshape(down_shape)
    down_in = core_swap(down_far)
    out_back = send_back(oa, ob)

    lanes = -(-(up_cols + seq_cols) // 256) * 256
    grad_middle, gm_near, gm_far, gain_two_part, up_far, up_near = feed_back(
        scalars, vectors, ga, gb, normed_two, slope, w_up, w_down, middle, mixed_near, mixed_in, w_out,
        parts, blocks, lanes, whole_rows, order=order,
    )
    if not whole_rows:
        up_all = up_far.reshape(parts, blocks, 2, own_rows, up_cols)
        out_all = up_near.reshape(blocks, 2, own_rows, parts, seq_cols).transpose(3, 0, 1, 2, 4)
        blank = jnp.zeros(up_all.shape[:-1] + (lanes - up_cols - seq_cols,), BF16)
        natural = jnp.concatenate([up_all, out_all, blank], axis=-1)
        up_far, up_near = (share(natural, at, 2) for at in (1 - c, c))
    gm_in = core_swap(gm_far)
    up_in = core_swap(up_far)

    fold_over = functools.partial(fold, "reduce", scalars, order=order)
    both = orders(block_bits)
    every = slice(None)

    def by_block(block, seq, rows):
        return (block, every if seq is None else seq, rows)

    def by_seq(block, seq, rows):
        return (every if seq is None else seq, block, rows)

    def pieces(rows, turn):
        if rows % 32:
            return [(both[turn], 0, rows)]
        return [(both[0], 0, rows // 2), (both[1], rows // 2, rows // 2)]

    def step_over(reductions, leaving, send, step):
        outs = [leaving(r, step) for r in reductions]
        sent = list(fold_over([o for out in outs for o in out]))
        for reduction, out in zip(reductions, outs):
            send(reduction, step, sent[: len(out)])
            del sent[: len(out)]

    step_blocks = functools.partial(step_over, leaving=Reduction.leaving, send=Reduction.send)
    step_seq = functools.partial(step_over, leaving=Reduction.leaving_seq, send=Reduction.send_seq)

    down = Reduction(
        swap, pieces(seq_cols, 0), seq_bits, [(0, unit, [(down_near, by_block, True), (down_in, by_block, False)])]
    )
    up = Reduction(
        swap, pieces(own_rows, 1), seq_bits, [(0, lanes, [(up_near, by_seq, True), (up_in, by_seq, False)])]
    )
    step_blocks([down], step=0)
    turned = turned_tokens(scalars, ha, hb, xa, xb, vectors, order=order)
    step_blocks([up], step=0)
    sides = ((near, gm_near, mixed_near, lse_near), (far, gm_in, mixed_far, lse_far))
    grads = []
    for pair in range(half // 128):
        grads.append(attend_back(scalars, *sides, pair, order=order))
        if pair == 0:
            for step in range(1, block_bits):
                step_blocks([down], step=step)
        if pair == 1:
            out_hidden = returned_blocks(scalars, *out_back, order=order)
    step_seq([down], step=0)
    part_far = project_back(scalars, grads, weight, 1, order=order)
    part_in = core_swap(part_far)
    for step in range(1, block_bits):
        step_blocks([up], step=step)
    qkv_w = qkv_weight(scalars, turned, grads, blocks, whole_rows, order=order)
    qkv_blocks = qkv_w[0].reshape(blocks, 2 * own_rows, 3 * half)
    project = Reduction(
        swap,
        [(both[h], h * own_rows, own_rows) for h in range(2)],
        seq_bits,
        [(0, 3 * half, [(qkv_blocks, lambda block, seq, rows: (block, rows), True)])],
        False,
    )
    if whole_rows:
        project.send(0, qkv_w[1:])
    else:
        qkv_blocks = qkv_w[0].reshape(blocks, 2, own_rows, 3 * half)
        project.roots = [
            [(0, 3 * half, [(qkv_blocks, lambda block, seq, rows, h=h: (block, h), False)])] for h in range(2)
        ]
        step_blocks([project], step=0)
    ia, ib, held = base_back(
        scalars, ha, hb, vectors, grad_middle, grads, weight, part_in, gain_two_part, order=order
    )
    in_back = send_back(ia, ib)

    meetings = [(None, 0, 1, 0)]
    meetings += [(2, at, 0, 1 << at) for at in range(seq_bits)]
    meetings += [(1, at, 2 << at, 0) for at in range(block_bits)]

    def next_meeting(held):
        which, at, row_bit, seq_bit = meetings.pop(0)
        return meet(scalars, held, swap(held, row_bit, seq_bit), which, at, order=order)

    step_seq([up], step=0)
    held = next_meeting(held)
    held = next_meeting(held)
    for step in range(1, block_bits):
        step_blocks([project], step=step)
    for step in range(1, seq_bits):
        step_seq([down], step=step)
    held = next_meeting(held)
    in_grad = returned_blocks(scalars, *in_back, order=order)
    entries = []
    for h in range(2):
        for _, block, terms in project.entries(h, (), lambda s: s[1]):
            entries.append(((h,), block, terms))
    qkv_far, qkv_mine = fold_over([((2, own_rows, 3 * half), BF16, entries)], split=True)
    while len(meetings) > 1:
        held = next_meeting(held)

    shape = (own_rows, 6 * half // parts)
    qkv_keep, *qkv_sends = call(
        columns_body,
        "qkv_columns",
        scalars,
        (qkv_mine, core_swap(qkv_far)),
        [whole(qkv_mine.shape)] * 2,
        [jax.ShapeDtypeStruct(shape, F32)] + [jax.ShapeDtypeStruct(shape, BF16)] * (parts - 1),
        [whole(shape)] * parts,
        vmem=12,
        order=order,
    )
    qkv_terms = [qkv_keep] + [swap(value, 0, at + 1) for at, value in enumerate(qkv_sends)]
    for step in range(1, seq_bits):
        step_seq([up], step=step)
    held = next_meeting(held)
    table = table_of(steps_all, held, step_table.shape[0], order=order)
    down_sum, up_all = fold_over(down.last() + up.last())
    entry = ((Ellipsis,), shape, [(value, lambda s: (slice(None),), False) for value in qkv_terms])
    qkv_shard = fold_over([(shape, F32, [entry])])[0]

    return (
        out_hidden,
        in_grad,
        table,
        held[0],
        qkv_shard,
        up_all[:, up_cols : up_cols + seq_cols],
        held[1],
        up_all[:, :up_cols],
        down_sum.T,
    )


def solution(mesh):
    tokens = P("rows", "seq", None)
    split = P("rows", "seq")
    in_specs = (tokens, P("rows"), P(), P(), P(), P(), P(), P(), P(), tokens)
    out_specs = (tokens, tokens, P(), P(), split, split, P(), split, split)
    body = functools.partial(on_device, mesh.shape["rows"], mesh.shape["seq"])
    return jax.shard_map(body, mesh=mesh, in_specs=in_specs, out_specs=out_specs, check_vma=False)
```

```python
import functools

import jax
import jax.numpy as jnp
from jax import lax
from jax.experimental import pallas as pl
from jax.experimental.pallas import tpu as pltpu
from jax.sharding import PartitionSpec as P

HEAD_DIM = 64
SCALE = HEAD_DIM ** (-0.5)
EPS = 1e-05
F32 = jnp.float32
BF16 = jnp.bfloat16
MIB = 1 << 20
PER_US = 1_000_000_000

NN = (((1,), (0,)), ((), ()))
NT = (((1,), (1,)), ((), ()))


def mm(a, b, dims=NN):
    return lax.dot_general(a, b, dims, preferred_element_type=F32)


def normalize(values):
    average = jnp.mean(values, axis=-1, keepdims=True)
    centred = values - average
    inverse_root = lax.rsqrt(jnp.mean(centred * centred, axis=-1, keepdims=True) + EPS)
    return (centred * inverse_root, inverse_root)


def norm_back(grad_normed, unit_rows, inverse_root, scale_gain):
    gained = grad_normed * scale_gain
    centred_grad = (
        gained
        - jnp.mean(gained, axis=-1, keepdims=True)
        - unit_rows * jnp.mean(gained * unit_rows, axis=-1, keepdims=True)
    )
    return (inverse_root * centred_grad, jnp.sum(grad_normed * unit_rows, axis=0, keepdims=True))


def whole(shape):
    return pl.BlockSpec(shape, lambda *_: (0,) * len(shape))


class Staged:
    def __init__(self, array):
        self.memory = pltpu.VMEM(array.shape, array.dtype)


class Order:
    def __init__(self):
        self.token = None


def call(
    body, name, scalars, ins, in_specs, outs, out_specs, grid=(1,), scratch=(), vmem=32, order=None, us=1.0, aliases=None
):
    ins, in_specs, outs, out_specs = list(ins), list(in_specs), list(outs), list(out_specs)
    count, given = len(ins), len(outs)
    staged = [at for at, spec in enumerate(in_specs) if isinstance(spec, Staged)]
    held = [in_specs[at].memory for at in staged]
    for at in staged:
        in_specs[at] = ANY
    waits = [] if order is None or order.token is None else [order.token]
    inner = body

    def body(scalars_ref, *refs):
        refs = list(refs)
        del refs[count : count + len(waits)]
        if order is not None:
            token = refs.pop(count + given)
            token[...] = jnp.zeros_like(token)
        if staged:
            sems, slots = refs.pop(), refs[len(refs) - len(held) :]
            del refs[len(refs) - len(held) :]
            copies = [pltpu.make_async_copy(refs[at], slot, sems.at[i]) for i, (at, slot) in enumerate(zip(staged, slots))]
            for copy in copies:
                copy.start()
            for at, slot in zip(staged, slots):
                refs[at] = slot
            for copy in copies:
                copy.wait()
        inner(scalars_ref, *refs)

    ins += waits
    in_specs += [ANY] * len(waits)
    if order is not None:
        outs.append(jax.ShapeDtypeStruct((8, 128), F32))
        out_specs.append(whole((8, 128)))
    scratch = list(scratch) + held + ([pltpu.SemaphoreType.DMA((len(staged),))] if staged else [])
    result = pl.pallas_call(
        body,
        name=name,
        grid_spec=pltpu.PrefetchScalarGridSpec(
            num_scalar_prefetch=1,
            grid=grid,
            in_specs=in_specs,
            out_specs=out_specs,
            scratch_shapes=scratch,
        ),
        out_shape=outs,
        input_output_aliases={at + 1: to for at, to in (aliases or {}).items()},
        cost_estimate=pl.CostEstimate(flops=int(us * PER_US), bytes_accessed=1 << 10, transcendentals=0),
        compiler_params=pltpu.CompilerParams(vmem_limit_bytes=vmem * MIB),
    )(scalars, *ins)
    result = list(result)
    if order is not None:
        order.token = result.pop()
    return result


def in_hbm(value):
    return pltpu.with_memory_space_constraint(value, pltpu.HBM)


ANY = pl.BlockSpec(memory_space=pl.ANY)


def gelu_both(upper):
    square = upper * upper
    turned = jnp.tanh(upper * (GELU_A + GELU_A * GELU_B * square))
    half_up = 0.5 + 0.5 * turned
    active = upper * half_up
    slope = half_up + active * (1.0 - turned) * (GELU_A + 3.0 * GELU_A * GELU_B * square)
    return active.astype(BF16), slope.astype(BF16)


class Copies:
    def __init__(self, sems):
        self.sems, self.count, self.outs = sems, 0, []

    def start(self, source, target):
        copy = pltpu.make_async_copy(source, target, self.sems.at[self.count])
        self.count += 1
        copy.start()
        return copy

    def out(self, source, target):
        self.outs.append(self.start(source, target))

    def finish(self):
        for copy in self.outs:
            copy.wait()


GELU_A, GELU_B = 0.7978845608028654, 0.044715


def stretches(parts):
    return [(at, min(at + 2, parts)) for at in range(0, parts, 2)]


def prepare_body(s_ref, row, first, second, wq, wk, wv, out, vectors):
    half = wq.shape[1]
    for t, w in enumerate((wq, wk, wv)):
        out[:, t * half : t * half + half] = w[...]
    for at, value in enumerate((row, first, second)):
        vectors[at : at + 1, :] = value[...]


def prepare(scalars, row, gain_one, gain_two, w_qkv, order=None):
    width = w_qkv.shape[0]
    half = width // 2
    specs = [whole((1, width))] * 3
    specs += [pl.BlockSpec((width, half), functools.partial(lambda t, g, s: (0, 2 * t + s[0]), t)) for t in range(3)]
    outs = [jax.ShapeDtypeStruct((width, 3 * half), BF16), jax.ShapeDtypeStruct((8, width), F32)]
    return call(
        prepare_body,
        "prepare",
        scalars,
        (row, gain_one, gain_two) + (in_hbm(w_qkv),) * 3,
        specs,
        outs,
        [whole(o.shape) for o in outs],
        order=order,
        us=2,
        vmem=12,
    )


def returned_body(s_ref, first, second, out, sems):
    at = bit(s_ref[2], 0)
    copies = Copies(sems)
    copies.out(first, out.at[at])
    copies.out(second, out.at[1 - at])
    copies.finish()


def returned_blocks(scalars, first, second, order=None):
    return call(
        returned_body,
        "returned",
        scalars,
        (first, second),
        [ANY] * 2,
        [pltpu.HBM((2,) + first.shape, first.dtype)],
        [ANY],
        scratch=[pltpu.SemaphoreType.DMA((2,))],
        order=order,
        us=3,
        vmem=4,
    )[0]


def qkv_body(s_ref, ha, hb, vectors, weight, out, normed):
    row, gain = vectors[0:1, :], vectors[1:2, :]
    rows = ha.shape[0]
    half = out.shape[1] // 3
    for at, block in enumerate((ha, hb)):
        unit, _ = normalize(block[...].astype(F32) + row)
        normed[pl.ds(at * rows, rows), :] = (unit * gain).astype(BF16)
    packed = mm(normed[...], weight[...]).astype(BF16)
    out[:, :half] = (packed[:, :half] * SCALE).astype(BF16)
    out[:, half:] = packed[:, half:]


def qkv(scalars, ha, hb, vectors, weight, order=None, us=2.3):
    rows, width = ha.shape
    ins = (ha, hb, vectors, weight)
    out = jax.ShapeDtypeStruct((2 * rows, weight.shape[1]), BF16)
    return call(
        qkv_body,
        "qkv",
        scalars,
        ins,
        [whole(a.shape) for a in ins],
        [out],
        [whole(out.shape)],
        scratch=[pltpu.VMEM((2 * rows, width), BF16)],
        order=order,
        us=us,
        vmem=16,
    )[0]


def attend_body(s_ref, q, k0, k1, v0, v1, mixed, lse):
    count, half = q.shape
    lanes = lax.broadcasted_iota(jnp.int32, (1, 128), 1)
    ones = jnp.ones((16, count), BF16)
    for pair in range(half // 128):
        cols = slice(128 * pair, 128 * pair + 128)
        q_pair = q[:, cols]
        vt = [v[:, cols].T for v in (v0, v1)]
        done = []
        for h in range(2):
            q_head = jnp.where((lanes >= 64) == (h == 1), q_pair, jnp.zeros_like(q_pair))
            scores = [mm(k[:, cols], q_head, NT) for k in (k0, k1)]
            highest = jnp.maximum(
                jnp.max(scores[0], axis=0, keepdims=True), jnp.max(scores[1], axis=0, keepdims=True)
            )
            total = None
            for part in range(2):
                weights = jnp.exp(scores[part] - highest).astype(BF16)
                left = jnp.concatenate([vt[part][64 * h : 64 * h + 64], ones], axis=0)
                term = mm(left, weights)
                total = term if total is None else total + term
            summed = total[64:65]
            done.append(total[:64] / summed)
            lse[2 * pair + h : 2 * pair + h + 1, :] = highest + jnp.log(summed)
        mixed[:, cols] = jnp.concatenate(done, axis=0).T.astype(BF16)


def attend(scalars, asked, near, far, order=None):
    count, half = asked.shape[0], asked.shape[1] // 3
    ins = (asked, near, far, near, far)
    outs = [jax.ShapeDtypeStruct((count, half), BF16), jax.ShapeDtypeStruct((8, count), F32)]
    return call(
        attend_body,
        "attend",
        scalars,
        ins,
        [pl.BlockSpec((count, half), functools.partial(lambda t, g, s: (0, t), t)) for t in (0, 1, 1, 2, 2)],
        outs,
        [whole(o.shape) for o in outs],
        order=order,
        us=6,
        vmem=24,
    )


def forward_pass_body(
    s_ref, vectors, ha, hb, m0, m1, wo, wu, wd, ga, gb,
    oa, ob, middle, normed, slope, far, near,
    tokens, mixed, out_w, up_w, down_w, grads, grads_t, mid, norm, out, slopes, shares, sems
):
    rows, half = ha.shape[0], m0.shape[1]
    parts = far.shape[0]
    chunk = 2 * half
    c = s_ref[0]
    copies = Copies(sems)
    first = [
        copies.start(m0, mixed.at[:, :half]),
        copies.start(m1, mixed.at[:, half:]),
        copies.start(wo.at[pl.ds(pl.multiple_of(c * half, half), half), :], out_w.at[:half, :]),
        copies.start(wo.at[pl.ds(pl.multiple_of((1 - c) * half, half), half), :], out_w.at[half:, :]),
        copies.start(ha, tokens.at[:rows, :]),
        copies.start(hb, tokens.at[rows:, :]),
    ]

    def ask(here):
        return (copies.start(wu.at[:, here], up_w.at[:, here]), copies.start(wd.at[here, :], down_w.at[here, :]))

    steps = [slice(low * chunk, high * chunk) for low, high in stretches(parts)]
    for copy in first:
        copy.wait()
    weights = [ask(steps[0])]
    turn = [copies.start(ga, grads.at[:rows, :]), copies.start(gb, grads.at[rows:, :])]
    mid[...] = tokens[...].astype(F32) + vectors[0:1, :] + mm(mixed[...], out_w[...])
    unit, _ = normalize(mid[...])
    norm[...] = (unit * vectors[2:3, :]).astype(BF16)
    copies.out(mid, middle)
    copies.out(norm, normed)
    for copy in turn:
        copy.wait()
    grads_t[...] = grads[...].T
    for i, here in enumerate(steps):
        if i + 1 < len(steps):
            weights.append(ask(steps[i + 1]))
        for copy in weights[i]:
            copy.wait()
        active, slopes[:, here] = gelu_both(mm(norm[...], up_w[:, here]))
        term = mm(active, down_w[here, :])
        out[...] = (mid if i == 0 else out)[...] + term
        value = mm(grads_t[...], active).astype(BF16)
        low, high = stretches(parts)[i]
        for part in range(low, high):
            for side in range(2):
                at = (part - low) * chunk + side * half
                shares[side, part] = value[:, at : at + half]
        copies.out(slopes.at[:, here], slope.at[:, here])
        copies.out(shares.at[1 - c, low:high], far.at[low:high])
        copies.out(shares.at[c, low:high], near.at[low:high])
    tokens[...] = out[...].astype(BF16)
    copies.out(tokens.at[:rows, :], oa)
    copies.out(tokens.at[rows:, :], ob)
    copies.finish()


def forward_pass(scalars, ha, hb, vectors, mine, other, w_out, w_up, w_down, ga, gb, parts, order=None):
    rows, width = ha.shape
    count, half = mine.shape
    ff = w_up.shape[1]
    outs = [
        jax.ShapeDtypeStruct((rows, width), BF16),
        jax.ShapeDtypeStruct((rows, width), BF16),
        pltpu.HBM((count, width), F32),
        pltpu.HBM((count, width), BF16),
        pltpu.HBM((count, ff), BF16),
        pltpu.HBM((parts, width, half), BF16),
        pltpu.HBM((parts, width, half), BF16),
    ]
    scratch = [
        pltpu.VMEM((count, width), BF16),
        pltpu.VMEM((count, width), BF16),
        pltpu.VMEM((width, width), BF16),
        pltpu.VMEM((width, ff), BF16),
        pltpu.VMEM((ff, width), BF16),
        pltpu.VMEM((count, width), BF16),
        pltpu.VMEM((width, count), BF16),
        pltpu.VMEM((count, width), F32),
        pltpu.VMEM((count, width), BF16),
        pltpu.VMEM((count, width), F32),
        pltpu.VMEM((count, ff), BF16),
        pltpu.VMEM((2, parts, width, half), BF16),
        pltpu.SemaphoreType.DMA((12 + 5 * parts,)),
    ]
    return call(
        forward_pass_body,
        "forward_pass",
        scalars,
        (vectors, ha, hb, mine, other, in_hbm(w_out), in_hbm(w_up), in_hbm(w_down), ga, gb),
        [whole(vectors.shape)] + [ANY] * 9,
        outs,
        [ANY] * 7,
        scratch=scratch,
        vmem=35,
        order=order,
        us=14,
    )


def feed_back_body(
    s_ref, vectors, ga, gb, normed, slope, wu, wd, middle, m0, m1, wo,
    grad_middle, gm_near, gm_far, gain_grad, *rest, aligned
):
    shares = rest[:2]
    grads, norm, norm_t, slopes, up_w, down_w, sums, mid, mixed, out_w, heads, held, *natural, sems = rest[2:]
    rows = ga.shape[0]
    half = m0.shape[1]
    parts = held.shape[1]
    chunk = wu.shape[1] // parts
    c = s_ref[0]
    copies = Copies(sems)
    first = [copies.start(ga, grads.at[:rows, :]), copies.start(gb, grads.at[rows:, :]), copies.start(normed, norm)]

    def ask(here):
        return (
            copies.start(wd.at[here, :], down_w.at[here, :]),
            copies.start(slope.at[:, here], slopes.at[:, here]),
            copies.start(wu.at[:, here], up_w.at[:, here]),
        )

    steps = [slice(low * chunk, high * chunk) for low, high in stretches(parts)]
    weights = [ask(steps[0])]
    for copy in first:
        copy.wait()
    norm_t[...] = norm[...].T
    last = []
    for i, here in enumerate(steps):
        if i + 1 < len(steps):
            weights.append(ask(steps[i + 1]))
        else:
            last = [
                copies.start(middle, mid),
                copies.start(wo.at[pl.ds(pl.multiple_of(c * half, half), half), :], out_w.at[:half, :]),
                copies.start(wo.at[pl.ds(pl.multiple_of((1 - c) * half, half), half), :], out_w.at[half:, :]),
                copies.start(m0, mixed.at[c]),
                copies.start(m1, mixed.at[1 - c]),
            ]
        for copy in weights[i]:
            copy.wait()
        grad_upper = (mm(grads[...], down_w[here, :], NT) * slopes[:, here].astype(F32)).astype(BF16)
        term = mm(grad_upper, up_w[:, here], NT)
        sums[...] = term if i == 0 else sums[...] + term
        value = mm(norm_t[...], grad_upper).astype(BF16)
        low, high = stretches(parts)[i]
        for part in range(low, high):
            mine = value[:, (part - low) * chunk : (part - low + 1) * chunk]
            if aligned:
                mine = mine.reshape(held.shape[2], 2, held.shape[3], chunk)
                held[0, part, :, :, :chunk] = mine[:, 0]
                held[1, part, :, :, :chunk] = mine[:, 1]
            else:
                held[0, part] = mine
        if not aligned:
            copies.out(held.at[0, low:high], shares[0].at[low:high])
    for copy in last:
        copy.wait()
    unit, root = normalize(mid[...])
    back, gain_sum = norm_back(sums[...], unit, root, vectors[2:3, :])
    gain_grad[...] = gain_sum
    mid[...] = grads[...].astype(F32) + back
    copies.out(mid, grad_middle)
    low_grad = mid[...].astype(BF16)
    heads[...] = mm(low_grad, out_w[...], NT).astype(BF16)
    copies.out(heads.at[:, :half], gm_near)
    copies.out(heads.at[:, half:], gm_far)
    turned = jnp.concatenate([mixed[0], mixed[1]], axis=1).T
    value = mm(turned, low_grad).astype(BF16)
    if aligned:
        blocks, own = held.shape[2:4]
        value = value.reshape(blocks, 2, own, 2 * half)
        cols = 2 * half // parts
        lanes = held.shape[4] - chunk
        for part in range(parts):
            mine = value[..., part * cols : (part + 1) * cols]
            pad = jnp.zeros(mine.shape[:-1] + (lanes - cols,), BF16)
            mine = jnp.concatenate([mine, pad], axis=-1)
            held[0, part, :, :, chunk:] = mine[:, 0]
            held[1, part, :, :, chunk:] = mine[:, 1]
        copies.out(held.at[1 - c], shares[0])
        copies.out(held.at[c], shares[1])
    else:
        natural[0][...] = value
        copies.out(natural[0], shares[1])
    copies.finish()


def feed_back(
    scalars, vectors, ga, gb, normed, slope, w_up, w_down, middle, mine, other, w_out, parts, blocks, lanes, aligned,
    order=None,
):
    rows, width = ga.shape
    count, half = 2 * rows, width // 2
    ff = w_up.shape[1]
    chunk = ff // parts
    if aligned:
        shares = [pltpu.HBM((parts, blocks, width // blocks // 2, lanes), BF16)] * 2
        held = [pltpu.VMEM((2,) + shares[0].shape, BF16)]
    else:
        shares = [jax.ShapeDtypeStruct((parts, width, chunk), BF16), jax.ShapeDtypeStruct((width, width), BF16)]
        held = [pltpu.VMEM((1,) + shares[0].shape, BF16), pltpu.VMEM((width, width), BF16)]
    scratch = [
        pltpu.VMEM((count, width), BF16),
        pltpu.VMEM((count, width), BF16),
        pltpu.VMEM((width, count), BF16),
        pltpu.VMEM((count, ff), BF16),
        pltpu.VMEM((width, ff), BF16),
        pltpu.VMEM((ff, width), BF16),
        pltpu.VMEM((count, width), F32),
        pltpu.VMEM((count, width), F32),
        pltpu.VMEM((2, count, half), BF16),
        pltpu.VMEM((width, width), BF16),
        pltpu.VMEM((count, width), BF16),
    ]
    scratch += held + [pltpu.SemaphoreType.DMA((13 + 5 * parts,))]
    outs = [
        pltpu.HBM((count, width), F32),
        pltpu.HBM((count, half), BF16),
        pltpu.HBM((count, half), BF16),
        jax.ShapeDtypeStruct((1, width), F32),
    ]
    return call(
        functools.partial(feed_back_body, aligned=aligned),
        "feed_back",
        scalars,
        (vectors, ga, gb, in_hbm(normed), in_hbm(slope), in_hbm(w_up), in_hbm(w_down), in_hbm(middle), mine, other, in_hbm(w_out)),
        [whole(vectors.shape)] + [ANY] * 10,
        outs + shares,
        [ANY] * 3 + [whole((1, width))] + [ANY] * 2,
        scratch=scratch,
        vmem=48,
        order=order,
        us=18,
    )


def attend_back_body(s_ref, *refs, pair):
    qs, dos, outs, lses = refs[0:2], refs[2:4], refs[4:6], refs[6:8]
    k0, k1, v0, v1, dq0, dq1, dk, dv, keys, vals = refs[8:]
    count = qs[0].shape[0]
    keys[:count, :], keys[count:, :] = k0[...], k1[...]
    vals[:count, :], vals[count:, :] = v0[...], v1[...]
    lanes = lax.broadcasted_iota(jnp.int32, (1, 128), 1)
    picks = lax.broadcasted_iota(jnp.int32, (8, 128), 1) // HEAD_DIM == lax.broadcasted_iota(jnp.int32, (8, 128), 0)
    picks = picks.astype(BF16)
    keys_t = keys[...].T
    turned = {}
    inners = []
    for b in range(2):
        product = dos[b][...].astype(F32) * outs[b][...].astype(F32)
        high = product.astype(BF16)
        low = (product - high.astype(F32)).astype(BF16)
        inners.append(mm(picks, high, NT) + mm(picks, low, NT))
        turned[b] = (qs[b][...].T, dos[b][...].T)
    grads_q = [[], []]
    grads_k, grads_v = [], []
    for h in range(2):
        head = slice(64 * h, 64 * h + 64)
        mask = (lanes >= 64) == (h == 1)
        grad_k = grad_v = None
        for b in range(2):
            q_head = jnp.where(mask, qs[b][...], jnp.zeros_like(qs[b][...]))
            do_head = jnp.where(mask, dos[b][...], jnp.zeros_like(dos[b][...]))
            weights = jnp.exp(mm(keys[...], q_head, NT) - lses[b][2 * pair + h : 2 * pair + h + 1, :])
            grad_weights = mm(vals[...], do_head, NT)
            grad_scores = (weights * (grad_weights - inners[b][h : h + 1, :])).astype(BF16)
            term = mm(turned[b][1][head], weights.astype(BF16), NT)
            grad_v = term if b == 0 else grad_v + term
            term = mm(turned[b][0][head], grad_scores, NT)
            grad_k = term if b == 0 else grad_k + term
            grads_q[b].append(mm(keys_t[head], grad_scores))
        grads_k.append(grad_k)
        grads_v.append(grad_v)
    for b, out in enumerate((dq0, dq1)):
        out[...] = (jnp.concatenate(grads_q[b], axis=0).T * SCALE).astype(BF16)
    dk[...] = jnp.concatenate(grads_k, axis=0).T.astype(BF16)
    dv[...] = jnp.concatenate(grads_v, axis=0).T.astype(BF16)


def attend_back(scalars, near, far, pair, order=None):
    count, half = near[1].shape
    ins = [a for both in zip(near, far) for a in both] + [near[0], far[0]] * 2
    pairs = half // 128
    lane = lambda t: pl.BlockSpec((count, 128), lambda g, s: (0, t * pairs + pair))
    one = jax.ShapeDtypeStruct((count, 128), BF16)
    two = jax.ShapeDtypeStruct((2 * count, 128), BF16)
    outs = [one, one, two, two]
    return call(
        functools.partial(attend_back_body, pair=pair),
        "attend_back",
        scalars,
        ins,
        [lane(0)] * 6 + [whole(near[3].shape)] * 2 + [lane(1), lane(1), lane(2), lane(2)],
        outs,
        [whole(o.shape) for o in outs],
        scratch=[pltpu.VMEM((2 * count, 128), BF16), pltpu.VMEM((2 * count, 128), BF16)],
        order=order,
        us=1.5,
        vmem=28,
    )


def side_by_side(refs):
    return jnp.concatenate([refs[3 * pair + t][...] for t in range(3) for pair in range(len(refs) // 3)], axis=1)


def pair_specs(grads, part, count):
    arrays, specs = [], []
    for near, far, dk, dv in grads:
        arrays += [(near, far)[part], dk, dv]
        specs += [whole((count, 128))] + [pl.BlockSpec((count, 128), lambda g, s: (part, 0))] * 2
    return arrays, specs


def project_back_body(s_ref, weight, *refs):
    refs[-1][...] = mm(side_by_side(refs[:-1]), weight[...], NT).astype(BF16)


def project_back(scalars, grads, weight, part, order=None):
    count = grads[0][0].shape[0]
    arrays, specs = pair_specs(grads, part, count)
    out = jax.ShapeDtypeStruct((count, weight.shape[0]), BF16)
    return call(
        project_back_body,
        "project_back",
        scalars,
        [weight] + arrays,
        [whole(weight.shape)] + specs,
        [out],
        [whole(out.shape)],
        order=order,
        us=1.0,
        vmem=16,
    )[0]


def turn_body(s_ref, ha, hb, xa, xb, vectors, *refs, count):
    out = refs[count]
    rows = ha.shape[0]
    for at, block in enumerate((ha, hb, xa, xb)):
        unit, _ = normalize(block[...].astype(F32) + vectors[0:1, :])
        out[:, at * rows : (at + 1) * rows] = (unit * vectors[1:2, :]).astype(BF16).T


def turned_tokens(scalars, ha, hb, xa, xb, vectors, awaited, carry, order=None):
    ins = (ha, hb, xa, xb, vectors)
    out = jax.ShapeDtypeStruct((ha.shape[1], 4 * ha.shape[0]), BF16)
    return call(
        functools.partial(turn_body, count=len(awaited) + len(carry)),
        "turned",
        scalars,
        ins + tuple(awaited) + tuple(in_hbm(value) for value in carry),
        [whole(a.shape) for a in ins] + [ANY] * (len(awaited) + len(carry)),
        [out] + [pltpu.HBM(value.shape, value.dtype) for value in carry],
        [whole(out.shape)] + [ANY] * len(carry),
        order=order,
        us=1,
        vmem=16,
        aliases={len(ins) + len(awaited) + at: 1 + at for at in range(len(carry))},
    )


def qkv_weight_body(s_ref, turned, *refs, pairs, aligned):
    out = refs[4 * pairs]
    grads = refs[-2] if aligned else refs[-1]
    count = refs[0].shape[0]
    lanes = grads.shape[1] // 3
    for pair in range(pairs):
        near, far, dk, dv = refs[4 * pair : 4 * pair + 4]
        here = slice(128 * pair, 128 * pair + 128)
        grads[:count, here] = near[...]
        grads[count:, here] = far[...]
        grads[:, lanes + 128 * pair : lanes + 128 * pair + 128] = dk[...]
        grads[:, 2 * lanes + 128 * pair : 2 * lanes + 128 * pair + 128] = dv[...]
    value = mm(turned[...], grads[...]).astype(BF16)
    if not aligned:
        out[...] = value
        return
    out[...] = value.reshape(out.shape)
    copies = Copies(refs[-1])
    bits = out.shape[0].bit_length() - 1
    for half, order in enumerate(orders(bits)):
        send = refs[4 * pairs + 1 + half]
        for g in range(send.shape[0]):
            copies.out(out.at[step_index(order, 0, s_ref[1], g), half], send.at[g])
    copies.finish()


def qkv_weight(scalars, turned, grads, blocks, aligned, order=None):
    width, count = turned.shape
    pairs = len(grads)
    lanes = 3 * 128 * pairs
    own = width // blocks // 2
    ins = [turned] + [a for four in grads for a in four]
    outs = [pltpu.HBM((blocks, 2, own, lanes) if aligned else (width, lanes), BF16)]
    specs = [whole(outs[0].shape)]
    scratch = [pltpu.VMEM((count, lanes), BF16)]
    if aligned:
        outs += [jax.ShapeDtypeStruct((blocks // 2, own, lanes), BF16)] * 2
        specs += [ANY] * 2
        scratch += [pltpu.SemaphoreType.DMA((blocks,))]
    return call(
        functools.partial(qkv_weight_body, pairs=pairs, aligned=aligned),
        "qkv_weight",
        scalars,
        ins,
        [whole(a.shape) for a in ins],
        outs,
        specs,
        scratch=scratch,
        order=order,
        us=2.5,
        vmem=24,
    )


def base_body(s_ref, ha, hb, vectors, grad_middle, weight, part_in, gain_two, *refs):
    ia, ib, sums = refs[-3:]
    rows = ha.shape[0]
    gain = vectors[1:2, :]
    grad_normed = mm(side_by_side(refs[:-3]), weight[...], NT) + part_in[...].astype(F32)
    gain_sum, base_sum = None, None
    for at, (block, out) in enumerate(((ha, ia), (hb, ib))):
        here = slice(at * rows, (at + 1) * rows)
        unit, root = normalize(block[...].astype(F32) + vectors[0:1, :])
        back, part = norm_back(grad_normed[here], unit, root, gain)
        grad = grad_middle[here, :] + back
        out[...] = grad.astype(BF16)
        gain_sum = part if gain_sum is None else gain_sum + part
        tokens = jnp.sum(grad, axis=0, keepdims=True)
        base_sum = tokens if base_sum is None else base_sum + tokens
    sums[0:1, :] = gain_sum
    sums[1:2, :] = gain_two[...]
    sums[2:3, :] = base_sum


def base_back(scalars, ha, hb, vectors, grad_middle, grads, weight, part_in, gain_two, order=None):
    rows, width = ha.shape
    arrays, specs = pair_specs(grads, 0, 2 * rows)
    grad_middle = in_hbm(grad_middle)
    ins = (ha, hb, vectors, grad_middle, weight, part_in, gain_two)
    outs = [
        jax.ShapeDtypeStruct((rows, width), BF16),
        jax.ShapeDtypeStruct((rows, width), BF16),
        jax.ShapeDtypeStruct((3, width), F32),
    ]
    return call(
        base_body,
        "base_back",
        scalars,
        list(ins) + arrays,
        [Staged(a) if a is grad_middle else whole(a.shape) for a in ins] + specs,
        outs,
        [whole(o.shape) for o in outs],
        order=order,
        us=1.75,
        vmem=24,
    )


def meet_body(s_ref, held, got, out, *, which, at):
    rows = held.shape[0] - 2
    out[0:2, :] = held[0:2, :] + got[0:2, :]
    if which is None:
        out[2:, :] = held[2:, :] + got[2:, :]
        return
    first = bit(s_ref[which], at) == 0
    mine, other = held[2:, :], got[2:, :]
    out[2 : 2 + rows, :] = jnp.where(first, mine, other)
    out[2 + rows :, :] = jnp.where(first, other, mine)


def meet(scalars, held, got, which, at, order=None):
    rows, lanes = held.shape
    out = jax.ShapeDtypeStruct((rows if which is None else 2 * rows - 2, lanes), F32)
    return call(
        functools.partial(meet_body, which=which, at=at),
        "meet",
        scalars,
        (held, got),
        [whole(held.shape)] * 2,
        [out],
        [whole(out.shape)],
        order=order,
        us=1.5,
        vmem=4,
    )[0]


def table_body(s_ref, sums, out):
    out[...] = jnp.zeros_like(out)
    for at in range(sums.shape[0] - 2):
        here = pl.ds(s_ref[at], 1)
        out[here, :] = out[here, :] + sums[at + 2 : at + 3, :]


def table_of(steps, sums, count, order=None):
    out = pltpu.HBM((count, sums.shape[1]), F32)
    return call(
        table_body,
        "table",
        steps,
        (sums,),
        [whole(sums.shape)],
        [out],
        [whole(out.shape)],
        order=order,
        us=1.25,
        vmem=12,
    )[0]


def fold(name, scalars, outs, order=None, split=False):
    ins, specs, known = [], [], {}
    for _, _, entries in outs:
        for _, _, terms in entries:
            for array, _, far in terms:
                if id(array) not in known:
                    known[id(array)] = len(ins)
                    ins.append(in_hbm(array) if far else array)
                    specs.append(ANY)
    scratch = [pltpu.VMEM(block, t[0].dtype) for _, _, entries in outs for _, block, terms in entries for t in terms]
    given = len(ins)

    def body(s_ref, *refs):
        arrays, targets = refs[:given], refs[given : given + len(shapes)]
        held = list(refs[given + len(shapes) : -1])
        copies = Copies(refs[-1])
        if split:
            sides, targets = targets, [held.pop()]
        waiting = []
        for (_, _, entries), target in zip(outs, targets):
            for to, _, terms in entries:
                mine = []
                for array, where, _ in terms:
                    slot = held.pop(0)
                    mine.append((copies.start(arrays[known[id(array)]].at[where(s_ref)], slot), slot))
                waiting.append((target, to, mine))
        for target, to, mine in waiting:
            total = None
            for copy, slot in mine:
                copy.wait()
                total = slot[...].astype(F32) if total is None else total + slot[...].astype(F32)
            target[to] = total.astype(target.dtype)
        if split:
            copies.out(targets[0].at[1 - s_ref[0]], sides[0])
            copies.out(targets[0].at[s_ref[0]], sides[1])
            copies.finish()

    shapes = [jax.ShapeDtypeStruct(o[0], o[1]) for o in outs]
    if split:
        shapes = [jax.ShapeDtypeStruct(outs[0][0][1:], outs[0][1])] * 2
        scratch.append(pltpu.VMEM(outs[0][0], outs[0][1]))
    return call(
        body,
        name,
        scalars,
        ins,
        specs,
        shapes,
        [ANY if split else whole(o.shape) for o in shapes],
        scratch=scratch + [pltpu.SemaphoreType.DMA((len(scratch) + 2,))],
        order=order,
        us=2.5,
        vmem=16,
    )


def bit(value, at):
    return (value >> at) & 1


def orders(bits):
    return (list(range(bits)), list(range(bits))[::-1])


def step_index(order, step, own, g):
    value = (1 - bit(own, order[step])) << order[step]
    for at in order[:step]:
        value = value + (bit(own, at) << at)
    for i, at in enumerate(order[step + 1 :]):
        value = value + (bit(g, i) << at)
    return value


def held_index(order, step, block):
    value = block * 0
    for i, at in enumerate(order[step + 1 :]):
        value = value + (bit(block, at) << i)
    return value


class Segment:
    def __init__(self, low, high, terms):
        self.low, self.high, self.terms = low, high, list(terms)


class Reduction:
    def __init__(self, swap, pieces, seq_bits, has_seq=True):
        self.swap, self.pieces, self.seq_bits = swap, pieces, seq_bits
        self.seq_orders = [orders(seq_bits)[at % 2] for at in range(len(pieces))]
        self.steps = len(pieces[0][0])
        self.rows = sum(p[2] for p in pieces)
        self.lanes = pieces[0][3][-1].high
        self.lead = (1 << seq_bits,) if has_seq else ()
        self.got = [[] for _ in pieces]
        self.got_seq = [[] for _ in pieces]

    def entries(self, at, to, block_of, seq_of=None):
        order, first, rows, segments = self.pieces[at]
        every = slice(None)
        out = []
        for segment in segments:
            width = segment.high - segment.low
            terms = []
            for array, where, far in segment.terms:
                place = lambda s, where=where: where(block_of(s), None if seq_of is None else seq_of(s))
                terms.append((array, place, far))
            for step, array in self.got[at]:

                def place(s, step=step, lanes=pl.ds(segment.low, width)):
                    block = held_index(order, step, block_of(s))
                    if not self.lead:
                        return (block, every, lanes)
                    return (block, every if seq_of is None else seq_of(s), every, lanes)

                terms.append((array, place, False))
            if seq_of is not None:
                for step, array in self.got_seq[at]:
                    place = lambda s, step=step, lanes=pl.ds(segment.low, width): (
                        held_index(self.seq_orders[at], step, seq_of(s)),
                        every,
                        lanes,
                    )
                    terms.append((array, place, False))
            block = (self.lead if seq_of is None else ()) + (rows, width)
            out.append((to + (Ellipsis, slice(segment.low, segment.high)), block, terms))
        return out

    def leaving(self, step):
        count = 1 << (self.steps - 1 - step)
        outs = []
        for at, (order, _, rows, _) in enumerate(self.pieces):
            entries = []
            for g in range(count):
                entries += self.entries(at, (g,), lambda s, g=g, order=order: step_index(order, step, s[1], g))
            outs.append(((count,) + self.lead + (rows, self.lanes), BF16, entries))
        if step == self.steps - 1 and self.lead:
            for at, (_, _, rows, _) in enumerate(self.pieces):
                outs.append((self.lead + (rows, self.lanes), F32, self.entries(at, (), lambda s: s[1])))
        return outs

    def send(self, step, sent):
        count = len(self.pieces)
        every = slice(None)
        for at, (order, _, _, segments) in enumerate(self.pieces):
            if len(sent) > count:
                self.got[at] = []
                for segment in segments:
                    lanes = pl.ds(segment.low, segment.high - segment.low)
                    where = lambda block, seq, lanes=lanes: (every if seq is None else seq, every, lanes)
                    segment.terms = [(sent[count + at], where, False)]
            self.got[at].append((step, self.swap(sent[at], 2 << order[step], 0)))

    def leaving_seq(self, step):
        count = 1 << (self.seq_bits - 1 - step)
        outs = []
        for at, (_, _, rows, _) in enumerate(self.pieces):
            entries = []
            for g in range(count):
                seq_of = lambda s, g=g, order=self.seq_orders[at]: step_index(order, step, s[2], g)
                entries += self.entries(at, (g,), lambda s: s[1], seq_of)
            outs.append(((count, rows, self.lanes), BF16, entries))
        return outs

    def send_seq(self, step, sent):
        for at, value in enumerate(sent):
            self.got_seq[at].append((step, self.swap(value, 0, 1 << self.seq_orders[at][step])))

    def last(self):
        out = []
        for at, segment in enumerate(self.pieces[0][3]):
            entries = []
            for piece, (_, first, rows, _) in enumerate(self.pieces):
                _, block, terms = self.entries(piece, (), lambda s: s[1], lambda s: s[2])[at]
                entries.append(((slice(first, first + rows),), block, terms))
            out.append(((self.rows, segment.high - segment.low), F32, entries))
        return out


def columns_body(s_ref, mine, other, keep, *sends):
    even = s_ref[0] == 0
    here, there = mine[...].astype(F32), other[...].astype(F32)
    half = here.shape[1] // 3
    first, second = jnp.where(even, here, there), jnp.where(even, there, here)
    columns = []
    for t in range(3):
        columns += [first[:, t * half : t * half + half], second[:, t * half : t * half + half]]
    columns = jnp.concatenate(columns, axis=1)
    lanes = keep.shape[1]
    for at, target in enumerate((keep, *sends)):
        for part in range(len(sends) + 1):

            @pl.when((s_ref[2] ^ at) == part)
            def _(target=target, part=part):
                target[...] = columns[:, part * lanes : part * lanes + lanes].astype(target.dtype)


def on_device(
    row_count, seq_count, hidden_in, timesteps, step_table, gain_one, w_qkv, w_out, gain_two, w_up, w_down, out_grad
):
    seqs_here, tokens_here, width = hidden_in.shape
    ff = w_up.shape[1]
    half = width // 2
    blocks = row_count // 2
    block_bits = blocks.bit_length() - 1
    seq_bits = seq_count.bit_length() - 1
    r = lax.axis_index("rows")
    z = lax.axis_index("seq")
    c = lax.rem(r, 2)
    b = lax.div(r, 2)
    odd = lax.rem(z, 2)
    axes = ("rows", "seq")

    def flat(row, seq):
        return row * seq_count + seq

    def swap(value, row_bit, seq_bit=0):
        pairs = [
            (flat(i, j), flat(i ^ row_bit, j ^ seq_bit)) for i in range(row_count) for j in range(seq_count)
        ]
        return lax.ppermute(value, axes, pairs)

    def core_swap(value):
        return swap(value, 1)

    moves = []
    for turn in range(2):
        moves.append(
            [
                (flat(2 * p + e, j), flat(2 * p + j // 2, 2 * e + (j + turn) % 2))
                for p in range(blocks)
                for e in range(2)
                for j in range(seq_count)
            ]
        )

    def gather_tokens(leaving):
        return tuple(lax.ppermute(value, axes, move) for value, move in zip(leaving, moves))

    def share(value, at, axis):
        return lax.dynamic_index_in_dim(value, at, axis, keepdims=False)

    def send_back(*values):
        return [lax.ppermute(value, axes, [(t, s) for s, t in move]) for value, move in zip(values, moves)]

    scalars = jnp.stack([c, b, z]).astype(jnp.int32)

    steps_all = lax.all_gather(timesteps, "rows", axis=0, tiled=True)
    steps_held = steps_all.reshape(blocks, seq_count).T.reshape(-1)
    step_now = lax.dynamic_index_in_dim(steps_all, seq_count * b + z, 0, keepdims=False)
    row = lax.dynamic_slice_in_dim(step_table, step_now, 1, 0).astype(F32)

    order = Order()
    weight, vectors = prepare(scalars, row, gain_one[None, :], gain_two[None, :], w_qkv)
    ha, hb = gather_tokens([share(hidden_in, at, 0) for at in (odd, 1 - odd)])
    xa, xb = core_swap(ha), core_swap(hb)
    near = qkv(scalars, ha, hb, vectors, weight, order=order, us=8)
    late_grad, _, _ = lax.optimization_barrier((out_grad, ha, hb))
    ga, gb = gather_tokens([share(late_grad, at, 0) for at in (odd, 1 - odd)])
    far = qkv(scalars, xa, xb, vectors, weight, order=order)
    mixed_far, lse_far = attend(scalars, far, near, far, order=order)
    mixed_in = core_swap(mixed_far)
    mixed_near, lse_near = attend(scalars, near, near, far, order=order)

    parts = seq_count
    unit = ff // row_count
    own_rows, seq_cols, up_cols = width // row_count, width // seq_count, ff // seq_count
    whole_units = blocks == parts and unit % 128 == 0
    whole_rows = own_rows % 32 == 0

    oa, ob, middle, normed_two, slope, down_far, down_near = forward_pass(
        scalars, ha, hb, vectors, mixed_near, mixed_in, w_out, w_up, w_down, ga, gb, parts, order=order
    )
    if not whole_units:
        sides = [jnp.where(c == side, down_near, down_far) for side in range(2)]
        natural = jnp.concatenate(sides, axis=2).transpose(1, 0, 2).reshape(parts, seq_cols, blocks, 2, unit)
        down_far, down_near = (share(natural, at, 3).transpose(2, 0, 1, 3) for at in (1 - c, c))
    down_shape = (blocks, parts, seq_cols, unit)
    down_far, down_near = down_far.reshape(down_shape), down_near.reshape(down_shape)
    down_in = core_swap(down_far)

    lanes = -(-(up_cols + seq_cols) // 256) * 256
    grad_middle, gm_near, gm_far, gain_two_part, up_far, up_near = feed_back(
        scalars, vectors, ga, gb, normed_two, slope, w_up, w_down, middle, mixed_near, mixed_in, w_out,
        parts, blocks, lanes, whole_rows, order=order,
    )
    if not whole_rows:
        up_all = up_far.reshape(parts, blocks, 2, own_rows, up_cols)
        out_all = up_near.reshape(blocks, 2, own_rows, parts, seq_cols).transpose(3, 0, 1, 2, 4)
        blank = jnp.zeros(up_all.shape[:-1] + (lanes - up_cols - seq_cols,), BF16)
        natural = jnp.concatenate([up_all, out_all, blank], axis=-1)
        up_far, up_near = (share(natural, at, 2) for at in (1 - c, c))

    fold_over = functools.partial(fold, "reduce", scalars, order=order)
    both = orders(block_bits)
    every = slice(None)

    def taken(array, by_seq, first, rows):
        def where(block, seq):
            seq = every if seq is None else seq
            return (seq, block, pl.ds(first, rows)) if by_seq else (block, seq, pl.ds(first, rows))

        return (array, where, array is down_near or array is up_near)

    def segment(low, high, arrays, by_seq, first, rows):
        return Segment(low, high, [taken(array, by_seq, first, rows) for array in arrays])

    def step_over(reductions, leaving, send, step):
        outs = [leaving(r, step) for r in reductions]
        sent = list(fold_over([o for out in outs for o in out]))
        for reduction, out in zip(reductions, outs):
            send(reduction, step, sent[: len(out)])
            del sent[: len(out)]

    step_blocks = functools.partial(step_over, leaving=Reduction.leaving, send=Reduction.send)
    step_seq = functools.partial(step_over, leaving=Reduction.leaving_seq, send=Reduction.send_seq)

    turned, gm_far, up_far, oa, ob = turned_tokens(
        scalars, ha, hb, xa, xb, vectors, (down_in,), (gm_far, up_far, oa, ob), order=order
    )
    up_in = core_swap(up_far)
    gm_in = core_swap(gm_far)
    out_back = send_back(oa, ob)
    downs, ups = (down_near, down_in), (up_near, up_in)
    joined = whole_units and whole_rows and 2 * unit == up_cols and seq_cols == 2 * own_rows
    if joined:
        rows = own_rows // 2
        pieces = []
        for at in range(2):
            segments = [segment(t * unit, (t + 1) * unit, downs, False, (2 * at + t) * rows, rows) for t in range(2)]
            segments.append(segment(2 * unit, 2 * unit + lanes, ups, True, at * rows, rows))
            pieces.append((both[at], at * rows, rows, segments))
        everything = [Reduction(swap, pieces, seq_bits)]
    else:
        down = Reduction(swap, [(both[0], 0, seq_cols, [segment(0, unit, downs, False, 0, seq_cols)])], seq_bits)
        up = Reduction(swap, [(both[1], 0, own_rows, [segment(0, lanes, ups, True, 0, own_rows)])], seq_bits)
        everything = [down, up]
    step_blocks(everything, step=0)
    sides = ((near, gm_near, mixed_near, lse_near), (far, gm_in, mixed_far, lse_far))
    grads = []
    for pair in range(half // 128):
        grads.append(attend_back(scalars, *sides, pair, order=order))
        if pair == 1:
            out_hidden = returned_blocks(scalars, *out_back, order=order)
    part_far = project_back(scalars, grads, weight, 1, order=order)
    part_in = core_swap(part_far)
    qkv_w = qkv_weight(scalars, turned, grads, blocks, whole_rows, order=order)
    for step in range(1, block_bits):
        step_blocks(everything, step=step)
    if whole_rows:
        qkv_blocks = qkv_w[0].reshape(blocks, 2 * own_rows, 3 * half)
        rows_of = lambda h: (lambda block, seq: (block, pl.ds(h * own_rows, own_rows)))
    else:
        qkv_blocks = qkv_w[0].reshape(blocks, 2, own_rows, 3 * half)
        rows_of = lambda h: (lambda block, seq: (block, h))
    project = Reduction(
        swap,
        [
            (both[h], h * own_rows, own_rows, [Segment(0, 3 * half, [(qkv_blocks, rows_of(h), True)])])
            for h in range(2)
        ],
        seq_bits,
        False,
    )
    if whole_rows:
        project.send(0, qkv_w[1:])
    else:
        step_blocks([project], step=0)
    ia, ib, held = base_back(
        scalars, ha, hb, vectors, grad_middle, grads, weight, part_in, gain_two_part, order=order
    )
    in_back = send_back(ia, ib)

    meetings = [(None, 0, 1, 0)]
    meetings += [(1, at, 2 << at, 0) for at in range(block_bits)]
    meetings += [(2, at, 0, 1 << at) for at in range(seq_bits)]

    def next_meeting(held):
        which, at, row_bit, seq_bit = meetings.pop(0)
        return meet(scalars, held, swap(held, row_bit, seq_bit), which, at, order=order)

    held = next_meeting(held)
    step_seq(everything, step=0)
    held = next_meeting(held)
    for step in range(1, block_bits):
        step_blocks([project], step=step)
    held = next_meeting(held)
    in_grad = returned_blocks(scalars, *in_back, order=order)
    entries = []
    for h in range(2):
        for _, block, terms in project.entries(h, (), lambda s: s[1]):
            entries.append(((h,), block, terms))
    qkv_far, qkv_mine = fold_over([((2, own_rows, 3 * half), BF16, entries)], split=True)
    held = next_meeting(held)
    held = next_meeting(held)
    while meetings:
        held = next_meeting(held)
    table = table_of(steps_held, held, step_table.shape[0], order=order)
    for step in range(1, seq_bits):
        step_seq(everything, step=step)
    shape = (own_rows, 6 * half // parts)
    qkv_keep, *qkv_sends = call(
        columns_body,
        "qkv_columns",
        scalars,
        (qkv_mine, core_swap(qkv_far)),
        [whole(qkv_mine.shape)] * 2,
        [jax.ShapeDtypeStruct(shape, F32)] + [jax.ShapeDtypeStruct(shape, BF16)] * (parts - 1),
        [whole(shape)] * parts,
        vmem=12,
        order=order,
    )
    qkv_terms = [qkv_keep] + [swap(value, 0, at + 1) for at, value in enumerate(qkv_sends)]
    if joined:
        left, right, up_all = fold_over(everything[0].last())
        down_sum = jnp.stack([left.reshape(2, rows, unit), right.reshape(2, rows, unit)], axis=1).reshape(seq_cols, unit)
    else:
        down_sum, up_all = fold_over(down.last() + up.last())
    entry = ((Ellipsis,), shape, [(value, lambda s: (slice(None),), False) for value in qkv_terms])
    qkv_shard = fold_over([(shape, F32, [entry])])[0]

    return (
        out_hidden,
        in_grad,
        table,
        held[0],
        qkv_shard,
        up_all[:, up_cols : up_cols + seq_cols],
        held[1],
        up_all[:, :up_cols],
        down_sum.T,
    )


def solution(mesh):
    tokens = P("rows", "seq", None)
    split = P("rows", "seq")
    in_specs = (tokens, P("rows"), P(), P(), P(), P(), P(), P(), P(), tokens)
    out_specs = (tokens, tokens, P(), P(), split, split, P(), split, split)
    body = functools.partial(on_device, mesh.shape["rows"], mesh.shape["seq"])
    return jax.shard_map(body, mesh=mesh, in_specs=in_specs, out_specs=out_specs, check_vma=False)
```

```python
import functools

import jax
import jax.numpy as jnp
from jax import lax
from jax.experimental import pallas as pl
from jax.experimental.pallas import tpu as pltpu
from jax.sharding import PartitionSpec as P

HEAD_DIM = 64
SCALE = HEAD_DIM ** (-0.5)
EPS = 1e-05
F32 = jnp.float32
BF16 = jnp.bfloat16
MIB = 1 << 20
PER_US = 1_000_000_000

NN = (((1,), (0,)), ((), ()))
NT = (((1,), (1,)), ((), ()))


def mm(a, b, dims=NN):
    return lax.dot_general(a, b, dims, preferred_element_type=F32)


def normalize(values):
    average = jnp.mean(values, axis=-1, keepdims=True)
    centred = values - average
    inverse_root = lax.rsqrt(jnp.mean(centred * centred, axis=-1, keepdims=True) + EPS)
    return (centred * inverse_root, inverse_root)


def norm_back(grad_normed, unit_rows, inverse_root, scale_gain):
    gained = grad_normed * scale_gain
    centred_grad = (
        gained
        - jnp.mean(gained, axis=-1, keepdims=True)
        - unit_rows * jnp.mean(gained * unit_rows, axis=-1, keepdims=True)
    )
    return (inverse_root * centred_grad, jnp.sum(grad_normed * unit_rows, axis=0, keepdims=True))


def whole(shape):
    return pl.BlockSpec(shape, lambda *_: (0,) * len(shape))


class Staged:
    def __init__(self, array):
        self.memory = pltpu.VMEM(array.shape, array.dtype)


class Order:
    def __init__(self):
        self.token = None


def call(
    body, name, scalars, ins, in_specs, outs, out_specs, grid=(1,), scratch=(), vmem=32, order=None, us=1.0, carry=()
):
    ins, in_specs, outs, out_specs = list(ins), list(in_specs), list(outs), list(out_specs)
    count, given = len(ins), len(outs)
    staged = [at for at, spec in enumerate(in_specs) if isinstance(spec, Staged)]
    held = [in_specs[at].memory for at in staged]
    for at in staged:
        in_specs[at] = ANY
    waits = [] if order is None or order.token is None else [order.token]
    inner = body

    def body(scalars_ref, *refs):
        refs = list(refs)
        del refs[count : count + len(carry) + len(waits)]
        del refs[count + given : count + given + len(carry)]
        if order is not None:
            token = refs.pop(count + given)
            token[...] = jnp.zeros_like(token)
        if staged:
            sems, slots = refs.pop(), refs[len(refs) - len(held) :]
            del refs[len(refs) - len(held) :]
            copies = [pltpu.make_async_copy(refs[at], slot, sems.at[i]) for i, (at, slot) in enumerate(zip(staged, slots))]
            for copy in copies:
                copy.start()
            for at, slot in zip(staged, slots):
                refs[at] = slot
            for copy in copies:
                copy.wait()
        inner(scalars_ref, *refs)

    ins += [in_hbm(value) for value in carry] + waits
    in_specs += [ANY] * (len(carry) + len(waits))
    outs += [pltpu.HBM(value.shape, value.dtype) for value in carry]
    out_specs += [ANY] * len(carry)
    if order is not None:
        outs.append(jax.ShapeDtypeStruct((8, 128), F32))
        out_specs.append(whole((8, 128)))
    scratch = list(scratch) + held + ([pltpu.SemaphoreType.DMA((len(staged),))] if staged else [])
    result = pl.pallas_call(
        body,
        name=name,
        grid_spec=pltpu.PrefetchScalarGridSpec(
            num_scalar_prefetch=1,
            grid=grid,
            in_specs=in_specs,
            out_specs=out_specs,
            scratch_shapes=scratch,
        ),
        out_shape=outs,
        input_output_aliases={1 + count + at: given + at for at in range(len(carry))},
        cost_estimate=pl.CostEstimate(flops=int(us * PER_US), bytes_accessed=1 << 10, transcendentals=0),
        compiler_params=pltpu.CompilerParams(vmem_limit_bytes=vmem * MIB),
    )(scalars, *ins)
    result = list(result)
    if order is not None:
        order.token = result.pop()
    return result


def in_hbm(value):
    return pltpu.with_memory_space_constraint(value, pltpu.HBM)


ANY = pl.BlockSpec(memory_space=pl.ANY)


def gelu_both(upper):
    square = upper * upper
    turned = jnp.tanh(upper * (GELU_A + GELU_A * GELU_B * square))
    half_up = 0.5 + 0.5 * turned
    active = upper * half_up
    slope = half_up + active * (1.0 - turned) * (GELU_A + 3.0 * GELU_A * GELU_B * square)
    return active.astype(BF16), slope.astype(BF16)


class Copies:
    def __init__(self, sems):
        self.sems, self.count, self.outs = sems, 0, []

    def start(self, source, target):
        copy = pltpu.make_async_copy(source, target, self.sems.at[self.count])
        self.count += 1
        copy.start()
        return copy

    def out(self, source, target):
        self.outs.append(self.start(source, target))

    def finish(self):
        for copy in self.outs:
            copy.wait()


GELU_A, GELU_B = 0.7978845608028654, 0.044715


def stretches(parts):
    return [(at, min(at + 2, parts)) for at in range(0, parts, 2)]


def prepare_body(s_ref, row, first, second, wq, wk, wv, out, vectors):
    half = wq.shape[1]
    for t, w in enumerate((wq, wk, wv)):
        out[:, t * half : t * half + half] = w[...]
    for at, value in enumerate((row, first, second)):
        vectors[at : at + 1, :] = value[...]


def prepare(scalars, row, gain_one, gain_two, w_qkv, order=None):
    width = w_qkv.shape[0]
    half = width // 2
    specs = [whole((1, width))] * 3
    specs += [pl.BlockSpec((width, half), functools.partial(lambda t, g, s: (0, 2 * t + s[0]), t)) for t in range(3)]
    outs = [jax.ShapeDtypeStruct((width, 3 * half), BF16), jax.ShapeDtypeStruct((8, width), F32)]
    return call(
        prepare_body,
        "prepare",
        scalars,
        (row, gain_one, gain_two) + (in_hbm(w_qkv),) * 3,
        specs,
        outs,
        [whole(o.shape) for o in outs],
        order=order,
        us=2,
        vmem=12,
    )


def returned_body(s_ref, first, second, out, sems):
    at = bit(s_ref[2], 0)
    copies = Copies(sems)
    copies.out(first, out.at[at])
    copies.out(second, out.at[1 - at])
    copies.finish()


def returned_blocks(scalars, first, second, order=None):
    return call(
        returned_body,
        "returned",
        scalars,
        (first, second),
        [ANY] * 2,
        [pltpu.HBM((2,) + first.shape, first.dtype)],
        [ANY],
        scratch=[pltpu.SemaphoreType.DMA((2,))],
        order=order,
        us=3,
        vmem=4,
    )[0]


def qkv_body(s_ref, ha, hb, vectors, weight, out, normed):
    row, gain = vectors[0:1, :], vectors[1:2, :]
    rows = ha.shape[0]
    half = out.shape[1] // 3
    for at, block in enumerate((ha, hb)):
        unit, _ = normalize(block[...].astype(F32) + row)
        normed[pl.ds(at * rows, rows), :] = (unit * gain).astype(BF16)
    packed = mm(normed[...], weight[...]).astype(BF16)
    out[:, :half] = (packed[:, :half] * SCALE).astype(BF16)
    out[:, half:] = packed[:, half:]


def qkv(scalars, ha, hb, vectors, weight, order=None, us=2.3):
    rows, width = ha.shape
    ins = (ha, hb, vectors, weight)
    out = jax.ShapeDtypeStruct((2 * rows, weight.shape[1]), BF16)
    return call(
        qkv_body,
        "qkv",
        scalars,
        ins,
        [whole(a.shape) for a in ins],
        [out],
        [whole(out.shape)],
        scratch=[pltpu.VMEM((2 * rows, width), BF16)],
        order=order,
        us=us,
        vmem=16,
    )[0]


def attend_body(s_ref, q, k0, k1, v0, v1, mixed, lse):
    count, half = q.shape
    lanes = lax.broadcasted_iota(jnp.int32, (1, 128), 1)
    ones = jnp.ones((16, count), BF16)
    for pair in range(half // 128):
        cols = slice(128 * pair, 128 * pair + 128)
        q_pair = q[:, cols]
        vt = [v[:, cols].T for v in (v0, v1)]
        done = []
        for h in range(2):
            q_head = jnp.where((lanes >= 64) == (h == 1), q_pair, jnp.zeros_like(q_pair))
            scores = [mm(k[:, cols], q_head, NT) for k in (k0, k1)]
            highest = jnp.maximum(
                jnp.max(scores[0], axis=0, keepdims=True), jnp.max(scores[1], axis=0, keepdims=True)
            )
            total = None
            for part in range(2):
                weights = jnp.exp(scores[part] - highest).astype(BF16)
                left = jnp.concatenate([vt[part][64 * h : 64 * h + 64], ones], axis=0)
                term = mm(left, weights)
                total = term if total is None else total + term
            summed = total[64:65]
            done.append(total[:64] / summed)
            lse[2 * pair + h : 2 * pair + h + 1, :] = highest + jnp.log(summed)
        mixed[:, cols] = jnp.concatenate(done, axis=0).T.astype(BF16)


def attend(scalars, asked, near, far, order=None):
    count, half = asked.shape[0], asked.shape[1] // 3
    ins = (asked, near, far, near, far)
    outs = [jax.ShapeDtypeStruct((count, half), BF16), jax.ShapeDtypeStruct((8, count), F32)]
    return call(
        attend_body,
        "attend",
        scalars,
        ins,
        [pl.BlockSpec((count, half), functools.partial(lambda t, g, s: (0, t), t)) for t in (0, 1, 1, 2, 2)],
        outs,
        [whole(o.shape) for o in outs],
        order=order,
        us=6,
        vmem=24,
    )


def forward_pass_body(
    s_ref, vectors, ha, hb, m0, m1, wo, wu, wd, ga, gb,
    oa, ob, middle, normed, slope, far, near,
    tokens, mixed, out_w, up_w, down_w, grads, grads_t, mid, norm, out, slopes, shares, sems
):
    rows, half = ha.shape[0], m0.shape[1]
    parts = far.shape[0]
    chunk = 2 * half
    c = s_ref[0]
    copies = Copies(sems)
    first = [
        copies.start(m0, mixed.at[:, :half]),
        copies.start(m1, mixed.at[:, half:]),
        copies.start(wo.at[pl.ds(pl.multiple_of(c * half, half), half), :], out_w.at[:half, :]),
        copies.start(wo.at[pl.ds(pl.multiple_of((1 - c) * half, half), half), :], out_w.at[half:, :]),
        copies.start(ha, tokens.at[:rows, :]),
        copies.start(hb, tokens.at[rows:, :]),
    ]

    def ask(here):
        return (copies.start(wu.at[:, here], up_w.at[:, here]), copies.start(wd.at[here, :], down_w.at[here, :]))

    steps = [slice(low * chunk, high * chunk) for low, high in stretches(parts)]
    for copy in first:
        copy.wait()
    weights = [ask(steps[0])]
    turn = [copies.start(ga, grads.at[:rows, :]), copies.start(gb, grads.at[rows:, :])]
    mid[...] = tokens[...].astype(F32) + vectors[0:1, :] + mm(mixed[...], out_w[...])
    unit, _ = normalize(mid[...])
    norm[...] = (unit * vectors[2:3, :]).astype(BF16)
    copies.out(mid, middle)
    copies.out(norm, normed)
    for copy in turn:
        copy.wait()
    grads_t[...] = grads[...].T
    for i, here in enumerate(steps):
        if i + 1 < len(steps):
            weights.append(ask(steps[i + 1]))
        for copy in weights[i]:
            copy.wait()
        active, slopes[:, here] = gelu_both(mm(norm[...], up_w[:, here]))
        term = mm(active, down_w[here, :])
        out[...] = (mid if i == 0 else out)[...] + term
        value = mm(grads_t[...], active).astype(BF16)
        low, high = stretches(parts)[i]
        for part in range(low, high):
            for side in range(2):
                at = (part - low) * chunk + side * half
                shares[side, part] = value[:, at : at + half]
        copies.out(slopes.at[:, here], slope.at[:, here])
        copies.out(shares.at[1 - c, low:high], far.at[low:high])
        copies.out(shares.at[c, low:high], near.at[low:high])
    tokens[...] = out[...].astype(BF16)
    copies.out(tokens.at[:rows, :], oa)
    copies.out(tokens.at[rows:, :], ob)
    copies.finish()


def forward_pass(scalars, ha, hb, vectors, mine, other, w_out, w_up, w_down, ga, gb, parts, order=None):
    rows, width = ha.shape
    count, half = mine.shape
    ff = w_up.shape[1]
    outs = [
        pltpu.HBM((rows, width), BF16),
        pltpu.HBM((rows, width), BF16),
        pltpu.HBM((count, width), F32),
        pltpu.HBM((count, width), BF16),
        pltpu.HBM((count, ff), BF16),
        pltpu.HBM((parts, width, half), BF16),
        pltpu.HBM((parts, width, half), BF16),
    ]
    scratch = [
        pltpu.VMEM((count, width), BF16),
        pltpu.VMEM((count, width), BF16),
        pltpu.VMEM((width, width), BF16),
        pltpu.VMEM((width, ff), BF16),
        pltpu.VMEM((ff, width), BF16),
        pltpu.VMEM((count, width), BF16),
        pltpu.VMEM((width, count), BF16),
        pltpu.VMEM((count, width), F32),
        pltpu.VMEM((count, width), BF16),
        pltpu.VMEM((count, width), F32),
        pltpu.VMEM((count, ff), BF16),
        pltpu.VMEM((2, parts, width, half), BF16),
        pltpu.SemaphoreType.DMA((12 + 5 * parts,)),
    ]
    return call(
        forward_pass_body,
        "forward_pass",
        scalars,
        (vectors, ha, hb, mine, other, in_hbm(w_out), in_hbm(w_up), in_hbm(w_down), ga, gb),
        [whole(vectors.shape)] + [ANY] * 9,
        outs,
        [ANY] * 7,
        scratch=scratch,
        vmem=35,
        order=order,
        us=14,
    )


def feed_back_body(
    s_ref, vectors, ga, gb, normed, slope, wu, wd, middle, m0, m1, wo,
    grad_middle, gm_near, gm_far, gain_grad, *rest, aligned
):
    shares = rest[:2]
    grads, norm, norm_t, slopes, up_w, down_w, sums, mid, mixed, out_w, heads, held, *natural, sems = rest[2:]
    rows = ga.shape[0]
    half = m0.shape[1]
    parts = held.shape[1]
    chunk = wu.shape[1] // parts
    c = s_ref[0]
    copies = Copies(sems)
    first = [copies.start(ga, grads.at[:rows, :]), copies.start(gb, grads.at[rows:, :]), copies.start(normed, norm)]

    def ask(here):
        return (
            copies.start(wd.at[here, :], down_w.at[here, :]),
            copies.start(slope.at[:, here], slopes.at[:, here]),
            copies.start(wu.at[:, here], up_w.at[:, here]),
        )

    steps = [slice(low * chunk, high * chunk) for low, high in stretches(parts)]
    weights = [ask(steps[0])]
    for copy in first:
        copy.wait()
    norm_t[...] = norm[...].T
    last = []
    for i, here in enumerate(steps):
        if i + 1 < len(steps):
            weights.append(ask(steps[i + 1]))
        else:
            last = [
                copies.start(middle, mid),
                copies.start(wo.at[pl.ds(pl.multiple_of(c * half, half), half), :], out_w.at[:half, :]),
                copies.start(wo.at[pl.ds(pl.multiple_of((1 - c) * half, half), half), :], out_w.at[half:, :]),
                copies.start(m0, mixed.at[c]),
                copies.start(m1, mixed.at[1 - c]),
            ]
        for copy in weights[i]:
            copy.wait()
        grad_upper = (mm(grads[...], down_w[here, :], NT) * slopes[:, here].astype(F32)).astype(BF16)
        term = mm(grad_upper, up_w[:, here], NT)
        sums[...] = term if i == 0 else sums[...] + term
        value = mm(norm_t[...], grad_upper).astype(BF16)
        low, high = stretches(parts)[i]
        for part in range(low, high):
            mine = value[:, (part - low) * chunk : (part - low + 1) * chunk]
            if aligned:
                mine = mine.reshape(held.shape[2], 2, held.shape[3], chunk)
                held[0, part, :, :, :chunk] = mine[:, 0]
                held[1, part, :, :, :chunk] = mine[:, 1]
            else:
                held[0, part] = mine
        if not aligned:
            copies.out(held.at[0, low:high], shares[0].at[low:high])
    for copy in last:
        copy.wait()
    unit, root = normalize(mid[...])
    back, gain_sum = norm_back(sums[...], unit, root, vectors[2:3, :])
    gain_grad[...] = gain_sum
    mid[...] = grads[...].astype(F32) + back
    copies.out(mid, grad_middle)
    low_grad = mid[...].astype(BF16)
    heads[...] = mm(low_grad, out_w[...], NT).astype(BF16)
    copies.out(heads.at[:, :half], gm_near)
    copies.out(heads.at[:, half:], gm_far)
    turned = jnp.concatenate([mixed[0], mixed[1]], axis=1).T
    value = mm(turned, low_grad).astype(BF16)
    if aligned:
        blocks, own = held.shape[2:4]
        value = value.reshape(blocks, 2, own, 2 * half)
        cols = 2 * half // parts
        lanes = held.shape[4] - chunk
        for part in range(parts):
            mine = value[..., part * cols : (part + 1) * cols]
            pad = jnp.zeros(mine.shape[:-1] + (lanes - cols,), BF16)
            mine = jnp.concatenate([mine, pad], axis=-1)
            held[0, part, :, :, chunk:] = mine[:, 0]
            held[1, part, :, :, chunk:] = mine[:, 1]
        copies.out(held.at[1 - c], shares[0])
        copies.out(held.at[c], shares[1])
    else:
        natural[0][...] = value
        copies.out(natural[0], shares[1])
    copies.finish()


def feed_back(
    scalars, vectors, ga, gb, normed, slope, w_up, w_down, middle, mine, other, w_out, parts, blocks, lanes, aligned,
    order=None,
):
    rows, width = ga.shape
    count, half = 2 * rows, width // 2
    ff = w_up.shape[1]
    chunk = ff // parts
    if aligned:
        shares = [pltpu.HBM((parts, blocks, width // blocks // 2, lanes), BF16)] * 2
        held = [pltpu.VMEM((2,) + shares[0].shape, BF16)]
    else:
        shares = [jax.ShapeDtypeStruct((parts, width, chunk), BF16), jax.ShapeDtypeStruct((width, width), BF16)]
        held = [pltpu.VMEM((1,) + shares[0].shape, BF16), pltpu.VMEM((width, width), BF16)]
    scratch = [
        pltpu.VMEM((count, width), BF16),
        pltpu.VMEM((count, width), BF16),
        pltpu.VMEM((width, count), BF16),
        pltpu.VMEM((count, ff), BF16),
        pltpu.VMEM((width, ff), BF16),
        pltpu.VMEM((ff, width), BF16),
        pltpu.VMEM((count, width), F32),
        pltpu.VMEM((count, width), F32),
        pltpu.VMEM((2, count, half), BF16),
        pltpu.VMEM((width, width), BF16),
        pltpu.VMEM((count, width), BF16),
    ]
    scratch += held + [pltpu.SemaphoreType.DMA((13 + 5 * parts,))]
    outs = [
        pltpu.HBM((count, width), F32),
        pltpu.HBM((count, half), BF16),
        pltpu.HBM((count, half), BF16),
        jax.ShapeDtypeStruct((1, width), F32),
    ]
    return call(
        functools.partial(feed_back_body, aligned=aligned),
        "feed_back",
        scalars,
        (vectors, ga, gb, in_hbm(normed), in_hbm(slope), in_hbm(w_up), in_hbm(w_down), in_hbm(middle), mine, other, in_hbm(w_out)),
        [whole(vectors.shape)] + [ANY] * 10,
        outs + shares,
        [ANY] * 3 + [whole((1, width))] + [ANY] * 2,
        scratch=scratch,
        vmem=48,
        order=order,
        us=18,
    )


def attend_back_body(s_ref, *refs, pair):
    qs, dos, outs, lses = refs[0:2], refs[2:4], refs[4:6], refs[6:8]
    k0, k1, v0, v1, dq0, dq1, dk, dv, keys, vals = refs[8:]
    count = qs[0].shape[0]
    keys[:count, :], keys[count:, :] = k0[...], k1[...]
    vals[:count, :], vals[count:, :] = v0[...], v1[...]
    lanes = lax.broadcasted_iota(jnp.int32, (1, 128), 1)
    picks = lax.broadcasted_iota(jnp.int32, (8, 128), 1) // HEAD_DIM == lax.broadcasted_iota(jnp.int32, (8, 128), 0)
    picks = picks.astype(BF16)
    keys_t = keys[...].T
    turned = {}
    inners = []
    for b in range(2):
        product = dos[b][...].astype(F32) * outs[b][...].astype(F32)
        high = product.astype(BF16)
        low = (product - high.astype(F32)).astype(BF16)
        inners.append(mm(picks, high, NT) + mm(picks, low, NT))
        turned[b] = (qs[b][...].T, dos[b][...].T)
    grads_q = [[], []]
    grads_k, grads_v = [], []
    for h in range(2):
        head = slice(64 * h, 64 * h + 64)
        mask = (lanes >= 64) == (h == 1)
        grad_k = grad_v = None
        for b in range(2):
            q_head = jnp.where(mask, qs[b][...], jnp.zeros_like(qs[b][...]))
            do_head = jnp.where(mask, dos[b][...], jnp.zeros_like(dos[b][...]))
            weights = jnp.exp(mm(keys[...], q_head, NT) - lses[b][2 * pair + h : 2 * pair + h + 1, :])
            grad_weights = mm(vals[...], do_head, NT)
            grad_scores = (weights * (grad_weights - inners[b][h : h + 1, :])).astype(BF16)
            term = mm(turned[b][1][head], weights.astype(BF16), NT)
            grad_v = term if b == 0 else grad_v + term
            term = mm(turned[b][0][head], grad_scores, NT)
            grad_k = term if b == 0 else grad_k + term
            grads_q[b].append(mm(keys_t[head], grad_scores))
        grads_k.append(grad_k)
        grads_v.append(grad_v)
    for b, out in enumerate((dq0, dq1)):
        out[...] = (jnp.concatenate(grads_q[b], axis=0).T * SCALE).astype(BF16)
    dk[...] = jnp.concatenate(grads_k, axis=0).T.astype(BF16)
    dv[...] = jnp.concatenate(grads_v, axis=0).T.astype(BF16)


def attend_back(scalars, near, far, pair, order=None):
    count, half = near[1].shape
    ins = [a for both in zip(near, far) for a in both] + [near[0], far[0]] * 2
    pairs = half // 128
    lane = lambda t: pl.BlockSpec((count, 128), lambda g, s: (0, t * pairs + pair))
    one = jax.ShapeDtypeStruct((count, 128), BF16)
    two = jax.ShapeDtypeStruct((2 * count, 128), BF16)
    outs = [one, one, two, two]
    return call(
        functools.partial(attend_back_body, pair=pair),
        "attend_back",
        scalars,
        ins,
        [lane(0)] * 6 + [whole(near[3].shape)] * 2 + [lane(1), lane(1), lane(2), lane(2)],
        outs,
        [whole(o.shape) for o in outs],
        scratch=[pltpu.VMEM((2 * count, 128), BF16), pltpu.VMEM((2 * count, 128), BF16)],
        order=order,
        us=1.5,
        vmem=28,
    )


def side_by_side(refs):
    return jnp.concatenate([refs[3 * pair + t][...] for t in range(3) for pair in range(len(refs) // 3)], axis=1)


def pair_specs(grads, part, count):
    arrays, specs = [], []
    for near, far, dk, dv in grads:
        arrays += [(near, far)[part], dk, dv]
        specs += [whole((count, 128))] + [pl.BlockSpec((count, 128), lambda g, s: (part, 0))] * 2
    return arrays, specs


def project_back_body(s_ref, weight, *refs):
    refs[-1][...] = mm(side_by_side(refs[:-1]), weight[...], NT).astype(BF16)


def project_back(scalars, grads, weight, part, order=None):
    count = grads[0][0].shape[0]
    arrays, specs = pair_specs(grads, part, count)
    out = jax.ShapeDtypeStruct((count, weight.shape[0]), BF16)
    return call(
        project_back_body,
        "project_back",
        scalars,
        [weight] + arrays,
        [whole(weight.shape)] + specs,
        [out],
        [whole(out.shape)],
        order=order,
        us=1.0,
        vmem=16,
    )[0]


def turn_body(s_ref, ha, hb, xa, xb, vectors, *refs):
    out = refs[-1]
    rows = ha.shape[0]
    for at, block in enumerate((ha, hb, xa, xb)):
        unit, _ = normalize(block[...].astype(F32) + vectors[0:1, :])
        out[:, at * rows : (at + 1) * rows] = (unit * vectors[1:2, :]).astype(BF16).T


def hold(scalars, awaited, carry, order=None):
    return call(
        lambda *refs: None, "hold", scalars, (awaited,), [ANY], [], [], carry=carry, order=order, us=0.5, vmem=4
    )


def turned_tokens(scalars, ha, hb, xa, xb, vectors, order=None):
    ins = (ha, hb, xa, xb, vectors)
    out = jax.ShapeDtypeStruct((ha.shape[1], 4 * ha.shape[0]), BF16)
    return call(
        turn_body,
        "turned",
        scalars,
        ins,
        [whole(a.shape) for a in ins],
        [out],
        [whole(out.shape)],
        order=order,
        us=1,
        vmem=16,
    )[0]


def qkv_weight_body(s_ref, turned, *refs, pairs, aligned):
    out = refs[4 * pairs]
    grads = refs[-2] if aligned else refs[-1]
    count = refs[0].shape[0]
    lanes = grads.shape[1] // 3
    for pair in range(pairs):
        near, far, dk, dv = refs[4 * pair : 4 * pair + 4]
        here = slice(128 * pair, 128 * pair + 128)
        grads[:count, here] = near[...]
        grads[count:, here] = far[...]
        grads[:, lanes + 128 * pair : lanes + 128 * pair + 128] = dk[...]
        grads[:, 2 * lanes + 128 * pair : 2 * lanes + 128 * pair + 128] = dv[...]
    value = mm(turned[...], grads[...]).astype(BF16)
    if not aligned:
        out[...] = value
        return
    out[...] = value.reshape(out.shape)
    copies = Copies(refs[-1])
    bits = out.shape[0].bit_length() - 1
    for half, order in enumerate(orders(bits)):
        send = refs[4 * pairs + 1 + half]
        for g in range(send.shape[0]):
            copies.out(out.at[step_index(order, 0, s_ref[1], g), half], send.at[g])
    copies.finish()


def qkv_weight(scalars, turned, grads, blocks, aligned, order=None):
    width, count = turned.shape
    pairs = len(grads)
    lanes = 3 * 128 * pairs
    own = width // blocks // 2
    ins = [turned] + [a for four in grads for a in four]
    outs = [pltpu.HBM((blocks, 2, own, lanes) if aligned else (width, lanes), BF16)]
    specs = [whole(outs[0].shape)]
    scratch = [pltpu.VMEM((count, lanes), BF16)]
    if aligned:
        outs += [jax.ShapeDtypeStruct((blocks // 2, own, lanes), BF16)] * 2
        specs += [ANY] * 2
        scratch += [pltpu.SemaphoreType.DMA((blocks,))]
    return call(
        functools.partial(qkv_weight_body, pairs=pairs, aligned=aligned),
        "qkv_weight",
        scalars,
        ins,
        [whole(a.shape) for a in ins],
        outs,
        specs,
        scratch=scratch,
        order=order,
        us=2.5,
        vmem=24,
    )


def base_body(s_ref, ha, hb, vectors, grad_middle, weight, part_in, gain_two, *refs):
    ia, ib, sums = refs[-3:]
    rows = ha.shape[0]
    gain = vectors[1:2, :]
    grad_normed = mm(side_by_side(refs[:-3]), weight[...], NT) + part_in[...].astype(F32)
    gain_sum, base_sum = None, None
    for at, (block, out) in enumerate(((ha, ia), (hb, ib))):
        here = slice(at * rows, (at + 1) * rows)
        unit, root = normalize(block[...].astype(F32) + vectors[0:1, :])
        back, part = norm_back(grad_normed[here], unit, root, gain)
        grad = grad_middle[here, :] + back
        out[...] = grad.astype(BF16)
        gain_sum = part if gain_sum is None else gain_sum + part
        tokens = jnp.sum(grad, axis=0, keepdims=True)
        base_sum = tokens if base_sum is None else base_sum + tokens
    sums[0:1, :] = gain_sum
    sums[1:2, :] = gain_two[...]
    sums[2:3, :] = base_sum


def base_back(scalars, ha, hb, vectors, grad_middle, grads, weight, part_in, gain_two, order=None):
    rows, width = ha.shape
    arrays, specs = pair_specs(grads, 0, 2 * rows)
    grad_middle = in_hbm(grad_middle)
    ins = (ha, hb, vectors, grad_middle, weight, part_in, gain_two)
    outs = [
        jax.ShapeDtypeStruct((rows, width), BF16),
        jax.ShapeDtypeStruct((rows, width), BF16),
        jax.ShapeDtypeStruct((3, width), F32),
    ]
    return call(
        base_body,
        "base_back",
        scalars,
        list(ins) + arrays,
        [Staged(a) if a is grad_middle else whole(a.shape) for a in ins] + specs,
        outs,
        [whole(o.shape) for o in outs],
        order=order,
        us=1.75,
        vmem=24,
    )


def meet_body(s_ref, held, got, out, *, which, at):
    rows = held.shape[0] - 2
    out[0:2, :] = held[0:2, :] + got[0:2, :]
    if which is None:
        out[2:, :] = held[2:, :] + got[2:, :]
        return
    first = bit(s_ref[which], at) == 0
    mine, other = held[2:, :], got[2:, :]
    out[2 : 2 + rows, :] = jnp.where(first, mine, other)
    out[2 + rows :, :] = jnp.where(first, other, mine)


def meet(scalars, held, got, which, at, carry=(), order=None):
    rows, lanes = held.shape
    out = jax.ShapeDtypeStruct((rows if which is None else 2 * rows - 2, lanes), F32)
    return call(
        functools.partial(meet_body, which=which, at=at),
        "meet",
        scalars,
        (held, got),
        [whole(held.shape)] * 2,
        [out],
        [whole(out.shape)],
        carry=carry,
        order=order,
        us=1.5,
        vmem=4,
    )


def table_body(s_ref, sums, out):
    out[...] = jnp.zeros_like(out)
    for at in range(sums.shape[0] - 2):
        here = pl.ds(s_ref[at], 1)
        out[here, :] = out[here, :] + sums[at + 2 : at + 3, :]


def table_of(steps, sums, count, order=None):
    out = pltpu.HBM((count, sums.shape[1]), F32)
    return call(
        table_body,
        "table",
        steps,
        (sums,),
        [whole(sums.shape)],
        [out],
        [whole(out.shape)],
        order=order,
        us=1.25,
        vmem=12,
    )[0]


def fold(name, scalars, outs, order=None, split=False):
    ins, specs, known = [], [], {}
    for _, _, entries in outs:
        for _, _, terms in entries:
            for array, _, far in terms:
                if id(array) not in known:
                    known[id(array)] = len(ins)
                    ins.append(in_hbm(array) if far else array)
                    specs.append(ANY)
    scratch = [pltpu.VMEM(block, t[0].dtype) for _, _, entries in outs for _, block, terms in entries for t in terms]
    given = len(ins)

    def body(s_ref, *refs):
        arrays, targets = refs[:given], refs[given : given + len(shapes)]
        held = list(refs[given + len(shapes) : -1])
        copies = Copies(refs[-1])
        if split:
            sides, targets = targets, [held.pop()]
        waiting = []
        for (_, _, entries), target in zip(outs, targets):
            for to, _, terms in entries:
                mine = []
                for array, where, _ in terms:
                    slot = held.pop(0)
                    mine.append((copies.start(arrays[known[id(array)]].at[where(s_ref)], slot), slot))
                waiting.append((target, to, mine))
        for target, to, mine in waiting:
            total = None
            for copy, slot in mine:
                copy.wait()
                total = slot[...].astype(F32) if total is None else total + slot[...].astype(F32)
            target[to] = total[..., : target[to].shape[-1]].astype(target.dtype)
        if split:
            copies.out(targets[0].at[1 - s_ref[0]], sides[0])
            copies.out(targets[0].at[s_ref[0]], sides[1])
            copies.finish()

    shapes = [jax.ShapeDtypeStruct(o[0], o[1]) for o in outs]
    if split:
        shapes = [pltpu.HBM(outs[0][0][1:], outs[0][1])] * 2
        scratch.append(pltpu.VMEM(outs[0][0], outs[0][1]))
    return call(
        body,
        name,
        scalars,
        ins,
        specs,
        shapes,
        [ANY if split else whole(o.shape) for o in shapes],
        scratch=scratch + [pltpu.SemaphoreType.DMA((len(scratch) + 2,))],
        order=order,
        us=2.5,
        vmem=16,
    )


def bit(value, at):
    return (value >> at) & 1


def orders(bits):
    return (list(range(bits)), list(range(bits))[::-1])


def step_index(order, step, own, g):
    value = (1 - bit(own, order[step])) << order[step]
    for at in order[:step]:
        value = value + (bit(own, at) << at)
    for i, at in enumerate(order[step + 1 :]):
        value = value + (bit(g, i) << at)
    return value


def held_index(order, step, block):
    value = block * 0
    for i, at in enumerate(order[step + 1 :]):
        value = value + (bit(block, at) << i)
    return value


class Segment:
    def __init__(self, low, high, terms):
        self.low, self.high, self.terms = low, high, list(terms)


class Reduction:
    def __init__(self, swap, pieces, seq_bits, has_seq=True):
        self.swap, self.pieces, self.seq_bits = swap, pieces, seq_bits
        self.seq_orders = [orders(seq_bits)[at % 2] for at in range(len(pieces))]
        self.steps = len(pieces[0][0])
        self.rows = sum(p[2] for p in pieces)
        self.lanes = pieces[0][3][-1].high
        self.lead = (1 << seq_bits,) if has_seq else ()
        self.got = [[] for _ in pieces]
        self.got_seq = [[] for _ in pieces]

    def entries(self, at, to, block_of, seq_of=None):
        order, first, rows, segments = self.pieces[at]
        every = slice(None)
        out = []
        for segment in segments:
            width = segment.high - segment.low
            terms = []
            for array, where, far in segment.terms:
                place = lambda s, where=where: where(block_of(s), None if seq_of is None else seq_of(s))
                terms.append((array, place, far))
            for step, array in self.got[at]:

                def place(s, step=step, lanes=pl.ds(segment.low, width)):
                    block = held_index(order, step, block_of(s))
                    if not self.lead:
                        return (block, every, lanes)
                    return (block, every if seq_of is None else seq_of(s), every, lanes)

                terms.append((array, place, False))
            if seq_of is not None:
                for step, array in self.got_seq[at]:
                    place = lambda s, step=step, lanes=pl.ds(segment.low, width): (
                        held_index(self.seq_orders[at], step, seq_of(s)),
                        every,
                        lanes,
                    )
                    terms.append((array, place, False))
            block = (self.lead if seq_of is None else ()) + (rows, width)
            out.append((to + (Ellipsis, slice(segment.low, segment.high)), block, terms))
        return out

    def leaving(self, step):
        count = 1 << (self.steps - 1 - step)
        outs = []
        for at, (order, _, rows, _) in enumerate(self.pieces):
            entries = []
            for g in range(count):
                entries += self.entries(at, (g,), lambda s, g=g, order=order: step_index(order, step, s[1], g))
            outs.append(((count,) + self.lead + (rows, self.lanes), BF16, entries))
        if step == self.steps - 1 and self.lead:
            for at, (_, _, rows, _) in enumerate(self.pieces):
                outs.append((self.lead + (rows, self.lanes), F32, self.entries(at, (), lambda s: s[1])))
        return outs

    def send(self, step, sent):
        count = len(self.pieces)
        every = slice(None)
        for at, (order, _, _, segments) in enumerate(self.pieces):
            if len(sent) > count:
                self.got[at] = []
                for segment in segments:
                    lanes = pl.ds(segment.low, segment.high - segment.low)
                    where = lambda block, seq, lanes=lanes: (every if seq is None else seq, every, lanes)
                    segment.terms = [(sent[count + at], where, False)]
            self.got[at].append((step, self.swap(sent[at], 2 << order[step], 0)))

    def leaving_seq(self, step):
        count = 1 << (self.seq_bits - 1 - step)
        outs = []
        for at, (_, _, rows, _) in enumerate(self.pieces):
            entries = []
            for g in range(count):
                seq_of = lambda s, g=g, order=self.seq_orders[at]: step_index(order, step, s[2], g)
                entries += self.entries(at, (g,), lambda s: s[1], seq_of)
            outs.append(((count, rows, self.lanes), BF16, entries))
        return outs

    def send_seq(self, step, sent):
        for at, value in enumerate(sent):
            self.got_seq[at].append((step, self.swap(value, 0, 1 << self.seq_orders[at][step])))

    def last(self, segment, lanes, row_of):
        entries = []
        for piece, (_, _, rows, _) in enumerate(self.pieces):
            _, block, terms = self.entries(piece, (), lambda s: s[1], lambda s: s[2])[segment]
            entries.append(((slice(row_of(piece), row_of(piece) + rows), lanes), block, terms))
        return entries


def columns_body(s_ref, mine, other, keep, *sends):
    even = s_ref[0] == 0
    here, there = mine[...].astype(F32), other[...].astype(F32)
    half = here.shape[1] // 3
    first, second = jnp.where(even, here, there), jnp.where(even, there, here)
    columns = []
    for t in range(3):
        columns += [first[:, t * half : t * half + half], second[:, t * half : t * half + half]]
    columns = jnp.concatenate(columns, axis=1)
    lanes = keep.shape[1]
    for at, target in enumerate((keep, *sends)):
        for part in range(len(sends) + 1):

            @pl.when((s_ref[2] ^ at) == part)
            def _(target=target, part=part):
                target[...] = columns[:, part * lanes : part * lanes + lanes].astype(target.dtype)


def on_device(
    row_count, seq_count, hidden_in, timesteps, step_table, gain_one, w_qkv, w_out, gain_two, w_up, w_down, out_grad
):
    seqs_here, tokens_here, width = hidden_in.shape
    ff = w_up.shape[1]
    half = width // 2
    blocks = row_count // 2
    block_bits = blocks.bit_length() - 1
    seq_bits = seq_count.bit_length() - 1
    r = lax.axis_index("rows")
    z = lax.axis_index("seq")
    c = lax.rem(r, 2)
    b = lax.div(r, 2)
    odd = lax.rem(z, 2)
    axes = ("rows", "seq")

    def flat(row, seq):
        return row * seq_count + seq

    def swap(value, row_bit, seq_bit=0):
        pairs = [
            (flat(i, j), flat(i ^ row_bit, j ^ seq_bit)) for i in range(row_count) for j in range(seq_count)
        ]
        return lax.ppermute(value, axes, pairs)

    def core_swap(value):
        return swap(value, 1)

    moves = []
    for turn in range(2):
        moves.append(
            [
                (flat(2 * p + e, j), flat(2 * p + j // 2, 2 * e + (j + turn) % 2))
                for p in range(blocks)
                for e in range(2)
                for j in range(seq_count)
            ]
        )

    def gather_tokens(leaving):
        return tuple(lax.ppermute(value, axes, move) for value, move in zip(leaving, moves))

    def share(value, at, axis):
        return lax.dynamic_index_in_dim(value, at, axis, keepdims=False)

    def send_back(*values):
        return [lax.ppermute(value, axes, [(t, s) for s, t in move]) for value, move in zip(values, moves)]

    scalars = jnp.stack([c, b, z]).astype(jnp.int32)

    steps_all = lax.all_gather(timesteps, "rows", axis=0, tiled=True)
    steps_held = steps_all.reshape(blocks, seq_count).T.reshape(-1)
    step_now = lax.dynamic_index_in_dim(steps_all, seq_count * b + z, 0, keepdims=False)
    row = lax.dynamic_slice_in_dim(step_table, step_now, 1, 0).astype(F32)

    order = Order()
    weight, vectors = prepare(scalars, row, gain_one[None, :], gain_two[None, :], w_qkv)
    ha, hb = gather_tokens([share(hidden_in, at, 0) for at in (odd, 1 - odd)])
    xa, xb = core_swap(ha), core_swap(hb)
    near = qkv(scalars, ha, hb, vectors, weight, order=order, us=8)
    late_grad, _, _ = lax.optimization_barrier((out_grad, ha, hb))
    ga, gb = gather_tokens([share(late_grad, at, 0) for at in (odd, 1 - odd)])
    far = qkv(scalars, xa, xb, vectors, weight, order=order)
    mixed_far, lse_far = attend(scalars, far, near, far, order=order)
    mixed_in = core_swap(mixed_far)
    mixed_near, lse_near = attend(scalars, near, near, far, order=order)

    parts = seq_count
    unit = ff // row_count
    own_rows, seq_cols, up_cols = width // row_count, width // seq_count, ff // seq_count
    whole_units = blocks == parts and unit % 128 == 0
    whole_rows = own_rows % 32 == 0

    oa, ob, middle, normed_two, slope, down_far, down_near = forward_pass(
        scalars, ha, hb, vectors, mixed_near, mixed_in, w_out, w_up, w_down, ga, gb, parts, order=order
    )
    if not whole_units:
        sides = [jnp.where(c == side, down_near, down_far) for side in range(2)]
        natural = jnp.concatenate(sides, axis=2).transpose(1, 0, 2).reshape(parts, seq_cols, blocks, 2, unit)
        down_far, down_near = (share(natural, at, 3).transpose(2, 0, 1, 3) for at in (1 - c, c))
    down_shape = (blocks, parts, seq_cols, unit)
    down_far, down_near = down_far.reshape(down_shape), down_near.reshape(down_shape)
    down_in = core_swap(down_far)

    lanes = -(-(up_cols + seq_cols) // 256) * 256
    grad_middle, gm_near, gm_far, gain_two_part, up_far, up_near = feed_back(
        scalars, vectors, ga, gb, normed_two, slope, w_up, w_down, middle, mixed_near, mixed_in, w_out,
        parts, blocks, lanes, whole_rows, order=order,
    )
    if not whole_rows:
        up_all = up_far.reshape(parts, blocks, 2, own_rows, up_cols)
        out_all = up_near.reshape(blocks, 2, own_rows, parts, seq_cols).transpose(3, 0, 1, 2, 4)
        blank = jnp.zeros(up_all.shape[:-1] + (lanes - up_cols - seq_cols,), BF16)
        natural = jnp.concatenate([up_all, out_all, blank], axis=-1)
        up_far, up_near = (share(natural, at, 2) for at in (1 - c, c))

    fold_over = functools.partial(fold, "reduce", scalars, order=order)
    both = orders(block_bits)
    every = slice(None)

    def taken(array, by_seq, first, rows, some):
        def where(block, seq):
            seq = every if seq is None else seq
            place = (seq, block) if by_seq else (block, seq)
            return place + (pl.ds(first, rows),) + (() if some is None else (some,))

        return (array, where, array is down_near or array is up_near)

    def segment(low, high, arrays, by_seq, first, rows, lanes=None):
        return Segment(low, high, [taken(array, by_seq, first, rows, lanes) for array in arrays])

    def up_segments(low, first, rows):
        cut = ((0, up_cols), (up_cols, lanes))
        return [segment(low + a, low + b, ups, True, first, rows, pl.ds(a, b - a)) for a, b in cut]

    def step_over(reductions, leaving, send, step):
        outs = [leaving(r, step) for r in reductions]
        sent = list(fold_over([o for out in outs for o in out]))
        for reduction, out in zip(reductions, outs):
            send(reduction, step, sent[: len(out)])
            del sent[: len(out)]

    step_blocks = functools.partial(step_over, leaving=Reduction.leaving, send=Reduction.send)
    step_seq = functools.partial(step_over, leaving=Reduction.leaving_seq, send=Reduction.send_seq)

    gm_far, up_far, oa, ob = hold(scalars, down_in, (gm_far, up_far, oa, ob), order=order)
    up_in = core_swap(up_far)
    gm_in = core_swap(gm_far)
    turned = turned_tokens(scalars, ha, hb, xa, xb, vectors, order=order)
    out_back = send_back(oa, ob)
    downs, ups = (down_near, down_in), (up_near, up_in)
    joined = whole_units and whole_rows and 2 * unit == up_cols and seq_cols == 2 * own_rows
    if joined:
        rows = own_rows // 2
        pieces = []
        for at in range(2):
            segments = [segment(t * unit, (t + 1) * unit, downs, False, (2 * at + t) * rows, rows) for t in range(2)]
            segments += up_segments(2 * unit, at * rows, rows)
            pieces.append((both[at], at * rows, rows, segments))
        everything = [Reduction(swap, pieces, seq_bits)]
    else:
        down = Reduction(swap, [(both[0], 0, seq_cols, [segment(0, unit, downs, False, 0, seq_cols)])], seq_bits)
        up = Reduction(swap, [(both[1], 0, own_rows, up_segments(0, 0, own_rows))], seq_bits)
        everything = [down, up]
    step_blocks(everything, step=0)
    sides = ((near, gm_near, mixed_near, lse_near), (far, gm_in, mixed_far, lse_far))
    grads = []
    for pair in range(half // 128):
        grads.append(attend_back(scalars, *sides, pair, order=order))
        if pair == 1:
            out_hidden = returned_blocks(scalars, *out_back, order=order)
    part_far = project_back(scalars, grads, weight, 1, order=order)
    part_in = core_swap(part_far)
    qkv_w = qkv_weight(scalars, turned, grads, blocks, whole_rows, order=order)
    for step in range(1, block_bits):
        step_blocks(everything, step=step)
    if whole_rows:
        qkv_blocks = qkv_w[0].reshape(blocks, 2 * own_rows, 3 * half)
        rows_of = lambda h: (lambda block, seq: (block, pl.ds(h * own_rows, own_rows)))
    else:
        qkv_blocks = qkv_w[0].reshape(blocks, 2, own_rows, 3 * half)
        rows_of = lambda h: (lambda block, seq: (block, h))
    project = Reduction(
        swap,
        [
            (both[h], h * own_rows, own_rows, [Segment(0, 3 * half, [(qkv_blocks, rows_of(h), True)])])
            for h in range(2)
        ],
        seq_bits,
        False,
    )
    if whole_rows:
        project.send(0, qkv_w[1:])
    else:
        step_blocks([project], step=0)
    ia, ib, held = base_back(
        scalars, ha, hb, vectors, grad_middle, grads, weight, part_in, gain_two_part, order=order
    )
    in_back = send_back(ia, ib)

    meetings = [(None, 0, 1, 0)]
    meetings += [(1, at, 2 << at, 0) for at in range(block_bits)]
    meetings += [(2, at, 0, 1 << at) for at in range(seq_bits)]

    def next_meeting(held, carry=()):
        which, at, row_bit, seq_bit = meetings.pop(0)
        out = meet(scalars, held, swap(held, row_bit, seq_bit), which, at, carry, order=order)
        return out if carry else out[0]

    held = next_meeting(held)
    in_grad = returned_blocks(scalars, *in_back, order=order)
    step_seq(everything, step=0)
    for step in range(1, block_bits):
        step_blocks([project], step=step)
    held = next_meeting(held)
    held = next_meeting(held)
    held = next_meeting(held)
    for step in range(1, seq_bits):
        step_seq(everything, step=step)
    entries = []
    for h in range(2):
        for _, block, terms in project.entries(h, (), lambda s: s[1]):
            entries.append(((h,), block, terms))
    qkv_far, qkv_mine = fold_over([((2, own_rows, 3 * half), BF16, entries)], split=True)
    held = next_meeting(held)
    shape = (own_rows, 6 * half // parts)
    qkv_keep, *qkv_sends = call(
        columns_body,
        "qkv_columns",
        scalars,
        (qkv_mine, core_swap(qkv_far)),
        [whole(qkv_mine.shape)] * 2,
        [jax.ShapeDtypeStruct(shape, F32)] + [jax.ShapeDtypeStruct(shape, BF16)] * (parts - 1),
        [whole(shape)] * parts,
        vmem=12,
        order=order,
    )
    qkv_terms = [qkv_keep] + [swap(value, 0, at + 1) for at, value in enumerate(qkv_sends)]
    while meetings:
        held = next_meeting(held)
    table = table_of(steps_held, held, step_table.shape[0], order=order)
    if joined:
        block = everything[0]
        down_entries = block.last(0, slice(None), lambda piece: 2 * piece * rows)
        down_entries += block.last(1, slice(None), lambda piece: (2 * piece + 1) * rows)
        up_block, up_at, row_of = block, 2, lambda piece: piece * rows
    else:
        down_entries = down.last(0, slice(None), lambda piece: 0)
        up_block, up_at, row_of = up, 0, lambda piece: 0
    up_entries = up_block.last(up_at, slice(0, up_cols), row_of)
    out_entries = up_block.last(up_at + 1, slice(0, seq_cols), row_of)
    qkv_entry = ((Ellipsis,), shape, [(value, lambda s: (slice(None),), False) for value in qkv_terms])
    down_shard, up_shard, out_shard, qkv_shard = fold_over(
        [
            ((seq_cols, unit), F32, down_entries),
            ((own_rows, up_cols), F32, up_entries),
            ((own_rows, seq_cols), F32, out_entries),
            (shape, F32, [qkv_entry]),
        ]
    )


    return (
        out_hidden,
        in_grad,
        table,
        held[0],
        qkv_shard,
        out_shard,
        held[1],
        up_shard,
        down_shard.T,
    )


def solution(mesh):
    tokens = P("rows", "seq", None)
    split = P("rows", "seq")
    in_specs = (tokens, P("rows"), P(), P(), P(), P(), P(), P(), P(), tokens)
    out_specs = (tokens, tokens, P(), P(), split, split, P(), split, split)
    body = functools.partial(on_device, mesh.shape["rows"], mesh.shape["seq"])
    return jax.shard_map(body, mesh=mesh, in_specs=in_specs, out_specs=out_specs, check_vma=False)
```

```python
import functools

import jax
import jax.numpy as jnp
from jax import lax
from jax.experimental import pallas as pl
from jax.experimental.pallas import tpu as pltpu
from jax.sharding import PartitionSpec as P

HEAD_DIM = 64
SCALE = HEAD_DIM ** (-0.5)
EPS = 1e-05
F32 = jnp.float32
BF16 = jnp.bfloat16
MIB = 1 << 20
PER_US = 1_000_000_000

NN = (((1,), (0,)), ((), ()))
NT = (((1,), (1,)), ((), ()))


def mm(a, b, dims=NN):
    return lax.dot_general(a, b, dims, preferred_element_type=F32)


def normalize(values):
    average = jnp.mean(values, axis=-1, keepdims=True)
    centred = values - average
    inverse_root = lax.rsqrt(jnp.mean(centred * centred, axis=-1, keepdims=True) + EPS)
    return (centred * inverse_root, inverse_root)


def norm_back(grad_normed, unit_rows, inverse_root, scale_gain):
    gained = grad_normed * scale_gain
    centred_grad = (
        gained
        - jnp.mean(gained, axis=-1, keepdims=True)
        - unit_rows * jnp.mean(gained * unit_rows, axis=-1, keepdims=True)
    )
    return (inverse_root * centred_grad, jnp.sum(grad_normed * unit_rows, axis=0, keepdims=True))


def whole(shape):
    return pl.BlockSpec(shape, lambda *_: (0,) * len(shape))


class Staged:
    def __init__(self, array):
        self.memory = pltpu.VMEM(array.shape, array.dtype)


class Order:
    def __init__(self):
        self.token = None


def call(
    body, name, scalars, ins, in_specs, outs, out_specs, grid=(1,), scratch=(), vmem=32, order=None, us=1.0, carry=()
):
    ins, in_specs, outs, out_specs = list(ins), list(in_specs), list(outs), list(out_specs)
    count, given = len(ins), len(outs)
    staged = [at for at, spec in enumerate(in_specs) if isinstance(spec, Staged)]
    held = [in_specs[at].memory for at in staged]
    for at in staged:
        in_specs[at] = ANY
    waits = [] if order is None or order.token is None else [order.token]
    inner = body

    def body(scalars_ref, *refs):
        refs = list(refs)
        del refs[count : count + len(carry) + len(waits)]
        del refs[count + given : count + given + len(carry)]
        if order is not None:
            token = refs.pop(count + given)
            token[...] = jnp.zeros_like(token)
        if staged:
            sems, slots = refs.pop(), refs[len(refs) - len(held) :]
            del refs[len(refs) - len(held) :]
            copies = [pltpu.make_async_copy(refs[at], slot, sems.at[i]) for i, (at, slot) in enumerate(zip(staged, slots))]
            for copy in copies:
                copy.start()
            for at, slot in zip(staged, slots):
                refs[at] = slot
            for copy in copies:
                copy.wait()
        inner(scalars_ref, *refs)

    ins += [in_hbm(value) for value in carry] + waits
    in_specs += [ANY] * (len(carry) + len(waits))
    outs += [pltpu.HBM(value.shape, value.dtype) for value in carry]
    out_specs += [ANY] * len(carry)
    if order is not None:
        outs.append(jax.ShapeDtypeStruct((8, 128), F32))
        out_specs.append(whole((8, 128)))
    scratch = list(scratch) + held + ([pltpu.SemaphoreType.DMA((len(staged),))] if staged else [])
    result = pl.pallas_call(
        body,
        name=name,
        grid_spec=pltpu.PrefetchScalarGridSpec(
            num_scalar_prefetch=1,
            grid=grid,
            in_specs=in_specs,
            out_specs=out_specs,
            scratch_shapes=scratch,
        ),
        out_shape=outs,
        input_output_aliases={1 + count + at: given + at for at in range(len(carry))},
        cost_estimate=pl.CostEstimate(flops=int(us * PER_US), bytes_accessed=1 << 10, transcendentals=0),
        compiler_params=pltpu.CompilerParams(vmem_limit_bytes=vmem * MIB),
    )(scalars, *ins)
    result = list(result)
    if order is not None:
        order.token = result.pop()
    return result


def in_hbm(value):
    return pltpu.with_memory_space_constraint(value, pltpu.HBM)


ANY = pl.BlockSpec(memory_space=pl.ANY)


def gelu_both(upper):
    square = upper * upper
    turned = jnp.tanh(upper * (GELU_A + GELU_A * GELU_B * square))
    half_up = 0.5 + 0.5 * turned
    active = upper * half_up
    slope = half_up + active * (1.0 - turned) * (GELU_A + 3.0 * GELU_A * GELU_B * square)
    return active.astype(BF16), slope.astype(BF16)


class Copies:
    def __init__(self, sems):
        self.sems, self.count, self.outs = sems, 0, []

    def start(self, source, target):
        copy = pltpu.make_async_copy(source, target, self.sems.at[self.count])
        self.count += 1
        copy.start()
        return copy

    def out(self, source, target):
        self.outs.append(self.start(source, target))

    def finish(self):
        for copy in self.outs:
            copy.wait()


GELU_A, GELU_B = 0.7978845608028654, 0.044715


def stretches(parts):
    return [(at, min(at + 2, parts)) for at in range(0, parts, 2)]


def prepare_body(s_ref, row, first, second, wq, wk, wv, out, vectors):
    half = wq.shape[1]
    for t, w in enumerate((wq, wk, wv)):
        out[:, t * half : t * half + half] = w[...]
    for at, value in enumerate((row, first, second)):
        vectors[at : at + 1, :] = value[...]


def prepare(scalars, row, gain_one, gain_two, w_qkv, order=None):
    width = w_qkv.shape[0]
    half = width // 2
    specs = [whole((1, width))] * 3
    specs += [pl.BlockSpec((width, half), functools.partial(lambda t, g, s: (0, 2 * t + s[0]), t)) for t in range(3)]
    outs = [jax.ShapeDtypeStruct((width, 3 * half), BF16), jax.ShapeDtypeStruct((8, width), F32)]
    return call(
        prepare_body,
        "prepare",
        scalars,
        (row, gain_one, gain_two) + (in_hbm(w_qkv),) * 3,
        specs,
        outs,
        [whole(o.shape) for o in outs],
        order=order,
        us=2,
        vmem=12,
    )


def returned_body(s_ref, first, second, out, sems):
    at = bit(s_ref[2], 0)
    copies = Copies(sems)
    copies.out(first, out.at[at])
    copies.out(second, out.at[1 - at])
    copies.finish()


def returned_blocks(scalars, first, second, order=None):
    return call(
        returned_body,
        "returned",
        scalars,
        (first, second),
        [ANY] * 2,
        [pltpu.HBM((2,) + first.shape, first.dtype)],
        [ANY],
        scratch=[pltpu.SemaphoreType.DMA((2,))],
        order=order,
        us=3,
        vmem=4,
    )[0]


def qkv_body(s_ref, ha, hb, vectors, weight, out, normed):
    row, gain = vectors[0:1, :], vectors[1:2, :]
    rows = ha.shape[0]
    half = out.shape[1] // 3
    for at, block in enumerate((ha, hb)):
        unit, _ = normalize(block[...].astype(F32) + row)
        normed[pl.ds(at * rows, rows), :] = (unit * gain).astype(BF16)
    packed = mm(normed[...], weight[...]).astype(BF16)
    out[:, :half] = (packed[:, :half] * SCALE).astype(BF16)
    out[:, half:] = packed[:, half:]


def qkv(scalars, ha, hb, vectors, weight, order=None, us=2.3):
    rows, width = ha.shape
    ins = (ha, hb, vectors, weight)
    out = jax.ShapeDtypeStruct((2 * rows, weight.shape[1]), BF16)
    return call(
        qkv_body,
        "qkv",
        scalars,
        ins,
        [whole(a.shape) for a in ins],
        [out],
        [whole(out.shape)],
        scratch=[pltpu.VMEM((2 * rows, width), BF16)],
        order=order,
        us=us,
        vmem=16,
    )[0]


def attend_body(s_ref, q, k0, k1, v0, v1, mixed, lse):
    count, half = q.shape
    lanes = lax.broadcasted_iota(jnp.int32, (1, 128), 1)
    ones = jnp.ones((16, count), BF16)
    for pair in range(half // 128):
        cols = slice(128 * pair, 128 * pair + 128)
        q_pair = q[:, cols]
        vt = [v[:, cols].T for v in (v0, v1)]
        done = []
        for h in range(2):
            q_head = jnp.where((lanes >= 64) == (h == 1), q_pair, jnp.zeros_like(q_pair))
            scores = [mm(k[:, cols], q_head, NT) for k in (k0, k1)]
            highest = jnp.maximum(
                jnp.max(scores[0], axis=0, keepdims=True), jnp.max(scores[1], axis=0, keepdims=True)
            )
            total = None
            for part in range(2):
                weights = jnp.exp(scores[part] - highest).astype(BF16)
                left = jnp.concatenate([vt[part][64 * h : 64 * h + 64], ones], axis=0)
                term = mm(left, weights)
                total = term if total is None else total + term
            summed = total[64:65]
            done.append(total[:64] / summed)
            lse[2 * pair + h : 2 * pair + h + 1, :] = highest + jnp.log(summed)
        mixed[:, cols] = jnp.concatenate(done, axis=0).T.astype(BF16)


def attend(scalars, asked, near, far, order=None):
    count, half = asked.shape[0], asked.shape[1] // 3
    ins = (asked, near, far, near, far)
    outs = [jax.ShapeDtypeStruct((count, half), BF16), jax.ShapeDtypeStruct((8, count), F32)]
    return call(
        attend_body,
        "attend",
        scalars,
        ins,
        [pl.BlockSpec((count, half), functools.partial(lambda t, g, s: (0, t), t)) for t in (0, 1, 1, 2, 2)],
        outs,
        [whole(o.shape) for o in outs],
        order=order,
        us=6,
        vmem=24,
    )


def forward_pass_body(
    s_ref, vectors, ha, hb, m0, m1, wo, wu, wd, ga, gb,
    oa, ob, middle, normed, slope, far, near,
    tokens, mixed, out_w, up_w, down_w, grads, grads_t, mid, norm, out, slopes, shares, sems
):
    rows, half = ha.shape[0], m0.shape[1]
    parts = far.shape[0]
    chunk = 2 * half
    c = s_ref[0]
    copies = Copies(sems)
    first = [
        copies.start(m0, mixed.at[:, :half]),
        copies.start(m1, mixed.at[:, half:]),
        copies.start(wo.at[pl.ds(pl.multiple_of(c * half, half), half), :], out_w.at[:half, :]),
        copies.start(wo.at[pl.ds(pl.multiple_of((1 - c) * half, half), half), :], out_w.at[half:, :]),
        copies.start(ha, tokens.at[:rows, :]),
        copies.start(hb, tokens.at[rows:, :]),
    ]

    def ask(here):
        return (copies.start(wu.at[:, here], up_w.at[:, here]), copies.start(wd.at[here, :], down_w.at[here, :]))

    steps = [slice(low * chunk, high * chunk) for low, high in stretches(parts)]
    for copy in first:
        copy.wait()
    weights = [ask(steps[0])]
    turn = [copies.start(ga, grads.at[:rows, :]), copies.start(gb, grads.at[rows:, :])]
    mid[...] = tokens[...].astype(F32) + vectors[0:1, :] + mm(mixed[...], out_w[...])
    unit, _ = normalize(mid[...])
    norm[...] = (unit * vectors[2:3, :]).astype(BF16)
    copies.out(mid, middle)
    copies.out(norm, normed)
    for copy in turn:
        copy.wait()
    grads_t[...] = grads[...].T
    for i, here in enumerate(steps):
        if i + 1 < len(steps):
            weights.append(ask(steps[i + 1]))
        for copy in weights[i]:
            copy.wait()
        active, slopes[:, here] = gelu_both(mm(norm[...], up_w[:, here]))
        term = mm(active, down_w[here, :])
        out[...] = (mid if i == 0 else out)[...] + term
        value = mm(grads_t[...], active).astype(BF16)
        low, high = stretches(parts)[i]
        for part in range(low, high):
            for side in range(2):
                at = (part - low) * chunk + side * half
                shares[side, part] = value[:, at : at + half]
        copies.out(slopes.at[:, here], slope.at[:, here])
        copies.out(shares.at[1 - c, low:high], far.at[low:high])
        copies.out(shares.at[c, low:high], near.at[low:high])
    tokens[...] = out[...].astype(BF16)
    copies.out(tokens.at[:rows, :], oa)
    copies.out(tokens.at[rows:, :], ob)
    copies.finish()


def forward_pass(scalars, ha, hb, vectors, mine, other, w_out, w_up, w_down, ga, gb, parts, order=None):
    rows, width = ha.shape
    count, half = mine.shape
    ff = w_up.shape[1]
    outs = [
        pltpu.HBM((rows, width), BF16),
        pltpu.HBM((rows, width), BF16),
        pltpu.HBM((count, width), F32),
        pltpu.HBM((count, width), BF16),
        pltpu.HBM((count, ff), BF16),
        pltpu.HBM((parts, width, half), BF16),
        pltpu.HBM((parts, width, half), BF16),
    ]
    scratch = [
        pltpu.VMEM((count, width), BF16),
        pltpu.VMEM((count, width), BF16),
        pltpu.VMEM((width, width), BF16),
        pltpu.VMEM((width, ff), BF16),
        pltpu.VMEM((ff, width), BF16),
        pltpu.VMEM((count, width), BF16),
        pltpu.VMEM((width, count), BF16),
        pltpu.VMEM((count, width), F32),
        pltpu.VMEM((count, width), BF16),
        pltpu.VMEM((count, width), F32),
        pltpu.VMEM((count, ff), BF16),
        pltpu.VMEM((2, parts, width, half), BF16),
        pltpu.SemaphoreType.DMA((12 + 5 * parts,)),
    ]
    return call(
        forward_pass_body,
        "forward_pass",
        scalars,
        (vectors, ha, hb, mine, other, in_hbm(w_out), in_hbm(w_up), in_hbm(w_down), ga, gb),
        [whole(vectors.shape)] + [ANY] * 9,
        outs,
        [ANY] * 7,
        scratch=scratch,
        vmem=35,
        order=order,
        us=14,
    )


def feed_back_body(
    s_ref, vectors, ga, gb, normed, slope, wu, wd, middle, m0, m1, wo,
    grad_middle, gm_near, gm_far, gain_grad, *rest, aligned
):
    shares = rest[:2]
    grads, norm, norm_t, slopes, up_w, down_w, sums, mid, mixed, out_w, heads, held, *natural, sems = rest[2:]
    rows = ga.shape[0]
    half = m0.shape[1]
    parts = held.shape[1]
    chunk = wu.shape[1] // parts
    c = s_ref[0]
    copies = Copies(sems)
    first = [copies.start(ga, grads.at[:rows, :]), copies.start(gb, grads.at[rows:, :]), copies.start(normed, norm)]

    def ask(here):
        return (
            copies.start(wd.at[here, :], down_w.at[here, :]),
            copies.start(slope.at[:, here], slopes.at[:, here]),
            copies.start(wu.at[:, here], up_w.at[:, here]),
        )

    steps = [slice(low * chunk, high * chunk) for low, high in stretches(parts)]
    weights = [ask(steps[0])]
    for copy in first:
        copy.wait()
    norm_t[...] = norm[...].T
    last = []
    for i, here in enumerate(steps):
        if i + 1 < len(steps):
            weights.append(ask(steps[i + 1]))
        else:
            last = [
                copies.start(middle, mid),
                copies.start(wo.at[pl.ds(pl.multiple_of(c * half, half), half), :], out_w.at[:half, :]),
                copies.start(wo.at[pl.ds(pl.multiple_of((1 - c) * half, half), half), :], out_w.at[half:, :]),
                copies.start(m0, mixed.at[c]),
                copies.start(m1, mixed.at[1 - c]),
            ]
        for copy in weights[i]:
            copy.wait()
        grad_upper = (mm(grads[...], down_w[here, :], NT) * slopes[:, here].astype(F32)).astype(BF16)
        term = mm(grad_upper, up_w[:, here], NT)
        sums[...] = term if i == 0 else sums[...] + term
        value = mm(norm_t[...], grad_upper).astype(BF16)
        low, high = stretches(parts)[i]
        for part in range(low, high):
            mine = value[:, (part - low) * chunk : (part - low + 1) * chunk]
            if aligned:
                mine = mine.reshape(held.shape[2], 2, held.shape[3], chunk)
                held[0, part, :, :, :chunk] = mine[:, 0]
                held[1, part, :, :, :chunk] = mine[:, 1]
            else:
                held[0, part] = mine
        if not aligned:
            copies.out(held.at[0, low:high], shares[0].at[low:high])
    for copy in last:
        copy.wait()
    unit, root = normalize(mid[...])
    back, gain_sum = norm_back(sums[...], unit, root, vectors[2:3, :])
    gain_grad[...] = gain_sum
    mid[...] = grads[...].astype(F32) + back
    copies.out(mid, grad_middle)
    low_grad = mid[...].astype(BF16)
    heads[...] = mm(low_grad, out_w[...], NT).astype(BF16)
    copies.out(heads.at[:, :half], gm_near)
    copies.out(heads.at[:, half:], gm_far)
    turned = jnp.concatenate([mixed[0], mixed[1]], axis=1).T
    value = mm(turned, low_grad).astype(BF16)
    if aligned:
        blocks, own = held.shape[2:4]
        value = value.reshape(blocks, 2, own, 2 * half)
        cols = 2 * half // parts
        lanes = held.shape[4] - chunk
        for part in range(parts):
            mine = value[..., part * cols : (part + 1) * cols]
            pad = jnp.zeros(mine.shape[:-1] + (lanes - cols,), BF16)
            mine = jnp.concatenate([mine, pad], axis=-1)
            held[0, part, :, :, chunk:] = mine[:, 0]
            held[1, part, :, :, chunk:] = mine[:, 1]
        copies.out(held.at[1 - c], shares[0])
        copies.out(held.at[c], shares[1])
    else:
        natural[0][...] = value
        copies.out(natural[0], shares[1])
    copies.finish()


def feed_back(
    scalars, vectors, ga, gb, normed, slope, w_up, w_down, middle, mine, other, w_out, parts, blocks, lanes, aligned,
    order=None,
):
    rows, width = ga.shape
    count, half = 2 * rows, width // 2
    ff = w_up.shape[1]
    chunk = ff // parts
    if aligned:
        shares = [pltpu.HBM((parts, blocks, width // blocks // 2, lanes), BF16)] * 2
        held = [pltpu.VMEM((2,) + shares[0].shape, BF16)]
    else:
        shares = [jax.ShapeDtypeStruct((parts, width, chunk), BF16), jax.ShapeDtypeStruct((width, width), BF16)]
        held = [pltpu.VMEM((1,) + shares[0].shape, BF16), pltpu.VMEM((width, width), BF16)]
    scratch = [
        pltpu.VMEM((count, width), BF16),
        pltpu.VMEM((count, width), BF16),
        pltpu.VMEM((width, count), BF16),
        pltpu.VMEM((count, ff), BF16),
        pltpu.VMEM((width, ff), BF16),
        pltpu.VMEM((ff, width), BF16),
        pltpu.VMEM((count, width), F32),
        pltpu.VMEM((count, width), F32),
        pltpu.VMEM((2, count, half), BF16),
        pltpu.VMEM((width, width), BF16),
        pltpu.VMEM((count, width), BF16),
    ]
    scratch += held + [pltpu.SemaphoreType.DMA((13 + 5 * parts,))]
    outs = [
        pltpu.HBM((count, width), F32),
        pltpu.HBM((count, half), BF16),
        pltpu.HBM((count, half), BF16),
        jax.ShapeDtypeStruct((1, width), F32),
    ]
    return call(
        functools.partial(feed_back_body, aligned=aligned),
        "feed_back",
        scalars,
        (vectors, ga, gb, in_hbm(normed), in_hbm(slope), in_hbm(w_up), in_hbm(w_down), in_hbm(middle), mine, other, in_hbm(w_out)),
        [whole(vectors.shape)] + [ANY] * 10,
        outs + shares,
        [ANY] * 3 + [whole((1, width))] + [ANY] * 2,
        scratch=scratch,
        vmem=48,
        order=order,
        us=18,
    )


def attend_back_body(s_ref, *refs, pair):
    qs, dos, outs, lses = refs[0:2], refs[2:4], refs[4:6], refs[6:8]
    k0, k1, v0, v1, dq0, dq1, dk, dv, keys, vals = refs[8:]
    count = qs[0].shape[0]
    keys[:count, :], keys[count:, :] = k0[...], k1[...]
    vals[:count, :], vals[count:, :] = v0[...], v1[...]
    lanes = lax.broadcasted_iota(jnp.int32, (1, 128), 1)
    picks = lax.broadcasted_iota(jnp.int32, (8, 128), 1) // HEAD_DIM == lax.broadcasted_iota(jnp.int32, (8, 128), 0)
    picks = picks.astype(BF16)
    keys_t = keys[...].T
    turned = {}
    inners = []
    for b in range(2):
        product = dos[b][...].astype(F32) * outs[b][...].astype(F32)
        high = product.astype(BF16)
        low = (product - high.astype(F32)).astype(BF16)
        inners.append(mm(picks, high, NT) + mm(picks, low, NT))
        turned[b] = (qs[b][...].T, dos[b][...].T)
    grads_q = [[], []]
    grads_k, grads_v = [], []
    for h in range(2):
        head = slice(64 * h, 64 * h + 64)
        mask = (lanes >= 64) == (h == 1)
        grad_k = grad_v = None
        for b in range(2):
            q_head = jnp.where(mask, qs[b][...], jnp.zeros_like(qs[b][...]))
            do_head = jnp.where(mask, dos[b][...], jnp.zeros_like(dos[b][...]))
            weights = jnp.exp(mm(keys[...], q_head, NT) - lses[b][2 * pair + h : 2 * pair + h + 1, :])
            grad_weights = mm(vals[...], do_head, NT)
            grad_scores = (weights * (grad_weights - inners[b][h : h + 1, :])).astype(BF16)
            term = mm(turned[b][1][head], weights.astype(BF16), NT)
            grad_v = term if b == 0 else grad_v + term
            term = mm(turned[b][0][head], grad_scores, NT)
            grad_k = term if b == 0 else grad_k + term
            grads_q[b].append(mm(keys_t[head], grad_scores))
        grads_k.append(grad_k)
        grads_v.append(grad_v)
    for b, out in enumerate((dq0, dq1)):
        out[...] = (jnp.concatenate(grads_q[b], axis=0).T * SCALE).astype(BF16)
    dk[...] = jnp.concatenate(grads_k, axis=0).T.astype(BF16)
    dv[...] = jnp.concatenate(grads_v, axis=0).T.astype(BF16)


def attend_back(scalars, near, far, pair, order=None):
    count, half = near[1].shape
    ins = [a for both in zip(near, far) for a in both] + [near[0], far[0]] * 2
    pairs = half // 128
    lane = lambda t: pl.BlockSpec((count, 128), lambda g, s: (0, t * pairs + pair))
    one = jax.ShapeDtypeStruct((count, 128), BF16)
    two = jax.ShapeDtypeStruct((2 * count, 128), BF16)
    outs = [one, one, two, two]
    return call(
        functools.partial(attend_back_body, pair=pair),
        "attend_back",
        scalars,
        ins,
        [lane(0)] * 6 + [whole(near[3].shape)] * 2 + [lane(1), lane(1), lane(2), lane(2)],
        outs,
        [whole(o.shape) for o in outs],
        scratch=[pltpu.VMEM((2 * count, 128), BF16), pltpu.VMEM((2 * count, 128), BF16)],
        order=order,
        us=1.5,
        vmem=28,
    )


def side_by_side(refs):
    return jnp.concatenate([refs[3 * pair + t][...] for t in range(3) for pair in range(len(refs) // 3)], axis=1)


def pair_specs(grads, part, count):
    arrays, specs = [], []
    for near, far, dk, dv in grads:
        arrays += [(near, far)[part], dk, dv]
        specs += [whole((count, 128))] + [pl.BlockSpec((count, 128), lambda g, s: (part, 0))] * 2
    return arrays, specs


def project_back_body(s_ref, weight, *refs):
    refs[-1][...] = mm(side_by_side(refs[:-1]), weight[...], NT).astype(BF16)


def project_back(scalars, grads, weight, part, order=None):
    count = grads[0][0].shape[0]
    arrays, specs = pair_specs(grads, part, count)
    out = jax.ShapeDtypeStruct((count, weight.shape[0]), BF16)
    return call(
        project_back_body,
        "project_back",
        scalars,
        [weight] + arrays,
        [whole(weight.shape)] + specs,
        [out],
        [whole(out.shape)],
        order=order,
        us=1.0,
        vmem=16,
    )[0]


def turn_body(s_ref, ha, hb, xa, xb, vectors, *refs):
    out = refs[-1]
    rows = ha.shape[0]
    for at, block in enumerate((ha, hb, xa, xb)):
        unit, _ = normalize(block[...].astype(F32) + vectors[0:1, :])
        out[:, at * rows : (at + 1) * rows] = (unit * vectors[1:2, :]).astype(BF16).T


def hold(scalars, awaited, carry, order=None):
    return call(
        lambda *refs: None, "hold", scalars, (awaited,), [ANY], [], [], carry=carry, order=order, us=0.5, vmem=4
    )


def turned_tokens(scalars, ha, hb, xa, xb, vectors, order=None):
    ins = (ha, hb, xa, xb, vectors)
    out = jax.ShapeDtypeStruct((ha.shape[1], 4 * ha.shape[0]), BF16)
    return call(
        turn_body,
        "turned",
        scalars,
        ins,
        [whole(a.shape) for a in ins],
        [out],
        [whole(out.shape)],
        order=order,
        us=1,
        vmem=16,
    )[0]


def qkv_weight_body(s_ref, turned, *refs, pairs, aligned):
    out = refs[4 * pairs]
    grads = refs[-2] if aligned else refs[-1]
    count = refs[0].shape[0]
    lanes = grads.shape[1] // 3
    for pair in range(pairs):
        near, far, dk, dv = refs[4 * pair : 4 * pair + 4]
        here = slice(128 * pair, 128 * pair + 128)
        grads[:count, here] = near[...]
        grads[count:, here] = far[...]
        grads[:, lanes + 128 * pair : lanes + 128 * pair + 128] = dk[...]
        grads[:, 2 * lanes + 128 * pair : 2 * lanes + 128 * pair + 128] = dv[...]
    value = mm(turned[...], grads[...]).astype(BF16)
    if not aligned:
        out[...] = value
        return
    out[...] = value.reshape(out.shape)
    copies = Copies(refs[-1])
    bits = out.shape[0].bit_length() - 1
    for half, order in enumerate(orders(bits)):
        send = refs[4 * pairs + 1 + half]
        for g in range(send.shape[0]):
            copies.out(out.at[step_index(order, 0, s_ref[1], g), half], send.at[g])
    copies.finish()


def qkv_weight(scalars, turned, grads, blocks, aligned, order=None):
    width, count = turned.shape
    pairs = len(grads)
    lanes = 3 * 128 * pairs
    own = width // blocks // 2
    ins = [turned] + [a for four in grads for a in four]
    outs = [pltpu.HBM((blocks, 2, own, lanes) if aligned else (width, lanes), BF16)]
    specs = [whole(outs[0].shape)]
    scratch = [pltpu.VMEM((count, lanes), BF16)]
    if aligned:
        outs += [jax.ShapeDtypeStruct((blocks // 2, own, lanes), BF16)] * 2
        specs += [ANY] * 2
        scratch += [pltpu.SemaphoreType.DMA((blocks,))]
    return call(
        functools.partial(qkv_weight_body, pairs=pairs, aligned=aligned),
        "qkv_weight",
        scalars,
        ins,
        [whole(a.shape) for a in ins],
        outs,
        specs,
        scratch=scratch,
        order=order,
        us=1.5,
        vmem=24,
    )


def base_body(s_ref, ha, hb, vectors, grad_middle, weight, part_in, gain_two, *refs):
    ia, ib, sums = refs[-3:]
    rows = ha.shape[0]
    gain = vectors[1:2, :]
    grad_normed = mm(side_by_side(refs[:-3]), weight[...], NT) + part_in[...].astype(F32)
    gain_sum, base_sum = None, None
    for at, (block, out) in enumerate(((ha, ia), (hb, ib))):
        here = slice(at * rows, (at + 1) * rows)
        unit, root = normalize(block[...].astype(F32) + vectors[0:1, :])
        back, part = norm_back(grad_normed[here], unit, root, gain)
        grad = grad_middle[here, :] + back
        out[...] = grad.astype(BF16)
        gain_sum = part if gain_sum is None else gain_sum + part
        tokens = jnp.sum(grad, axis=0, keepdims=True)
        base_sum = tokens if base_sum is None else base_sum + tokens
    sums[0:1, :] = gain_sum
    sums[1:2, :] = gain_two[...]
    sums[2:3, :] = base_sum


def base_back(scalars, ha, hb, vectors, grad_middle, grads, weight, part_in, gain_two, order=None):
    rows, width = ha.shape
    arrays, specs = pair_specs(grads, 0, 2 * rows)
    grad_middle = in_hbm(grad_middle)
    ins = (ha, hb, vectors, grad_middle, weight, part_in, gain_two)
    outs = [
        jax.ShapeDtypeStruct((rows, width), BF16),
        jax.ShapeDtypeStruct((rows, width), BF16),
        jax.ShapeDtypeStruct((3, width), F32),
    ]
    return call(
        base_body,
        "base_back",
        scalars,
        list(ins) + arrays,
        [Staged(a) if a is grad_middle else whole(a.shape) for a in ins] + specs,
        outs,
        [whole(o.shape) for o in outs],
        order=order,
        us=1.75,
        vmem=24,
    )


def meet_body(s_ref, held, got, out, *, which, at):
    rows = held.shape[0] - 2
    out[0:2, :] = held[0:2, :] + got[0:2, :]
    if which is None:
        out[2:, :] = held[2:, :] + got[2:, :]
        return
    first = bit(s_ref[which], at) == 0
    mine, other = held[2:, :], got[2:, :]
    out[2 : 2 + rows, :] = jnp.where(first, mine, other)
    out[2 + rows :, :] = jnp.where(first, other, mine)


def meet(scalars, held, got, which, at, carry=(), order=None):
    rows, lanes = held.shape
    out = jax.ShapeDtypeStruct((rows if which is None else 2 * rows - 2, lanes), F32)
    return call(
        functools.partial(meet_body, which=which, at=at),
        "meet",
        scalars,
        (held, got),
        [whole(held.shape)] * 2,
        [out],
        [whole(out.shape)],
        carry=carry,
        order=order,
        us=1.5,
        vmem=4,
    )


def table_body(s_ref, sums, out):
    out[...] = jnp.zeros_like(out)
    for at in range(sums.shape[0] - 2):
        here = pl.ds(s_ref[at], 1)
        out[here, :] = out[here, :] + sums[at + 2 : at + 3, :]


def table_of(steps, sums, count, order=None):
    out = pltpu.HBM((count, sums.shape[1]), F32)
    return call(
        table_body,
        "table",
        steps,
        (sums,),
        [whole(sums.shape)],
        [out],
        [whole(out.shape)],
        order=order,
        us=1.25,
        vmem=12,
    )[0]


def fold(name, scalars, outs, order=None, split=False):
    ins, specs, known = [], [], {}
    for _, _, entries in outs:
        for _, _, terms in entries:
            for array, _, far in terms:
                if id(array) not in known:
                    known[id(array)] = len(ins)
                    ins.append(in_hbm(array) if far else array)
                    specs.append(ANY)
    scratch = [pltpu.VMEM(block, t[0].dtype) for _, _, entries in outs for _, block, terms in entries for t in terms]
    given = len(ins)

    def body(s_ref, *refs):
        arrays, targets = refs[:given], refs[given : given + len(shapes)]
        held = list(refs[given + len(shapes) : -1])
        copies = Copies(refs[-1])
        if split:
            sides, targets = targets, [held.pop()]
        waiting = []
        for (_, _, entries), target in zip(outs, targets):
            for to, _, terms in entries:
                mine = []
                for array, where, _ in terms:
                    slot = held.pop(0)
                    mine.append((copies.start(arrays[known[id(array)]].at[where(s_ref)], slot), slot))
                waiting.append((target, to, mine))
        for target, to, mine in waiting:
            total = None
            for copy, slot in mine:
                copy.wait()
                total = slot[...].astype(F32) if total is None else total + slot[...].astype(F32)
            target[to] = total[..., : target[to].shape[-1]].astype(target.dtype)
        if split:
            copies.out(targets[0].at[1 - s_ref[0]], sides[0])
            copies.out(targets[0].at[s_ref[0]], sides[1])
            copies.finish()

    shapes = [jax.ShapeDtypeStruct(o[0], o[1]) for o in outs]
    if split:
        shapes = [pltpu.HBM(outs[0][0][1:], outs[0][1])] * 2
        scratch.append(pltpu.VMEM(outs[0][0], outs[0][1]))
    return call(
        body,
        name,
        scalars,
        ins,
        specs,
        shapes,
        [ANY if split else whole(o.shape) for o in shapes],
        scratch=scratch + [pltpu.SemaphoreType.DMA((len(scratch) + 2,))],
        order=order,
        us=1.5,
        vmem=16,
    )


def bit(value, at):
    return (value >> at) & 1


def orders(bits):
    return (list(range(bits)), list(range(bits))[::-1])


def step_index(order, step, own, g):
    value = (1 - bit(own, order[step])) << order[step]
    for at in order[:step]:
        value = value + (bit(own, at) << at)
    for i, at in enumerate(order[step + 1 :]):
        value = value + (bit(g, i) << at)
    return value


def held_index(order, step, block):
    value = block * 0
    for i, at in enumerate(order[step + 1 :]):
        value = value + (bit(block, at) << i)
    return value


class Segment:
    def __init__(self, low, high, terms):
        self.low, self.high, self.terms = low, high, list(terms)


class Reduction:
    def __init__(self, swap, pieces, seq_bits, has_seq=True):
        self.swap, self.pieces, self.seq_bits = swap, pieces, seq_bits
        self.seq_orders = [orders(seq_bits)[at % 2] for at in range(len(pieces))]
        self.steps = len(pieces[0][0])
        self.rows = sum(p[2] for p in pieces)
        self.lanes = pieces[0][3][-1].high
        self.lead = (1 << seq_bits,) if has_seq else ()
        self.got = [[] for _ in pieces]
        self.got_seq = [[] for _ in pieces]

    def entries(self, at, to, block_of, seq_of=None):
        order, first, rows, segments = self.pieces[at]
        every = slice(None)
        out = []
        for segment in segments:
            width = segment.high - segment.low
            terms = []
            for array, where, far in segment.terms:
                place = lambda s, where=where: where(block_of(s), None if seq_of is None else seq_of(s))
                terms.append((array, place, far))
            for step, array in self.got[at]:

                def place(s, step=step, lanes=pl.ds(segment.low, width)):
                    block = held_index(order, step, block_of(s))
                    if not self.lead:
                        return (block, every, lanes)
                    return (block, every if seq_of is None else seq_of(s), every, lanes)

                terms.append((array, place, False))
            if seq_of is not None:
                for step, array in self.got_seq[at]:
                    place = lambda s, step=step, lanes=pl.ds(segment.low, width): (
                        held_index(self.seq_orders[at], step, seq_of(s)),
                        every,
                        lanes,
                    )
                    terms.append((array, place, False))
            block = (self.lead if seq_of is None else ()) + (rows, width)
            out.append((to + (Ellipsis, slice(segment.low, segment.high)), block, terms))
        return out

    def leaving(self, step):
        count = 1 << (self.steps - 1 - step)
        outs = []
        for at, (order, _, rows, _) in enumerate(self.pieces):
            entries = []
            for g in range(count):
                entries += self.entries(at, (g,), lambda s, g=g, order=order: step_index(order, step, s[1], g))
            outs.append(((count,) + self.lead + (rows, self.lanes), BF16, entries))
        if step == self.steps - 1 and self.lead:
            for at, (_, _, rows, _) in enumerate(self.pieces):
                outs.append((self.lead + (rows, self.lanes), F32, self.entries(at, (), lambda s: s[1])))
        return outs

    def send(self, step, sent):
        count = len(self.pieces)
        every = slice(None)
        for at, (order, _, _, segments) in enumerate(self.pieces):
            if len(sent) > count:
                self.got[at] = []
                for segment in segments:
                    lanes = pl.ds(segment.low, segment.high - segment.low)
                    where = lambda block, seq, lanes=lanes: (every if seq is None else seq, every, lanes)
                    segment.terms = [(sent[count + at], where, False)]
            self.got[at].append((step, self.swap(sent[at], 2 << order[step], 0)))

    def leaving_seq(self, step):
        count = 1 << (self.seq_bits - 1 - step)
        outs = []
        for at, (_, _, rows, _) in enumerate(self.pieces):
            entries = []
            for g in range(count):
                seq_of = lambda s, g=g, order=self.seq_orders[at]: step_index(order, step, s[2], g)
                entries += self.entries(at, (g,), lambda s: s[1], seq_of)
            outs.append(((count, rows, self.lanes), BF16, entries))
        return outs

    def send_seq(self, step, sent):
        for at, value in enumerate(sent):
            self.got_seq[at].append((step, self.swap(value, 0, 1 << self.seq_orders[at][step])))

    def last(self, segment, lanes, row_of):
        entries = []
        for piece, (_, _, rows, _) in enumerate(self.pieces):
            _, block, terms = self.entries(piece, (), lambda s: s[1], lambda s: s[2])[segment]
            entries.append(((slice(row_of(piece), row_of(piece) + rows), lanes), block, terms))
        return entries


def columns_body(s_ref, mine, other, keep, *sends):
    even = s_ref[0] == 0
    here, there = mine[...].astype(F32), other[...].astype(F32)
    half = here.shape[1] // 3
    first, second = jnp.where(even, here, there), jnp.where(even, there, here)
    columns = []
    for t in range(3):
        columns += [first[:, t * half : t * half + half], second[:, t * half : t * half + half]]
    columns = jnp.concatenate(columns, axis=1)
    lanes = keep.shape[1]
    for at, target in enumerate((keep, *sends)):
        for part in range(len(sends) + 1):

            @pl.when((s_ref[2] ^ at) == part)
            def _(target=target, part=part):
                target[...] = columns[:, part * lanes : part * lanes + lanes].astype(target.dtype)


def on_device(
    row_count, seq_count, hidden_in, timesteps, step_table, gain_one, w_qkv, w_out, gain_two, w_up, w_down, out_grad
):
    seqs_here, tokens_here, width = hidden_in.shape
    ff = w_up.shape[1]
    half = width // 2
    blocks = row_count // 2
    block_bits = blocks.bit_length() - 1
    seq_bits = seq_count.bit_length() - 1
    r = lax.axis_index("rows")
    z = lax.axis_index("seq")
    c = lax.rem(r, 2)
    b = lax.div(r, 2)
    odd = lax.rem(z, 2)
    axes = ("rows", "seq")

    def flat(row, seq):
        return row * seq_count + seq

    def swap(value, row_bit, seq_bit=0):
        pairs = [
            (flat(i, j), flat(i ^ row_bit, j ^ seq_bit)) for i in range(row_count) for j in range(seq_count)
        ]
        return lax.ppermute(value, axes, pairs)

    def core_swap(value):
        return swap(value, 1)

    moves = []
    for turn in range(2):
        moves.append(
            [
                (flat(2 * p + e, j), flat(2 * p + j // 2, 2 * e + (j + turn) % 2))
                for p in range(blocks)
                for e in range(2)
                for j in range(seq_count)
            ]
        )

    def gather_tokens(leaving):
        return tuple(lax.ppermute(value, axes, move) for value, move in zip(leaving, moves))

    def share(value, at, axis):
        return lax.dynamic_index_in_dim(value, at, axis, keepdims=False)

    def send_back(*values):
        return [lax.ppermute(value, axes, [(t, s) for s, t in move]) for value, move in zip(values, moves)]

    scalars = jnp.stack([c, b, z]).astype(jnp.int32)

    steps_all = lax.all_gather(timesteps, "rows", axis=0, tiled=True)
    steps_held = steps_all.reshape(blocks, seq_count).T.reshape(-1)
    step_now = lax.dynamic_index_in_dim(steps_all, seq_count * b + z, 0, keepdims=False)
    row = lax.dynamic_slice_in_dim(step_table, step_now, 1, 0).astype(F32)

    order = Order()
    weight, vectors = prepare(scalars, row, gain_one[None, :], gain_two[None, :], w_qkv)
    ha, hb = gather_tokens([share(hidden_in, at, 0) for at in (odd, 1 - odd)])
    xa, xb = core_swap(ha), core_swap(hb)
    near = qkv(scalars, ha, hb, vectors, weight, order=order, us=2)
    late_grad, _, _ = lax.optimization_barrier((out_grad, ha, hb))
    ga, gb = gather_tokens([share(late_grad, at, 0) for at in (odd, 1 - odd)])
    far = qkv(scalars, xa, xb, vectors, weight, order=order)
    mixed_far, lse_far = attend(scalars, far, near, far, order=order)
    mixed_in = core_swap(mixed_far)
    mixed_near, lse_near = attend(scalars, near, near, far, order=order)

    parts = seq_count
    unit = ff // row_count
    own_rows, seq_cols, up_cols = width // row_count, width // seq_count, ff // seq_count
    whole_units = blocks == parts and unit % 128 == 0
    whole_rows = own_rows % 32 == 0

    oa, ob, middle, normed_two, slope, down_far, down_near = forward_pass(
        scalars, ha, hb, vectors, mixed_near, mixed_in, w_out, w_up, w_down, ga, gb, parts, order=order
    )
    if not whole_units:
        sides = [jnp.where(c == side, down_near, down_far) for side in range(2)]
        natural = jnp.concatenate(sides, axis=2).transpose(1, 0, 2).reshape(parts, seq_cols, blocks, 2, unit)
        down_far, down_near = (share(natural, at, 3).transpose(2, 0, 1, 3) for at in (1 - c, c))
    down_shape = (blocks, parts, seq_cols, unit)
    down_far, down_near = down_far.reshape(down_shape), down_near.reshape(down_shape)
    down_in = core_swap(down_far)

    lanes = -(-(up_cols + seq_cols) // 256) * 256
    grad_middle, gm_near, gm_far, gain_two_part, up_far, up_near = feed_back(
        scalars, vectors, ga, gb, normed_two, slope, w_up, w_down, middle, mixed_near, mixed_in, w_out,
        parts, blocks, lanes, whole_rows, order=order,
    )
    if not whole_rows:
        up_all = up_far.reshape(parts, blocks, 2, own_rows, up_cols)
        out_all = up_near.reshape(blocks, 2, own_rows, parts, seq_cols).transpose(3, 0, 1, 2, 4)
        blank = jnp.zeros(up_all.shape[:-1] + (lanes - up_cols - seq_cols,), BF16)
        natural = jnp.concatenate([up_all, out_all, blank], axis=-1)
        up_far, up_near = (share(natural, at, 2) for at in (1 - c, c))

    fold_over = functools.partial(fold, "reduce", scalars, order=order)
    both = orders(block_bits)
    every = slice(None)

    def taken(array, by_seq, first, rows, some):
        def where(block, seq):
            seq = every if seq is None else seq
            place = (seq, block) if by_seq else (block, seq)
            return place + (pl.ds(first, rows),) + (() if some is None else (some,))

        return (array, where, array is down_near or array is up_near)

    def segment(low, high, arrays, by_seq, first, rows, lanes=None):
        return Segment(low, high, [taken(array, by_seq, first, rows, lanes) for array in arrays])

    def up_segments(low, first, rows):
        cut = ((0, up_cols), (up_cols, lanes))
        return [segment(low + a, low + b, ups, True, first, rows, pl.ds(a, b - a)) for a, b in cut]

    def step_over(reductions, leaving, send, step):
        outs = [leaving(r, step) for r in reductions]
        sent = list(fold_over([o for out in outs for o in out]))
        for reduction, out in zip(reductions, outs):
            send(reduction, step, sent[: len(out)])
            del sent[: len(out)]

    step_blocks = functools.partial(step_over, leaving=Reduction.leaving, send=Reduction.send)
    step_seq = functools.partial(step_over, leaving=Reduction.leaving_seq, send=Reduction.send_seq)

    gm_far, up_far, oa, ob = hold(scalars, down_in, (gm_far, up_far, oa, ob), order=order)
    up_in = core_swap(up_far)
    gm_in = core_swap(gm_far)
    turned = turned_tokens(scalars, ha, hb, xa, xb, vectors, order=order)
    out_back = send_back(oa, ob)
    downs, ups = (down_near, down_in), (up_near, up_in)
    joined = whole_units and whole_rows and 2 * unit == up_cols and seq_cols == 2 * own_rows
    if joined:
        rows = own_rows // 2
        pieces = []
        for at in range(2):
            segments = [segment(t * unit, (t + 1) * unit, downs, False, (2 * at + t) * rows, rows) for t in range(2)]
            segments += up_segments(2 * unit, at * rows, rows)
            pieces.append((both[at], at * rows, rows, segments))
        everything = [Reduction(swap, pieces, seq_bits)]
    else:
        down = Reduction(swap, [(both[0], 0, seq_cols, [segment(0, unit, downs, False, 0, seq_cols)])], seq_bits)
        up = Reduction(swap, [(both[1], 0, own_rows, up_segments(0, 0, own_rows))], seq_bits)
        everything = [down, up]
    step_blocks(everything, step=0)
    sides = ((near, gm_near, mixed_near, lse_near), (far, gm_in, mixed_far, lse_far))
    grads = []
    for pair in range(half // 128):
        grads.append(attend_back(scalars, *sides, pair, order=order))
        if pair == 1:
            out_hidden = returned_blocks(scalars, *out_back, order=order)
    part_far = project_back(scalars, grads, weight, 1, order=order)
    part_in = core_swap(part_far)
    qkv_w = qkv_weight(scalars, turned, grads, blocks, whole_rows, order=order)
    for step in range(1, block_bits):
        step_blocks(everything, step=step)
    if whole_rows:
        qkv_blocks = qkv_w[0].reshape(blocks, 2 * own_rows, 3 * half)
        rows_of = lambda h: (lambda block, seq: (block, pl.ds(h * own_rows, own_rows)))
    else:
        qkv_blocks = qkv_w[0].reshape(blocks, 2, own_rows, 3 * half)
        rows_of = lambda h: (lambda block, seq: (block, h))
    project = Reduction(
        swap,
        [
            (both[h], h * own_rows, own_rows, [Segment(0, 3 * half, [(qkv_blocks, rows_of(h), True)])])
            for h in range(2)
        ],
        seq_bits,
        False,
    )
    if whole_rows:
        project.send(0, qkv_w[1:])
    else:
        step_blocks([project], step=0)
    ia, ib, held = base_back(
        scalars, ha, hb, vectors, grad_middle, grads, weight, part_in, gain_two_part, order=order
    )
    in_back = send_back(ia, ib)

    meetings = [(None, 0, 1, 0)]
    meetings += [(1, at, 2 << at, 0) for at in range(block_bits)]
    meetings += [(2, at, 0, 1 << at) for at in range(seq_bits)]

    def next_meeting(held, carry=()):
        which, at, row_bit, seq_bit = meetings.pop(0)
        out = meet(scalars, held, swap(held, row_bit, seq_bit), which, at, carry, order=order)
        return out if carry else out[0]

    held = next_meeting(held)
    in_grad = returned_blocks(scalars, *in_back, order=order)
    step_seq(everything, step=0)
    for step in range(1, block_bits):
        step_blocks([project], step=step)
    held = next_meeting(held)
    held = next_meeting(held)
    held = next_meeting(held)
    for step in range(1, seq_bits):
        step_seq(everything, step=step)
    entries = []
    for h in range(2):
        for _, block, terms in project.entries(h, (), lambda s: s[1]):
            entries.append(((h,), block, terms))
    qkv_far, qkv_mine = fold_over([((2, own_rows, 3 * half), BF16, entries)], split=True)
    held = next_meeting(held)
    shape = (own_rows, 6 * half // parts)
    qkv_keep, *qkv_sends = call(
        columns_body,
        "qkv_columns",
        scalars,
        (qkv_mine, core_swap(qkv_far)),
        [whole(qkv_mine.shape)] * 2,
        [jax.ShapeDtypeStruct(shape, F32)] + [jax.ShapeDtypeStruct(shape, BF16)] * (parts - 1),
        [whole(shape)] * parts,
        vmem=12,
        order=order,
    )
    qkv_terms = [qkv_keep] + [swap(value, 0, at + 1) for at, value in enumerate(qkv_sends)]
    while meetings:
        held = next_meeting(held)
    table = table_of(steps_held, held, step_table.shape[0], order=order)
    if joined:
        block = everything[0]
        down_entries = block.last(0, slice(None), lambda piece: 2 * piece * rows)
        down_entries += block.last(1, slice(None), lambda piece: (2 * piece + 1) * rows)
        up_block, up_at, row_of = block, 2, lambda piece: piece * rows
    else:
        down_entries = down.last(0, slice(None), lambda piece: 0)
        up_block, up_at, row_of = up, 0, lambda piece: 0
    up_entries = up_block.last(up_at, slice(0, up_cols), row_of)
    out_entries = up_block.last(up_at + 1, slice(0, seq_cols), row_of)
    qkv_entry = ((Ellipsis,), shape, [(value, lambda s: (slice(None),), False) for value in qkv_terms])
    down_shard, up_shard, out_shard, qkv_shard = fold_over(
        [
            ((seq_cols, unit), F32, down_entries),
            ((own_rows, up_cols), F32, up_entries),
            ((own_rows, seq_cols), F32, out_entries),
            (shape, F32, [qkv_entry]),
        ]
    )


    return (
        out_hidden,
        in_grad,
        table,
        held[0],
        qkv_shard,
        out_shard,
        held[1],
        up_shard,
        down_shard.T,
    )


def solution(mesh):
    tokens = P("rows", "seq", None)
    split = P("rows", "seq")
    in_specs = (tokens, P("rows"), P(), P(), P(), P(), P(), P(), P(), tokens)
    out_specs = (tokens, tokens, P(), P(), split, split, P(), split, split)
    body = functools.partial(on_device, mesh.shape["rows"], mesh.shape["seq"])
    return jax.shard_map(body, mesh=mesh, in_specs=in_specs, out_specs=out_specs, check_vma=False)
```

```python
import functools

import jax
import jax.numpy as jnp
from jax import lax
from jax.experimental import pallas as pl
from jax.experimental.pallas import tpu as pltpu
from jax.sharding import PartitionSpec as P

HEAD_DIM = 64
SCALE = HEAD_DIM ** (-0.5)
EPS = 1e-05
F32 = jnp.float32
BF16 = jnp.bfloat16
MIB = 1 << 20
PER_US = 1_000_000_000

NN = (((1,), (0,)), ((), ()))
NT = (((1,), (1,)), ((), ()))


def mm(a, b, dims=NN):
    return lax.dot_general(a, b, dims, preferred_element_type=F32)


def normalize(values):
    average = jnp.mean(values, axis=-1, keepdims=True)
    centred = values - average
    inverse_root = lax.rsqrt(jnp.mean(centred * centred, axis=-1, keepdims=True) + EPS)
    return (centred * inverse_root, inverse_root)


def norm_back(grad_normed, unit_rows, inverse_root, scale_gain):
    gained = grad_normed * scale_gain
    centred_grad = (
        gained
        - jnp.mean(gained, axis=-1, keepdims=True)
        - unit_rows * jnp.mean(gained * unit_rows, axis=-1, keepdims=True)
    )
    return (inverse_root * centred_grad, jnp.sum(grad_normed * unit_rows, axis=0, keepdims=True))


def whole(shape):
    return pl.BlockSpec(shape, lambda *_: (0,) * len(shape))


class Staged:
    def __init__(self, array):
        self.memory = pltpu.VMEM(array.shape, array.dtype)


class Order:
    def __init__(self):
        self.token = None


def call(
    body, name, scalars, ins, in_specs, outs, out_specs, grid=(1,), scratch=(), vmem=32, order=None, us=1.0, carry=()
):
    ins, in_specs, outs, out_specs = list(ins), list(in_specs), list(outs), list(out_specs)
    count, given = len(ins), len(outs)
    staged = [at for at, spec in enumerate(in_specs) if isinstance(spec, Staged)]
    held = [in_specs[at].memory for at in staged]
    for at in staged:
        in_specs[at] = ANY
    waits = [] if order is None or order.token is None else [order.token]
    inner = body

    def body(scalars_ref, *refs):
        refs = list(refs)
        del refs[count : count + len(carry) + len(waits)]
        del refs[count + given : count + given + len(carry)]
        if order is not None:
            token = refs.pop(count + given)
            token[...] = jnp.zeros_like(token)
        if staged:
            sems, slots = refs.pop(), refs[len(refs) - len(held) :]
            del refs[len(refs) - len(held) :]
            copies = [pltpu.make_async_copy(refs[at], slot, sems.at[i]) for i, (at, slot) in enumerate(zip(staged, slots))]
            for copy in copies:
                copy.start()
            for at, slot in zip(staged, slots):
                refs[at] = slot
            for copy in copies:
                copy.wait()
        inner(scalars_ref, *refs)

    ins += [in_hbm(value) for value in carry] + waits
    in_specs += [ANY] * (len(carry) + len(waits))
    outs += [pltpu.HBM(value.shape, value.dtype) for value in carry]
    out_specs += [ANY] * len(carry)
    if order is not None:
        outs.append(jax.ShapeDtypeStruct((8, 128), F32))
        out_specs.append(whole((8, 128)))
    scratch = list(scratch) + held + ([pltpu.SemaphoreType.DMA((len(staged),))] if staged else [])
    result = pl.pallas_call(
        body,
        name=name,
        grid_spec=pltpu.PrefetchScalarGridSpec(
            num_scalar_prefetch=1,
            grid=grid,
            in_specs=in_specs,
            out_specs=out_specs,
            scratch_shapes=scratch,
        ),
        out_shape=outs,
        input_output_aliases={1 + count + at: given + at for at in range(len(carry))},
        cost_estimate=pl.CostEstimate(flops=int(us * PER_US), bytes_accessed=1 << 10, transcendentals=0),
        compiler_params=pltpu.CompilerParams(vmem_limit_bytes=vmem * MIB),
    )(scalars, *ins)
    result = list(result)
    if order is not None:
        order.token = result.pop()
    return result


def in_hbm(value):
    return pltpu.with_memory_space_constraint(value, pltpu.HBM)


ANY = pl.BlockSpec(memory_space=pl.ANY)


def gelu_both(upper):
    square = upper * upper
    turned = jnp.tanh(upper * (GELU_A + GELU_A * GELU_B * square))
    half_up = 0.5 + 0.5 * turned
    active = upper * half_up
    slope = half_up + active * (1.0 - turned) * (GELU_A + 3.0 * GELU_A * GELU_B * square)
    return active.astype(BF16), slope.astype(BF16)


class Copies:
    def __init__(self, sems):
        self.sems, self.count, self.outs = sems, 0, []

    def start(self, source, target):
        copy = pltpu.make_async_copy(source, target, self.sems.at[self.count])
        self.count += 1
        copy.start()
        return copy

    def out(self, source, target):
        self.outs.append(self.start(source, target))

    def finish(self):
        for copy in self.outs:
            copy.wait()


GELU_A, GELU_B = 0.7978845608028654, 0.044715


def stretches(parts):
    return [(at, min(at + 2, parts)) for at in range(0, parts, 2)]


def prepare_body(s_ref, row, first, second, wq, wk, wv, out, vectors):
    half = wq.shape[1]
    for t, w in enumerate((wq, wk, wv)):
        out[:, t * half : t * half + half] = w[...]
    for at, value in enumerate((row, first, second)):
        vectors[at : at + 1, :] = value[...]


def prepare(scalars, row, gain_one, gain_two, w_qkv, order=None):
    width = w_qkv.shape[0]
    half = width // 2
    specs = [whole((1, width))] * 3
    specs += [pl.BlockSpec((width, half), functools.partial(lambda t, g, s: (0, 2 * t + s[0]), t)) for t in range(3)]
    outs = [jax.ShapeDtypeStruct((width, 3 * half), BF16), jax.ShapeDtypeStruct((8, width), F32)]
    return call(
        prepare_body,
        "prepare",
        scalars,
        (row, gain_one, gain_two) + (in_hbm(w_qkv),) * 3,
        specs,
        outs,
        [whole(o.shape) for o in outs],
        order=order,
        us=2,
        vmem=12,
    )


def returned_body(s_ref, first, second, out, sems):
    at = bit(s_ref[2], 0)
    copies = Copies(sems)
    copies.out(first, out.at[at])
    copies.out(second, out.at[1 - at])
    copies.finish()


def returned_blocks(scalars, first, second, order=None):
    return call(
        returned_body,
        "returned",
        scalars,
        (first, second),
        [ANY] * 2,
        [pltpu.HBM((2,) + first.shape, first.dtype)],
        [ANY],
        scratch=[pltpu.SemaphoreType.DMA((2,))],
        order=order,
        us=3,
        vmem=4,
    )[0]


def qkv_body(s_ref, ha, hb, vectors, weight, out, normed):
    row, gain = vectors[0:1, :], vectors[1:2, :]
    rows = ha.shape[0]
    half = out.shape[1] // 3
    for at, block in enumerate((ha, hb)):
        unit, _ = normalize(block[...].astype(F32) + row)
        normed[pl.ds(at * rows, rows), :] = (unit * gain).astype(BF16)
    packed = mm(normed[...], weight[...]).astype(BF16)
    out[:, :half] = (packed[:, :half] * SCALE).astype(BF16)
    out[:, half:] = packed[:, half:]


def qkv(scalars, ha, hb, vectors, weight, order=None, us=2.3):
    rows, width = ha.shape
    ins = (ha, hb, vectors, weight)
    out = jax.ShapeDtypeStruct((2 * rows, weight.shape[1]), BF16)
    return call(
        qkv_body,
        "qkv",
        scalars,
        ins,
        [whole(a.shape) for a in ins],
        [out],
        [whole(out.shape)],
        scratch=[pltpu.VMEM((2 * rows, width), BF16)],
        order=order,
        us=us,
        vmem=16,
    )[0]


def attend_body(s_ref, q, k0, k1, v0, v1, mixed, lse):
    count, half = q.shape
    lanes = lax.broadcasted_iota(jnp.int32, (1, 128), 1)
    ones = jnp.ones((16, count), BF16)
    for pair in range(half // 128):
        cols = slice(128 * pair, 128 * pair + 128)
        q_pair = q[:, cols]
        vt = [v[:, cols].T for v in (v0, v1)]
        done = []
        for h in range(2):
            q_head = jnp.where((lanes >= 64) == (h == 1), q_pair, jnp.zeros_like(q_pair))
            scores = [mm(k[:, cols], q_head, NT) for k in (k0, k1)]
            highest = jnp.maximum(
                jnp.max(scores[0], axis=0, keepdims=True), jnp.max(scores[1], axis=0, keepdims=True)
            )
            total = None
            for part in range(2):
                weights = jnp.exp(scores[part] - highest).astype(BF16)
                left = jnp.concatenate([vt[part][64 * h : 64 * h + 64], ones], axis=0)
                term = mm(left, weights)
                total = term if total is None else total + term
            summed = total[64:65]
            done.append(total[:64] / summed)
            lse[2 * pair + h : 2 * pair + h + 1, :] = highest + jnp.log(summed)
        mixed[:, cols] = jnp.concatenate(done, axis=0).T.astype(BF16)


def attend(scalars, asked, near, far, order=None):
    count, half = asked.shape[0], asked.shape[1] // 3
    ins = (asked, near, far, near, far)
    outs = [jax.ShapeDtypeStruct((count, half), BF16), jax.ShapeDtypeStruct((8, count), F32)]
    return call(
        attend_body,
        "attend",
        scalars,
        ins,
        [pl.BlockSpec((count, half), functools.partial(lambda t, g, s: (0, t), t)) for t in (0, 1, 1, 2, 2)],
        outs,
        [whole(o.shape) for o in outs],
        order=order,
        us=6,
        vmem=24,
    )


def forward_pass_body(
    s_ref, vectors, ha, hb, m0, m1, wo, wu, wd, ga, gb,
    oa, ob, middle, normed, slope, far, near,
    tokens, mixed, out_w, up_w, down_w, grads, grads_t, mid, norm, out, slopes, shares, sems
):
    rows, half = ha.shape[0], m0.shape[1]
    parts = far.shape[0]
    chunk = 2 * half
    c = s_ref[0]
    copies = Copies(sems)
    first = [
        copies.start(m0, mixed.at[:, :half]),
        copies.start(m1, mixed.at[:, half:]),
        copies.start(wo.at[pl.ds(pl.multiple_of(c * half, half), half), :], out_w.at[:half, :]),
        copies.start(wo.at[pl.ds(pl.multiple_of((1 - c) * half, half), half), :], out_w.at[half:, :]),
        copies.start(ha, tokens.at[:rows, :]),
        copies.start(hb, tokens.at[rows:, :]),
    ]

    def ask(here):
        return (copies.start(wu.at[:, here], up_w.at[:, here]), copies.start(wd.at[here, :], down_w.at[here, :]))

    steps = [slice(low * chunk, high * chunk) for low, high in stretches(parts)]
    for copy in first:
        copy.wait()
    weights = [ask(steps[0])]
    turn = [copies.start(ga, grads.at[:rows, :]), copies.start(gb, grads.at[rows:, :])]
    mid[...] = tokens[...].astype(F32) + vectors[0:1, :] + mm(mixed[...], out_w[...])
    unit, _ = normalize(mid[...])
    norm[...] = (unit * vectors[2:3, :]).astype(BF16)
    copies.out(mid, middle)
    copies.out(norm, normed)
    for copy in turn:
        copy.wait()
    grads_t[...] = grads[...].T
    for i, here in enumerate(steps):
        if i + 1 < len(steps):
            weights.append(ask(steps[i + 1]))
        for copy in weights[i]:
            copy.wait()
        active, slopes[:, here] = gelu_both(mm(norm[...], up_w[:, here]))
        term = mm(active, down_w[here, :])
        out[...] = (mid if i == 0 else out)[...] + term
        value = mm(grads_t[...], active).astype(BF16)
        low, high = stretches(parts)[i]
        for part in range(low, high):
            for side in range(2):
                at = (part - low) * chunk + side * half
                shares[side, part] = value[:, at : at + half]
        copies.out(slopes.at[:, here], slope.at[:, here])
        copies.out(shares.at[1 - c, low:high], far.at[low:high])
        copies.out(shares.at[c, low:high], near.at[low:high])
    tokens[...] = out[...].astype(BF16)
    copies.out(tokens.at[:rows, :], oa)
    copies.out(tokens.at[rows:, :], ob)
    copies.finish()


def forward_pass(scalars, ha, hb, vectors, mine, other, w_out, w_up, w_down, ga, gb, parts, order=None):
    rows, width = ha.shape
    count, half = mine.shape
    ff = w_up.shape[1]
    outs = [
        pltpu.HBM((rows, width), BF16),
        pltpu.HBM((rows, width), BF16),
        pltpu.HBM((count, width), F32),
        pltpu.HBM((count, width), BF16),
        pltpu.HBM((count, ff), BF16),
        pltpu.HBM((parts, width, half), BF16),
        pltpu.HBM((parts, width, half), BF16),
    ]
    scratch = [
        pltpu.VMEM((count, width), BF16),
        pltpu.VMEM((count, width), BF16),
        pltpu.VMEM((width, width), BF16),
        pltpu.VMEM((width, ff), BF16),
        pltpu.VMEM((ff, width), BF16),
        pltpu.VMEM((count, width), BF16),
        pltpu.VMEM((width, count), BF16),
        pltpu.VMEM((count, width), F32),
        pltpu.VMEM((count, width), BF16),
        pltpu.VMEM((count, width), F32),
        pltpu.VMEM((count, ff), BF16),
        pltpu.VMEM((2, parts, width, half), BF16),
        pltpu.SemaphoreType.DMA((12 + 5 * parts,)),
    ]
    return call(
        forward_pass_body,
        "forward_pass",
        scalars,
        (vectors, ha, hb, mine, other, in_hbm(w_out), in_hbm(w_up), in_hbm(w_down), ga, gb),
        [whole(vectors.shape)] + [ANY] * 9,
        outs,
        [ANY] * 7,
        scratch=scratch,
        vmem=35,
        order=order,
        us=14,
    )


def feed_back_body(
    s_ref, vectors, ga, gb, normed, slope, wu, wd, middle, m0, m1, wo,
    grad_middle, gm_near, gm_far, gain_grad, *rest, aligned
):
    shares = rest[:2]
    grads, norm, norm_t, slopes, up_w, down_w, sums, mid, mixed, out_w, heads, held, *natural, sems = rest[2:]
    rows = ga.shape[0]
    half = m0.shape[1]
    parts = held.shape[1]
    chunk = wu.shape[1] // parts
    c = s_ref[0]
    copies = Copies(sems)
    first = [copies.start(ga, grads.at[:rows, :]), copies.start(gb, grads.at[rows:, :]), copies.start(normed, norm)]

    def ask(here):
        return (
            copies.start(wd.at[here, :], down_w.at[here, :]),
            copies.start(slope.at[:, here], slopes.at[:, here]),
            copies.start(wu.at[:, here], up_w.at[:, here]),
        )

    steps = [slice(low * chunk, high * chunk) for low, high in stretches(parts)]
    weights = [ask(steps[0])]
    for copy in first:
        copy.wait()
    norm_t[...] = norm[...].T
    last = []
    for i, here in enumerate(steps):
        if i + 1 < len(steps):
            weights.append(ask(steps[i + 1]))
        else:
            last = [
                copies.start(middle, mid),
                copies.start(wo.at[pl.ds(pl.multiple_of(c * half, half), half), :], out_w.at[:half, :]),
                copies.start(wo.at[pl.ds(pl.multiple_of((1 - c) * half, half), half), :], out_w.at[half:, :]),
                copies.start(m0, mixed.at[c]),
                copies.start(m1, mixed.at[1 - c]),
            ]
        for copy in weights[i]:
            copy.wait()
        grad_upper = (mm(grads[...], down_w[here, :], NT) * slopes[:, here].astype(F32)).astype(BF16)
        term = mm(grad_upper, up_w[:, here], NT)
        sums[...] = term if i == 0 else sums[...] + term
        value = mm(norm_t[...], grad_upper).astype(BF16)
        low, high = stretches(parts)[i]
        for part in range(low, high):
            mine = value[:, (part - low) * chunk : (part - low + 1) * chunk]
            if aligned:
                mine = mine.reshape(held.shape[2], 2, held.shape[3], chunk)
                held[0, part, :, :, :chunk] = mine[:, 0]
                held[1, part, :, :, :chunk] = mine[:, 1]
            else:
                held[0, part] = mine
        if aligned:
            for side, target in ((1 - c, shares[0]), (c, shares[1])):
                copies.out(held.at[side, low:high, :, :, :chunk], target.at[low:high, :, :, :chunk])
        else:
            copies.out(held.at[0, low:high], shares[0].at[low:high])
    for copy in last:
        copy.wait()
    unit, root = normalize(mid[...])
    back, gain_sum = norm_back(sums[...], unit, root, vectors[2:3, :])
    gain_grad[...] = gain_sum
    mid[...] = grads[...].astype(F32) + back
    copies.out(mid, grad_middle)
    low_grad = mid[...].astype(BF16)
    heads[...] = mm(low_grad, out_w[...], NT).astype(BF16)
    copies.out(heads.at[:, :half], gm_near)
    copies.out(heads.at[:, half:], gm_far)
    turned = jnp.concatenate([mixed[0], mixed[1]], axis=1).T
    value = mm(turned, low_grad).astype(BF16)
    if aligned:
        blocks, own = held.shape[2:4]
        value = value.reshape(blocks, 2, own, 2 * half)
        cols = 2 * half // parts
        lanes = held.shape[4] - chunk
        for part in range(parts):
            mine = value[..., part * cols : (part + 1) * cols]
            pad = jnp.zeros(mine.shape[:-1] + (lanes - cols,), BF16)
            mine = jnp.concatenate([mine, pad], axis=-1)
            held[0, part, :, :, chunk:] = mine[:, 0]
            held[1, part, :, :, chunk:] = mine[:, 1]
        for side, target in ((1 - c, shares[0]), (c, shares[1])):
            copies.out(held.at[side, :, :, :, chunk:], target.at[:, :, :, chunk:])
    else:
        natural[0][...] = value
        copies.out(natural[0], shares[1])
    copies.finish()


def feed_back(
    scalars, vectors, ga, gb, normed, slope, w_up, w_down, middle, mine, other, w_out, parts, blocks, lanes, aligned,
    order=None,
):
    rows, width = ga.shape
    count, half = 2 * rows, width // 2
    ff = w_up.shape[1]
    chunk = ff // parts
    if aligned:
        shares = [pltpu.HBM((parts, blocks, width // blocks // 2, lanes), BF16)] * 2
        held = [pltpu.VMEM((2,) + shares[0].shape, BF16)]
    else:
        shares = [jax.ShapeDtypeStruct((parts, width, chunk), BF16), jax.ShapeDtypeStruct((width, width), BF16)]
        held = [pltpu.VMEM((1,) + shares[0].shape, BF16), pltpu.VMEM((width, width), BF16)]
    scratch = [
        pltpu.VMEM((count, width), BF16),
        pltpu.VMEM((count, width), BF16),
        pltpu.VMEM((width, count), BF16),
        pltpu.VMEM((count, ff), BF16),
        pltpu.VMEM((width, ff), BF16),
        pltpu.VMEM((ff, width), BF16),
        pltpu.VMEM((count, width), F32),
        pltpu.VMEM((count, width), F32),
        pltpu.VMEM((2, count, half), BF16),
        pltpu.VMEM((width, width), BF16),
        pltpu.VMEM((count, width), BF16),
    ]
    scratch += held + [pltpu.SemaphoreType.DMA((13 + 5 * parts,))]
    outs = [
        pltpu.HBM((count, width), F32),
        pltpu.HBM((count, half), BF16),
        pltpu.HBM((count, half), BF16),
        jax.ShapeDtypeStruct((1, width), F32),
    ]
    return call(
        functools.partial(feed_back_body, aligned=aligned),
        "feed_back",
        scalars,
        (vectors, ga, gb, in_hbm(normed), in_hbm(slope), in_hbm(w_up), in_hbm(w_down), in_hbm(middle), mine, other, in_hbm(w_out)),
        [whole(vectors.shape)] + [ANY] * 10,
        outs + shares,
        [ANY] * 3 + [whole((1, width))] + [ANY] * 2,
        scratch=scratch,
        vmem=48,
        order=order,
        us=18,
    )


def attend_back_body(s_ref, *refs, pair):
    qs, dos, outs, lses = refs[0:2], refs[2:4], refs[4:6], refs[6:8]
    k0, k1, v0, v1, dq0, dq1, dk, dv, keys, vals = refs[8:]
    count = qs[0].shape[0]
    keys[:count, :], keys[count:, :] = k0[...], k1[...]
    vals[:count, :], vals[count:, :] = v0[...], v1[...]
    lanes = lax.broadcasted_iota(jnp.int32, (1, 128), 1)
    picks = lax.broadcasted_iota(jnp.int32, (8, 128), 1) // HEAD_DIM == lax.broadcasted_iota(jnp.int32, (8, 128), 0)
    picks = picks.astype(BF16)
    keys_t = keys[...].T
    turned = {}
    inners = []
    for b in range(2):
        product = dos[b][...].astype(F32) * outs[b][...].astype(F32)
        high = product.astype(BF16)
        low = (product - high.astype(F32)).astype(BF16)
        inners.append(mm(picks, high, NT) + mm(picks, low, NT))
        turned[b] = (qs[b][...].T, dos[b][...].T)
    grads_q = [[], []]
    grads_k, grads_v = [], []
    for h in range(2):
        head = slice(64 * h, 64 * h + 64)
        mask = (lanes >= 64) == (h == 1)
        grad_k = grad_v = None
        for b in range(2):
            q_head = jnp.where(mask, qs[b][...], jnp.zeros_like(qs[b][...]))
            do_head = jnp.where(mask, dos[b][...], jnp.zeros_like(dos[b][...]))
            weights = jnp.exp(mm(keys[...], q_head, NT) - lses[b][2 * pair + h : 2 * pair + h + 1, :])
            grad_weights = mm(vals[...], do_head, NT)
            grad_scores = (weights * (grad_weights - inners[b][h : h + 1, :])).astype(BF16)
            term = mm(turned[b][1][head], weights.astype(BF16), NT)
            grad_v = term if b == 0 else grad_v + term
            term = mm(turned[b][0][head], grad_scores, NT)
            grad_k = term if b == 0 else grad_k + term
            grads_q[b].append(mm(keys_t[head], grad_scores))
        grads_k.append(grad_k)
        grads_v.append(grad_v)
    for b, out in enumerate((dq0, dq1)):
        out[...] = (jnp.concatenate(grads_q[b], axis=0).T * SCALE).astype(BF16)
    dk[...] = jnp.concatenate(grads_k, axis=0).T.astype(BF16)
    dv[...] = jnp.concatenate(grads_v, axis=0).T.astype(BF16)


def attend_back(scalars, near, far, pair, order=None):
    count, half = near[1].shape
    ins = [a for both in zip(near, far) for a in both] + [near[0], far[0]] * 2
    pairs = half // 128
    lane = lambda t: pl.BlockSpec((count, 128), lambda g, s: (0, t * pairs + pair))
    one = jax.ShapeDtypeStruct((count, 128), BF16)
    two = jax.ShapeDtypeStruct((2 * count, 128), BF16)
    outs = [one, one, two, two]
    return call(
        functools.partial(attend_back_body, pair=pair),
        "attend_back",
        scalars,
        ins,
        [lane(0)] * 6 + [whole(near[3].shape)] * 2 + [lane(1), lane(1), lane(2), lane(2)],
        outs,
        [whole(o.shape) for o in outs],
        scratch=[pltpu.VMEM((2 * count, 128), BF16), pltpu.VMEM((2 * count, 128), BF16)],
        order=order,
        us=1.5,
        vmem=28,
    )


def side_by_side(refs):
    return jnp.concatenate([refs[3 * pair + t][...] for t in range(3) for pair in range(len(refs) // 3)], axis=1)


def pair_specs(grads, part, count):
    arrays, specs = [], []
    for near, far, dk, dv in grads:
        arrays += [(near, far)[part], dk, dv]
        specs += [whole((count, 128))] + [pl.BlockSpec((count, 128), lambda g, s: (part, 0))] * 2
    return arrays, specs


def project_back_body(s_ref, weight, *refs):
    refs[-1][...] = mm(side_by_side(refs[:-1]), weight[...], NT).astype(BF16)


def project_back(scalars, grads, weight, part, order=None):
    count = grads[0][0].shape[0]
    arrays, specs = pair_specs(grads, part, count)
    out = jax.ShapeDtypeStruct((count, weight.shape[0]), BF16)
    return call(
        project_back_body,
        "project_back",
        scalars,
        [weight] + arrays,
        [whole(weight.shape)] + specs,
        [out],
        [whole(out.shape)],
        order=order,
        us=1.0,
        vmem=16,
    )[0]


def turn_body(s_ref, ha, hb, xa, xb, vectors, *refs):
    out = refs[-1]
    rows = ha.shape[0]
    for at, block in enumerate((ha, hb, xa, xb)):
        unit, _ = normalize(block[...].astype(F32) + vectors[0:1, :])
        out[:, at * rows : (at + 1) * rows] = (unit * vectors[1:2, :]).astype(BF16).T


def hold(scalars, awaited, carry, order=None):
    return call(
        lambda *refs: None, "hold", scalars, (awaited,), [ANY], [], [], carry=carry, order=order, us=0.5, vmem=4
    )


def turned_tokens(scalars, ha, hb, xa, xb, vectors, order=None):
    ins = (ha, hb, xa, xb, vectors)
    out = jax.ShapeDtypeStruct((ha.shape[1], 4 * ha.shape[0]), BF16)
    return call(
        turn_body,
        "turned",
        scalars,
        ins,
        [whole(a.shape) for a in ins],
        [out],
        [whole(out.shape)],
        order=order,
        us=1,
        vmem=16,
    )[0]


def qkv_weight_body(s_ref, turned, *refs, pairs, aligned):
    out = refs[4 * pairs]
    grads = refs[-2] if aligned else refs[-1]
    count = refs[0].shape[0]
    lanes = grads.shape[1] // 3
    for pair in range(pairs):
        near, far, dk, dv = refs[4 * pair : 4 * pair + 4]
        here = slice(128 * pair, 128 * pair + 128)
        grads[:count, here] = near[...]
        grads[count:, here] = far[...]
        grads[:, lanes + 128 * pair : lanes + 128 * pair + 128] = dk[...]
        grads[:, 2 * lanes + 128 * pair : 2 * lanes + 128 * pair + 128] = dv[...]
    value = mm(turned[...], grads[...]).astype(BF16)
    if not aligned:
        out[...] = value
        return
    out[...] = value.reshape(out.shape)
    copies = Copies(refs[-1])
    bits = out.shape[0].bit_length() - 1
    for half, order in enumerate(orders(bits)):
        send = refs[4 * pairs + 1 + half]
        for g in range(send.shape[0]):
            copies.out(out.at[step_index(order, 0, s_ref[1], g), half], send.at[g])
    copies.finish()


def qkv_weight(scalars, turned, grads, blocks, aligned, order=None):
    width, count = turned.shape
    pairs = len(grads)
    lanes = 3 * 128 * pairs
    own = width // blocks // 2
    ins = [turned] + [a for four in grads for a in four]
    outs = [pltpu.HBM((blocks, 2, own, lanes) if aligned else (width, lanes), BF16)]
    specs = [whole(outs[0].shape)]
    scratch = [pltpu.VMEM((count, lanes), BF16)]
    if aligned:
        outs += [jax.ShapeDtypeStruct((blocks // 2, own, lanes), BF16)] * 2
        specs += [ANY] * 2
        scratch += [pltpu.SemaphoreType.DMA((blocks,))]
    return call(
        functools.partial(qkv_weight_body, pairs=pairs, aligned=aligned),
        "qkv_weight",
        scalars,
        ins,
        [whole(a.shape) for a in ins],
        outs,
        specs,
        scratch=scratch,
        order=order,
        us=1.5,
        vmem=24,
    )


def base_body(s_ref, ha, hb, vectors, grad_middle, weight, part_in, gain_two, *refs):
    ia, ib, sums = refs[-3:]
    rows = ha.shape[0]
    gain = vectors[1:2, :]
    grad_normed = mm(side_by_side(refs[:-3]), weight[...], NT) + part_in[...].astype(F32)
    gain_sum, base_sum = None, None
    for at, (block, out) in enumerate(((ha, ia), (hb, ib))):
        here = slice(at * rows, (at + 1) * rows)
        unit, root = normalize(block[...].astype(F32) + vectors[0:1, :])
        back, part = norm_back(grad_normed[here], unit, root, gain)
        grad = grad_middle[here, :] + back
        out[...] = grad.astype(BF16)
        gain_sum = part if gain_sum is None else gain_sum + part
        tokens = jnp.sum(grad, axis=0, keepdims=True)
        base_sum = tokens if base_sum is None else base_sum + tokens
    sums[0:1, :] = gain_sum
    sums[1:2, :] = gain_two[...]
    sums[2:3, :] = base_sum


def base_back(scalars, ha, hb, vectors, grad_middle, grads, weight, part_in, gain_two, order=None):
    rows, width = ha.shape
    arrays, specs = pair_specs(grads, 0, 2 * rows)
    grad_middle = in_hbm(grad_middle)
    ins = (ha, hb, vectors, grad_middle, weight, part_in, gain_two)
    outs = [
        jax.ShapeDtypeStruct((rows, width), BF16),
        jax.ShapeDtypeStruct((rows, width), BF16),
        jax.ShapeDtypeStruct((3, width), F32),
    ]
    return call(
        base_body,
        "base_back",
        scalars,
        list(ins) + arrays,
        [Staged(a) if a is grad_middle else whole(a.shape) for a in ins] + specs,
        outs,
        [whole(o.shape) for o in outs],
        order=order,
        us=1.75,
        vmem=24,
    )


def meet_body(s_ref, held, got, out, *, which, at):
    rows = held.shape[0] - 2
    out[0:2, :] = held[0:2, :] + got[0:2, :]
    if which is None:
        out[2:, :] = held[2:, :] + got[2:, :]
        return
    first = bit(s_ref[which], at) == 0
    mine, other = held[2:, :], got[2:, :]
    out[2 : 2 + rows, :] = jnp.where(first, mine, other)
    out[2 + rows :, :] = jnp.where(first, other, mine)


def meet(scalars, held, got, which, at, carry=(), order=None):
    rows, lanes = held.shape
    out = jax.ShapeDtypeStruct((rows if which is None else 2 * rows - 2, lanes), F32)
    return call(
        functools.partial(meet_body, which=which, at=at),
        "meet",
        scalars,
        (held, got),
        [whole(held.shape)] * 2,
        [out],
        [whole(out.shape)],
        carry=carry,
        order=order,
        us=1.5,
        vmem=4,
    )


def table_body(s_ref, sums, out):
    out[...] = jnp.zeros_like(out)
    for at in range(sums.shape[0] - 2):
        here = pl.ds(s_ref[at], 1)
        out[here, :] = out[here, :] + sums[at + 2 : at + 3, :]


def table_of(steps, sums, count, order=None):
    out = pltpu.HBM((count, sums.shape[1]), F32)
    return call(
        table_body,
        "table",
        steps,
        (sums,),
        [whole(sums.shape)],
        [out],
        [whole(out.shape)],
        order=order,
        us=1.25,
        vmem=12,
    )[0]


def fold(name, scalars, outs, order=None, split=False):
    ins, specs, known = [], [], {}
    for _, _, entries in outs:
        for _, _, terms in entries:
            for array, _, far in terms:
                if id(array) not in known:
                    known[id(array)] = len(ins)
                    ins.append(in_hbm(array) if far else array)
                    specs.append(ANY)
    scratch = [pltpu.VMEM(block, t[0].dtype) for _, _, entries in outs for _, block, terms in entries for t in terms]
    given = len(ins)

    def body(s_ref, *refs):
        arrays, targets = refs[:given], refs[given : given + len(shapes)]
        held = list(refs[given + len(shapes) : -1])
        copies = Copies(refs[-1])
        if split:
            sides, targets = targets, [held.pop()]
        waiting = []
        for (_, _, entries), target in zip(outs, targets):
            for to, _, terms in entries:
                mine = []
                for array, where, _ in terms:
                    slot = held.pop(0)
                    mine.append((copies.start(arrays[known[id(array)]].at[where(s_ref)], slot), slot))
                waiting.append((target, to, mine))
        for target, to, mine in waiting:
            total = None
            for copy, slot in mine:
                copy.wait()
                total = slot[...].astype(F32) if total is None else total + slot[...].astype(F32)
            target[to] = total[..., : target[to].shape[-1]].astype(target.dtype)
        if split:
            copies.out(targets[0].at[1 - s_ref[0]], sides[0])
            copies.out(targets[0].at[s_ref[0]], sides[1])
            copies.finish()

    shapes = [jax.ShapeDtypeStruct(o[0], o[1]) for o in outs]
    if split:
        shapes = [pltpu.HBM(outs[0][0][1:], outs[0][1])] * 2
        scratch.append(pltpu.VMEM(outs[0][0], outs[0][1]))
    return call(
        body,
        name,
        scalars,
        ins,
        specs,
        shapes,
        [ANY if split else whole(o.shape) for o in shapes],
        scratch=scratch + [pltpu.SemaphoreType.DMA((len(scratch) + 2,))],
        order=order,
        us=1.5,
        vmem=16,
    )


def bit(value, at):
    return (value >> at) & 1


def orders(bits):
    return (list(range(bits)), list(range(bits))[::-1])


def step_index(order, step, own, g):
    value = (1 - bit(own, order[step])) << order[step]
    for at in order[:step]:
        value = value + (bit(own, at) << at)
    for i, at in enumerate(order[step + 1 :]):
        value = value + (bit(g, i) << at)
    return value


def held_index(order, step, block):
    value = block * 0
    for i, at in enumerate(order[step + 1 :]):
        value = value + (bit(block, at) << i)
    return value


class Segment:
    def __init__(self, low, high, terms):
        self.low, self.high, self.terms = low, high, list(terms)


class Reduction:
    def __init__(self, swap, pieces, seq_bits, has_seq=True):
        self.swap, self.pieces, self.seq_bits = swap, pieces, seq_bits
        self.seq_orders = [orders(seq_bits)[at % 2] for at in range(len(pieces))]
        self.steps = len(pieces[0][0])
        self.rows = sum(p[2] for p in pieces)
        self.lanes = pieces[0][3][-1].high
        self.lead = (1 << seq_bits,) if has_seq else ()
        self.got = [[] for _ in pieces]
        self.got_seq = [[] for _ in pieces]

    def entries(self, at, to, block_of, seq_of=None):
        order, first, rows, segments = self.pieces[at]
        every = slice(None)
        out = []
        for segment in segments:
            width = segment.high - segment.low
            terms = []
            for array, where, far in segment.terms:
                place = lambda s, where=where: where(block_of(s), None if seq_of is None else seq_of(s))
                terms.append((array, place, far))
            for step, array in self.got[at]:

                def place(s, step=step, lanes=pl.ds(segment.low, width)):
                    block = held_index(order, step, block_of(s))
                    if not self.lead:
                        return (block, every, lanes)
                    return (block, every if seq_of is None else seq_of(s), every, lanes)

                terms.append((array, place, False))
            if seq_of is not None:
                for step, array in self.got_seq[at]:
                    place = lambda s, step=step, lanes=pl.ds(segment.low, width): (
                        held_index(self.seq_orders[at], step, seq_of(s)),
                        every,
                        lanes,
                    )
                    terms.append((array, place, False))
            block = (self.lead if seq_of is None else ()) + (rows, width)
            out.append((to + (Ellipsis, slice(segment.low, segment.high)), block, terms))
        return out

    def leaving(self, step):
        count = 1 << (self.steps - 1 - step)
        outs = []
        for at, (order, _, rows, _) in enumerate(self.pieces):
            entries = []
            for g in range(count):
                entries += self.entries(at, (g,), lambda s, g=g, order=order: step_index(order, step, s[1], g))
            outs.append(((count,) + self.lead + (rows, self.lanes), BF16, entries))
        if step == self.steps - 1 and self.lead:
            for at, (_, _, rows, _) in enumerate(self.pieces):
                outs.append((self.lead + (rows, self.lanes), F32, self.entries(at, (), lambda s: s[1])))
        return outs

    def send(self, step, sent):
        count = len(self.pieces)
        every = slice(None)
        for at, (order, _, _, segments) in enumerate(self.pieces):
            if len(sent) > count:
                self.got[at] = []
                for segment in segments:
                    lanes = pl.ds(segment.low, segment.high - segment.low)
                    where = lambda block, seq, lanes=lanes: (every if seq is None else seq, every, lanes)
                    segment.terms = [(sent[count + at], where, False)]
            self.got[at].append((step, self.swap(sent[at], 2 << order[step], 0)))

    def leaving_seq(self, step):
        count = 1 << (self.seq_bits - 1 - step)
        outs = []
        for at, (_, _, rows, _) in enumerate(self.pieces):
            entries = []
            for g in range(count):
                seq_of = lambda s, g=g, order=self.seq_orders[at]: step_index(order, step, s[2], g)
                entries += self.entries(at, (g,), lambda s: s[1], seq_of)
            outs.append(((count, rows, self.lanes), BF16, entries))
        return outs

    def send_seq(self, step, sent):
        for at, value in enumerate(sent):
            self.got_seq[at].append((step, self.swap(value, 0, 1 << self.seq_orders[at][step])))

    def last(self, segment, lanes, row_of):
        entries = []
        for piece, (_, _, rows, _) in enumerate(self.pieces):
            _, block, terms = self.entries(piece, (), lambda s: s[1], lambda s: s[2])[segment]
            entries.append(((slice(row_of(piece), row_of(piece) + rows), lanes), block, terms))
        return entries


def columns_body(s_ref, mine, other, keep, *sends):
    even = s_ref[0] == 0
    here, there = mine[...].astype(F32), other[...].astype(F32)
    half = here.shape[1] // 3
    first, second = jnp.where(even, here, there), jnp.where(even, there, here)
    columns = []
    for t in range(3):
        columns += [first[:, t * half : t * half + half], second[:, t * half : t * half + half]]
    columns = jnp.concatenate(columns, axis=1)
    lanes = keep.shape[1]
    for at, target in enumerate((keep, *sends)):
        for part in range(len(sends) + 1):

            @pl.when((s_ref[2] ^ at) == part)
            def _(target=target, part=part):
                target[...] = columns[:, part * lanes : part * lanes + lanes].astype(target.dtype)


def on_device(
    row_count, seq_count, hidden_in, timesteps, step_table, gain_one, w_qkv, w_out, gain_two, w_up, w_down, out_grad
):
    seqs_here, tokens_here, width = hidden_in.shape
    ff = w_up.shape[1]
    half = width // 2
    blocks = row_count // 2
    block_bits = blocks.bit_length() - 1
    seq_bits = seq_count.bit_length() - 1
    r = lax.axis_index("rows")
    z = lax.axis_index("seq")
    c = lax.rem(r, 2)
    b = lax.div(r, 2)
    odd = lax.rem(z, 2)
    axes = ("rows", "seq")

    def flat(row, seq):
        return row * seq_count + seq

    def swap(value, row_bit, seq_bit=0):
        pairs = [
            (flat(i, j), flat(i ^ row_bit, j ^ seq_bit)) for i in range(row_count) for j in range(seq_count)
        ]
        return lax.ppermute(value, axes, pairs)

    def core_swap(value):
        return swap(value, 1)

    moves = []
    for turn in range(2):
        moves.append(
            [
                (flat(2 * p + e, j), flat(2 * p + j // 2, 2 * e + (j + turn) % 2))
                for p in range(blocks)
                for e in range(2)
                for j in range(seq_count)
            ]
        )

    def gather_tokens(leaving):
        return tuple(lax.ppermute(value, axes, move) for value, move in zip(leaving, moves))

    def share(value, at, axis):
        return lax.dynamic_index_in_dim(value, at, axis, keepdims=False)

    def send_back(*values):
        return [lax.ppermute(value, axes, [(t, s) for s, t in move]) for value, move in zip(values, moves)]

    scalars = jnp.stack([c, b, z]).astype(jnp.int32)

    steps_all = lax.all_gather(timesteps, "rows", axis=0, tiled=True)
    steps_held = steps_all.reshape(blocks, seq_count).T.reshape(-1)
    step_now = lax.dynamic_index_in_dim(steps_all, seq_count * b + z, 0, keepdims=False)
    row = lax.dynamic_slice_in_dim(step_table, step_now, 1, 0).astype(F32)

    order = Order()
    weight, vectors = prepare(scalars, row, gain_one[None, :], gain_two[None, :], w_qkv)
    ha, hb = gather_tokens([share(hidden_in, at, 0) for at in (odd, 1 - odd)])
    xa, xb = core_swap(ha), core_swap(hb)
    near = qkv(scalars, ha, hb, vectors, weight, order=order, us=2)
    late_grad, _, _ = lax.optimization_barrier((out_grad, ha, hb))
    ga, gb = gather_tokens([share(late_grad, at, 0) for at in (odd, 1 - odd)])
    far = qkv(scalars, xa, xb, vectors, weight, order=order)
    mixed_far, lse_far = attend(scalars, far, near, far, order=order)
    mixed_in = core_swap(mixed_far)
    mixed_near, lse_near = attend(scalars, near, near, far, order=order)

    parts = seq_count
    unit = ff // row_count
    own_rows, seq_cols, up_cols = width // row_count, width // seq_count, ff // seq_count
    whole_units = blocks == parts and unit % 128 == 0
    whole_rows = own_rows % 32 == 0

    oa, ob, middle, normed_two, slope, down_far, down_near = forward_pass(
        scalars, ha, hb, vectors, mixed_near, mixed_in, w_out, w_up, w_down, ga, gb, parts, order=order
    )
    if not whole_units:
        sides = [jnp.where(c == side, down_near, down_far) for side in range(2)]
        natural = jnp.concatenate(sides, axis=2).transpose(1, 0, 2).reshape(parts, seq_cols, blocks, 2, unit)
        down_far, down_near = (share(natural, at, 3).transpose(2, 0, 1, 3) for at in (1 - c, c))
    down_shape = (blocks, parts, seq_cols, unit)
    down_far, down_near = down_far.reshape(down_shape), down_near.reshape(down_shape)
    down_in = core_swap(down_far)

    lanes = -(-(up_cols + seq_cols) // 256) * 256
    grad_middle, gm_near, gm_far, gain_two_part, up_far, up_near = feed_back(
        scalars, vectors, ga, gb, normed_two, slope, w_up, w_down, middle, mixed_near, mixed_in, w_out,
        parts, blocks, lanes, whole_rows, order=order,
    )
    if not whole_rows:
        up_all = up_far.reshape(parts, blocks, 2, own_rows, up_cols)
        out_all = up_near.reshape(blocks, 2, own_rows, parts, seq_cols).transpose(3, 0, 1, 2, 4)
        blank = jnp.zeros(up_all.shape[:-1] + (lanes - up_cols - seq_cols,), BF16)
        natural = jnp.concatenate([up_all, out_all, blank], axis=-1)
        up_far, up_near = (share(natural, at, 2) for at in (1 - c, c))

    fold_over = functools.partial(fold, "reduce", scalars, order=order)
    both = orders(block_bits)
    every = slice(None)

    def taken(array, by_seq, first, rows, some):
        def where(block, seq):
            seq = every if seq is None else seq
            place = (seq, block) if by_seq else (block, seq)
            return place + (pl.ds(first, rows),) + (() if some is None else (some,))

        return (array, where, array is down_near or array is up_near)

    def segment(low, high, arrays, by_seq, first, rows, lanes=None):
        return Segment(low, high, [taken(array, by_seq, first, rows, lanes) for array in arrays])

    def up_segments(low, first, rows):
        cut = ((0, up_cols), (up_cols, lanes))
        return [segment(low + a, low + b, ups, True, first, rows, pl.ds(a, b - a)) for a, b in cut]

    def step_over(reductions, leaving, send, step):
        outs = [leaving(r, step) for r in reductions]
        sent = list(fold_over([o for out in outs for o in out]))
        for reduction, out in zip(reductions, outs):
            send(reduction, step, sent[: len(out)])
            del sent[: len(out)]

    step_blocks = functools.partial(step_over, leaving=Reduction.leaving, send=Reduction.send)
    step_seq = functools.partial(step_over, leaving=Reduction.leaving_seq, send=Reduction.send_seq)

    gm_far, up_far, oa, ob = hold(scalars, down_in, (gm_far, up_far, oa, ob), order=order)
    up_in = core_swap(up_far)
    gm_in = core_swap(gm_far)
    turned = turned_tokens(scalars, ha, hb, xa, xb, vectors, order=order)
    out_back = send_back(oa, ob)
    downs, ups = (down_near, down_in), (up_near, up_in)
    joined = whole_units and whole_rows and 2 * unit == up_cols and seq_cols == 2 * own_rows
    if joined:
        rows = own_rows // 2
        pieces = []
        for at in range(2):
            segments = [segment(t * unit, (t + 1) * unit, downs, False, (2 * at + t) * rows, rows) for t in range(2)]
            segments += up_segments(2 * unit, at * rows, rows)
            pieces.append((both[at], at * rows, rows, segments))
        everything = [Reduction(swap, pieces, seq_bits)]
    else:
        down = Reduction(swap, [(both[0], 0, seq_cols, [segment(0, unit, downs, False, 0, seq_cols)])], seq_bits)
        up = Reduction(swap, [(both[1], 0, own_rows, up_segments(0, 0, own_rows))], seq_bits)
        everything = [down, up]
    step_blocks(everything, step=0)
    sides = ((near, gm_near, mixed_near, lse_near), (far, gm_in, mixed_far, lse_far))
    grads = []
    for pair in range(half // 128):
        grads.append(attend_back(scalars, *sides, pair, order=order))
        if pair == 1:
            out_hidden = returned_blocks(scalars, *out_back, order=order)
    part_far = project_back(scalars, grads, weight, 1, order=order)
    part_in = core_swap(part_far)
    qkv_w = qkv_weight(scalars, turned, grads, blocks, whole_rows, order=order)
    for step in range(1, block_bits):
        step_blocks(everything, step=step)
    if whole_rows:
        qkv_blocks = qkv_w[0].reshape(blocks, 2 * own_rows, 3 * half)
        rows_of = lambda h: (lambda block, seq: (block, pl.ds(h * own_rows, own_rows)))
    else:
        qkv_blocks = qkv_w[0].reshape(blocks, 2, own_rows, 3 * half)
        rows_of = lambda h: (lambda block, seq: (block, h))
    project = Reduction(
        swap,
        [
            (both[h], h * own_rows, own_rows, [Segment(0, 3 * half, [(qkv_blocks, rows_of(h), True)])])
            for h in range(2)
        ],
        seq_bits,
        False,
    )
    if whole_rows:
        project.send(0, qkv_w[1:])
    else:
        step_blocks([project], step=0)
    ia, ib, held = base_back(
        scalars, ha, hb, vectors, grad_middle, grads, weight, part_in, gain_two_part, order=order
    )
    in_back = send_back(ia, ib)

    meetings = [(None, 0, 1, 0)]
    meetings += [(1, at, 2 << at, 0) for at in range(block_bits)]
    meetings += [(2, at, 0, 1 << at) for at in range(seq_bits)]

    def next_meeting(held, carry=()):
        which, at, row_bit, seq_bit = meetings.pop(0)
        out = meet(scalars, held, swap(held, row_bit, seq_bit), which, at, carry, order=order)
        return out if carry else out[0]

    held = next_meeting(held)
    in_grad = returned_blocks(scalars, *in_back, order=order)
    step_seq(everything, step=0)
    for step in range(1, block_bits):
        step_blocks([project], step=step)
    held = next_meeting(held)
    held = next_meeting(held)
    held = next_meeting(held)
    for step in range(1, seq_bits):
        step_seq(everything, step=step)
    entries = []
    for h in range(2):
        for _, block, terms in project.entries(h, (), lambda s: s[1]):
            entries.append(((h,), block, terms))
    qkv_far, qkv_mine = fold_over([((2, own_rows, 3 * half), BF16, entries)], split=True)
    held = next_meeting(held)
    shape = (own_rows, 6 * half // parts)
    qkv_keep, *qkv_sends = call(
        columns_body,
        "qkv_columns",
        scalars,
        (qkv_mine, core_swap(qkv_far)),
        [whole(qkv_mine.shape)] * 2,
        [jax.ShapeDtypeStruct(shape, F32)] + [jax.ShapeDtypeStruct(shape, BF16)] * (parts - 1),
        [whole(shape)] * parts,
        vmem=12,
        order=order,
    )
    qkv_terms = [qkv_keep] + [swap(value, 0, at + 1) for at, value in enumerate(qkv_sends)]
    while meetings:
        held = next_meeting(held)
    table = table_of(steps_held, held, step_table.shape[0], order=order)
    if joined:
        block = everything[0]
        down_entries = block.last(0, slice(None), lambda piece: 2 * piece * rows)
        down_entries += block.last(1, slice(None), lambda piece: (2 * piece + 1) * rows)
        up_block, up_at, row_of = block, 2, lambda piece: piece * rows
    else:
        down_entries = down.last(0, slice(None), lambda piece: 0)
        up_block, up_at, row_of = up, 0, lambda piece: 0
    up_entries = up_block.last(up_at, slice(0, up_cols), row_of)
    out_entries = up_block.last(up_at + 1, slice(0, seq_cols), row_of)
    qkv_entry = ((Ellipsis,), shape, [(value, lambda s: (slice(None),), False) for value in qkv_terms])
    down_shard, up_shard, out_shard, qkv_shard = fold_over(
        [
            ((seq_cols, unit), F32, down_entries),
            ((own_rows, up_cols), F32, up_entries),
            ((own_rows, seq_cols), F32, out_entries),
            (shape, F32, [qkv_entry]),
        ]
    )


    return (
        out_hidden,
        in_grad,
        table,
        held[0],
        qkv_shard,
        out_shard,
        held[1],
        up_shard,
        down_shard.T,
    )


def solution(mesh):
    tokens = P("rows", "seq", None)
    split = P("rows", "seq")
    in_specs = (tokens, P("rows"), P(), P(), P(), P(), P(), P(), P(), tokens)
    out_specs = (tokens, tokens, P(), P(), split, split, P(), split, split)
    body = functools.partial(on_device, mesh.shape["rows"], mesh.shape["seq"])
    return jax.shard_map(body, mesh=mesh, in_specs=in_specs, out_specs=out_specs, check_vma=False)
```
